32 devices in a mesh: grp: 4 (over y, core), sub: 8 (over z, x).
Axes of the slice: x: 2, y: 2, z: 4, core: 2. Of those that a mesh axis runs over, the one named last changes fastest.
Arguments:
- source: float32 [16, 64, 512], P('grp', 'sub'), may hold values from -6 to 6
- fine_coefficients: float32 [27, 16, 64, 512], P(None, 'grp', 'sub'), may hold values from -0.2 to 7, as said below
- middle_coefficients: float32 [27, 8, 32, 256], P(None, 'grp', 'sub'), may hold values from -0.2 to 7, as said below
- coarse_coefficients: float32 [27, 4, 16, 128], P(None, 'grp'), may hold values from -0.2 to 7, as said below
Outputs:
- fine_iterate: float32 [16, 64, 512], P('grp', 'sub')
- middle_iterate: float32 [8, 32, 256], P('grp', 'sub')
- coarse_iterate: float32 [4, 16, 128], P('grp')
The draws below stay inside these ranges and needn't reach their ends.
Inputs may be any that keep to these rules, and one draw needn't show every extreme that they name: `fine_coefficients`: entries other than entry 13 are at most 0; entry 13 of each cell exceeds the sum of the magnitudes of that cell's other 26 entries. `middle_coefficients`: entries other than entry 13 are at most 0; entry 13 of each cell exceeds the sum of the magnitudes of that cell's other 26 entries. `coarse_coefficients`: entries other than entry 13 are at most 0; entry 13 of each cell exceeds the sum of the magnitudes of that cell's other 26 entries.
All inputs are finite; a program needn't handle non-finite values.
Results may differ from the reference program's by a relative error of at most 0.00002.
Values sent between devices are 32-bit elements; how exact they have to be, the bound alone decides.
No kernel may reach another device: no remote copies, remote signals or barrier semaphores. Data moves between devices by JAX's collectives and lax.ppermute only.
A program may use at most 64 MiB of HBM per device.

```python
import jax
import jax.numpy as jnp

NU0 = 3
NU1 = 3
NB = 16
NX0 = 16
NY0 = 64
NZ0 = 512
NX1 = 8
NY1 = 32
NZ1 = 256
NX2 = 4
NY2 = 16
NZ2 = 128


def stencil_draw(key, extent_x, extent_y, extent_z):
    key_perm = jax.random.fold_in(key, 11)
    key_weights = jax.random.fold_in(key, 23)
    key_margin = jax.random.fold_in(key, 37)
    shape = (extent_x, extent_y, extent_z)
    spread = jnp.clip(0.6 * jax.random.normal(key_perm, shape, jnp.float32), -1.5, 1.5)
    weights = jax.random.uniform(key_weights, (27,) + shape, jnp.float32, 0.3, 1.0)
    margin = jax.random.uniform(key_margin, shape, jnp.float32, 0.1, 0.4)
    permeability = jnp.exp(spread)
    is_center = (jnp.arange(27) == 13)[:, None, None, None]
    offdiagonal = jnp.where(is_center, 0.0, -permeability[None] * weights / 26.0)
    center = jnp.sum(-offdiagonal, axis=0) + permeability * margin
    return jnp.where(is_center, center[None], offdiagonal)


def draw_fine_coefficients(key, part):
    return stencil_draw(key, NX0, NY0, NZ0)


def draw_middle_coefficients(key, part):
    return stencil_draw(key, NX1, NY1, NZ1)


def draw_coarse_coefficients(key, part):
    return stencil_draw(key, NX2, NY2, NZ2)


def levels(key, shape, cuts, least, high):
    factor_of, own = 1.0, jax.random.fold_in(key, 6)
    for position, shards_of in cuts:
        draws = jnp.exp(jax.random.uniform(jax.random.fold_in(own, position), (shards_of,), jnp.float32, least / len(cuts), high / len(cuts)))
        factor_of = factor_of * jnp.repeat(draws, shape[position] // shards_of).reshape([-1 if axis == position else 1 for axis in range(len(shape))])
    return factor_of


def normal_values(own_key, dims, scale, bound, shards=(), dtype=jnp.bfloat16):
    values = jax.random.normal(own_key, dims, jnp.float32) * scale
    if len(shards) > 0:
        values = levels(own_key, dims, shards, -0.22, 0.18) * values
    return jnp.clip(values, min=-bound, max=bound).astype(dtype)


def setup_inputs(seed: int = 0) -> dict:
    keys = jax.random.split(jax.random.key(seed), 5)
    source = normal_values(keys[0], (NX0, NY0, NZ0), 1.0, 6.0, ((0, 4), (1, 8)), jnp.float32)
    fine_coefficients = draw_fine_coefficients(jax.random.fold_in(keys[4], 71), 0)
    middle_coefficients = draw_middle_coefficients(jax.random.fold_in(keys[4], 71), 0)
    coarse_coefficients = draw_coarse_coefficients(jax.random.fold_in(keys[4], 71), 0)
    return dict(source=source, fine_coefficients=fine_coefficients, middle_coefficients=middle_coefficients, coarse_coefficients=coarse_coefficients)


JACOBI_WEIGHT = 0.8
CENTER_TERM = 13


def stencil_apply(coefficients, field):
    extent_x, extent_y, extent_z = field.shape
    padded = jnp.pad(field, 1)
    accumulated = jnp.zeros(field.shape, jnp.float32)
    for term_index in range(27):
        offset_x = term_index // 9
        offset_y = (term_index // 3) % 3
        offset_z = term_index % 3
        accumulated = accumulated + coefficients[term_index] * padded[offset_x:offset_x + extent_x, offset_y:offset_y + extent_y, offset_z:offset_z + extent_z]
    return accumulated


def relax_sweeps(coefficients, source, sweeps):
    diagonal = coefficients[CENTER_TERM]
    current = JACOBI_WEIGHT * source / diagonal
    for sweep_index in range(sweeps - 1):
        current = current + JACOBI_WEIGHT * (source - stencil_apply(coefficients, current)) / diagonal
    return current


def restrict(residual):
    extent_x, extent_y, extent_z = residual.shape
    blocks = residual.reshape(extent_x // 2, 2, extent_y // 2, 2, extent_z // 2, 2)
    return 0.5 * jnp.sum(blocks, axis=(1, 3, 5))


def reference(source, fine_coefficients, middle_coefficients, coarse_coefficients):
    fine_iterate = relax_sweeps(fine_coefficients, source, NU0)
    fine_residual = source - stencil_apply(fine_coefficients, fine_iterate)
    middle_source = restrict(fine_residual)
    middle_iterate = relax_sweeps(middle_coefficients, middle_source, NU1)
    middle_residual = middle_source - stencil_apply(middle_coefficients, middle_iterate)
    coarse_source = restrict(middle_residual)
    coarse_iterate = relax_sweeps(coarse_coefficients, coarse_source, NB)
    return (fine_iterate, middle_iterate, coarse_iterate)
```

```python
import functools

import jax
import jax.numpy as jnp
from jax import lax
from jax.experimental import pallas as pl
from jax.experimental.pallas import tpu as pltpu
from jax.sharding import PartitionSpec as P

NU0 = 3
NB = 16
WEIGHT = 0.8
CENTER = 13
LANES = 128
ROWS = 8
BASE = 8


def shape(*dims):
    return jax.ShapeDtypeStruct(dims, jnp.float32)


def call(kernel, outs, args, scratch=(), in_specs=None, grid=None):
    vmem = pl.BlockSpec(memory_space=pltpu.VMEM)
    return pl.pallas_call(
        kernel,
        out_shape=outs,
        in_specs=in_specs or [vmem] * len(args),
        out_specs=jax.tree.map(lambda _: vmem, outs),
        scratch_shapes=list(scratch),
        compiler_params=pltpu.CompilerParams(vmem_limit_bytes=48 << 20),
    )(*args)


def even(axis):
    return lax.rem(lax.axis_index(axis), 2) == 0


def pick(condition, a, b):
    return jnp.where(jnp.broadcast_to(condition, a.shape), a, b)


def shifted(values):
    extent = values.shape[-1]
    lane = lax.broadcasted_iota(jnp.int32, values.shape, values.ndim - 1)
    before = pltpu.roll(values, 1, values.ndim - 1)
    after = pltpu.roll(values, extent - 1, values.ndim - 1)
    return (
        jnp.where(lane == 0, 0.0, before),
        values,
        jnp.where(lane == extent - 1, 0.0, after),
    )


def place(padded, plane, row, values):
    for z, part in enumerate(shifted(values)):
        padded[z, plane, row : row + values.shape[0], :] = part


def stencil(padded, coefficient, first, planes, row, lanes):
    sums = [None] * planes
    for p in range(planes + 2):
        near = [
            [padded[z, first + p, row - 1 + y : row - 1 + y + ROWS, lanes] for z in range(3)]
            for y in range(3)
        ]
        for x in range(3):
            if not 0 <= p - x < planes:
                continue
            for y in range(3):
                for z in range(3):
                    term = coefficient(9 * x + 3 * y + z, p - x, lanes) * near[y][z]
                    sums[p - x] = term if sums[p - x] is None else sums[p - x] + term
    return sums


def lane_tiles(extent):
    return [slice(l, l + LANES) for l in range(0, extent, LANES)]


def paired_lanes(values):
    extent = values.shape[-1]
    row = lax.broadcasted_iota(jnp.int32, (extent, extent // 2), 0)
    column = lax.broadcasted_iota(jnp.int32, (extent, extent // 2), 1)
    pairs = jnp.where(lax.shift_right_logical(row, 1) == column, 1.0, 0.0)
    return lax.dot_general(
        values,
        pairs,
        (((1,), (0,)), ((), ())),
        precision=lax.Precision.HIGHEST,
        preferred_element_type=jnp.float32,
    )


def paired_rows(values):
    return values + pltpu.roll(values, values.shape[0] - 1, 0)


def put_edges(v, to_x, to_zx):
    last = v.shape[1] - 1
    for x in range(v.shape[0]):
        first_row, last_row = v[x, 0:1, :], v[x, last : last + 1, :]
        to_x[x : x + 1, :] = pick(even("sub"), last_row, first_row)
        to_zx[x : x + 1, :] = pick(even("sub"), first_row, last_row)


def start_kernel(f, center, v, to_x, to_zx):
    v[...] = WEIGHT * f[...] / center[0]
    put_edges(v, to_x, to_zx)


def faces_kernel(v, from_x, from_zx, to_core, to_y):
    planes, rows, _ = v.shape
    before = pick(even("sub"), from_zx[...], from_x[...])
    after = pick(even("sub"), from_x[...], from_zx[...])
    for ref, swap in ((to_core, False), (to_y, True)):
        def choose(a, b):
            return pick(even("grp"), b, a) if swap else pick(even("grp"), a, b)

        ref[0:rows, :] = choose(v[planes - 1], v[0])
        ref[rows : rows + 1, :] = choose(before[planes - 1 :], before[0:1])
        ref[rows + 1 : rows + 2, :] = choose(after[planes - 1 :], after[0:1])


def fill_fine(groups, padded, v, from_x, from_zx, from_core, from_y):
    planes, rows, _ = v.shape
    group = lax.axis_index("grp")
    for x in range(planes):
        place(padded, x + 1, BASE, v[x])
    befores = shifted(pick(even("sub"), from_zx[...], from_x[...]))
    afters = shifted(pick(even("sub"), from_x[...], from_zx[...]))
    for z in range(3):
        for x in range(planes):
            padded[z, x + 1, BASE - 1 : BASE, :] = befores[z][x : x + 1]
            padded[z, x + 1, BASE + rows : BASE + rows + 1, :] = afters[z][x : x + 1]
    low = pick(even("grp"), from_y[...], from_core[...])
    high = pick(even("grp"), from_core[...], from_y[...])
    low = pick(group == 0, jnp.zeros_like(low), low)
    high = pick(group == groups - 1, jnp.zeros_like(high), high)
    for plane, face in ((0, low), (planes + 1, high)):
        for z, part in enumerate(shifted(face)):
            padded[z, plane, BASE : BASE + rows, :] = part[0:rows]
            padded[z, plane, BASE - 1 : BASE, :] = part[rows : rows + 1]
            padded[z, plane, BASE + rows : BASE + rows + 1, :] = part[rows + 1 : rows + 2]


def sweep_kernel(groups, v, f, c, from_x, from_zx, from_core, from_y, out, to_x, to_zx, padded):
    planes, rows, extent = v.shape
    fill_fine(groups, padded, v, from_x, from_zx, from_core, from_y)
    for lanes in lane_tiles(extent):
        sums = stencil(padded, lambda k, x, l: c[k, x, :, l], 0, planes, BASE, lanes)
        for x in range(planes):
            out[x, :, lanes] = v[x, :, lanes] + WEIGHT * (f[x, :, lanes] - sums[x]) / c[CENTER, x, :, lanes]
    put_edges(out, to_x, to_zx)


def residual_kernel(groups, v, f, c, from_x, from_zx, from_core, from_y, center, source, to_x, to_zx, padded, held):
    planes, rows, extent = v.shape
    fill_fine(groups, padded, v, from_x, from_zx, from_core, from_y)
    for lanes in lane_tiles(extent):
        sums = stencil(padded, lambda k, x, l: c[k, x, :, l], 0, planes, BASE, lanes)
        r = [f[x, :, lanes] - sums[x] for x in range(planes)]
        for x in range(planes // 2):
            held[x * rows : (x + 1) * rows, lanes] = r[2 * x] + r[2 * x + 1]
    total = 0.5 * paired_rows(paired_lanes(held[...]))
    half = rows // 2
    for x in range(planes // 2):
        for y in range(half):
            row = x * rows + 2 * y
            source[x, y : y + 1, :] = total[row : row + 1]
    for x in range(planes // 2):
        mine = source[x]
        iterate = WEIGHT * mine / center[0, x]
        first = (mine[0:1], mine[1:2], iterate[2:3])
        last = (mine[half - 2 : half - 1], mine[half - 1 : half], iterate[half - 3 : half - 2])
        for i in range(3):
            row = 4 * x + i
            to_x[row : row + 1, :] = pick(even("sub"), last[i], first[i])
            to_zx[row : row + 1, :] = pick(even("sub"), first[i], last[i])


def middle_faces_kernel(source, from_x, from_zx, out):
    planes, half, _ = source.shape
    before = pick(even("sub"), from_zx[...], from_x[...])
    after = pick(even("sub"), from_x[...], from_zx[...])
    for x in range(planes):
        row = x * ROWS
        out[row : row + 2, :] = before[4 * x : 4 * x + 2]
        out[row + 2 : row + 2 + half, :] = source[x]
        out[row + 2 + half : row + ROWS, :] = after[4 * x : 4 * x + 2]
        extra = planes * ROWS + 2 * x
        out[extra : extra + 1, :] = before[4 * x + 2 : 4 * x + 3]
        out[extra + 1 : extra + 2, :] = after[4 * x + 2 : 4 * x + 3]


def coefficient_edges_kernel(c, to_x, to_zx):
    rows = c.shape[2]
    first, last = c[:, :, 0:2, :], c[:, :, rows - 2 : rows, :]
    to_x[...] = pick(even("sub"), last, first)
    to_zx[...] = pick(even("sub"), first, last)


def coefficient_pack_kernel(c, from_x, from_zx, coarse, out):
    _, planes, rows, extent = c.shape
    tiles = extent // LANES
    before = pick(even("sub"), from_zx[...], from_x[...])
    after = pick(even("sub"), from_x[...], from_zx[...])
    for x in range(planes):
        for l, lanes in enumerate(lane_tiles(extent)):
            row = (x * tiles + l) * ROWS
            out[:, row : row + 2, :] = before[:, x, :, lanes]
            out[:, row + 2 : row + 2 + rows, :] = c[:, x, :, lanes]
            out[:, row + 2 + rows : row + ROWS, :] = after[:, x, :, lanes]
    row = planes * tiles * ROWS
    for x in range(coarse.shape[1]):
        out[:, row : row + coarse.shape[2], :] = coarse[:, x]
        row += coarse.shape[2]


def middle_kernel(groups, subs, planes, *refs):
    packed, parts = refs[0], refs[1 : 1 + groups]
    iterate, coarse, padded, held = refs[1 + groups :]
    extent = packed.shape[-1]
    tiles = extent // LANES
    own = ROWS - 4
    group, sub = lax.axis_index("grp"), lax.axis_index("sub")
    total = groups * planes
    y = lax.broadcasted_iota(jnp.int32, (ROWS, extent), 0) + sub * own - 2
    inside = (y >= 0) & (y < subs * own)

    for plane in (0, total + 1):
        for z in range(3):
            padded[z, plane, :, :] = jnp.zeros(padded.shape[2:], jnp.float32)

    def owner_of(j):
        return jnp.bitwise_xor(group, j)

    def part_row(x, l):
        return (x * tiles + l.start // LANES) * ROWS

    for j in range(groups):
        o = owner_of(j)
        for x in range(planes):
            at = o * planes + x + 1
            extra = planes * ROWS + 2 * x
            for lanes in lane_tiles(extent):
                row = part_row(x, lanes)
                f = packed[o, x * ROWS : (x + 1) * ROWS, lanes]
                held[lanes.start // LANES] = WEIGHT * f / parts[j][CENTER, row : row + ROWS, :]
            v = jnp.concatenate([held[l] for l in range(tiles)], axis=1)
            place(padded, at, BASE, jnp.where(inside, v, 0.0))
            place(padded, at, BASE - 1, packed[o, extra : extra + 1, :])
            place(padded, at, BASE + ROWS, packed[o, extra + 1 : extra + 2, :])

    def sums_of(j, lanes):
        return stencil(
            padded,
            lambda k, x, l: parts[j][k, part_row(x, l) : part_row(x, l) + ROWS, :],
            owner_of(j) * planes,
            planes,
            BASE,
            lanes,
        )

    for _ in range(2):
        fresh = []
        for j in range(groups):
            o = owner_of(j)
            columns = [[] for _ in range(planes)]
            for lanes in lane_tiles(extent):
                sums = sums_of(j, lanes)
                for x in range(planes):
                    row = part_row(x, lanes)
                    f = packed[o, x * ROWS : (x + 1) * ROWS, lanes]
                    v = padded[1, o * planes + x + 1, BASE : BASE + ROWS, lanes]
                    v = v + WEIGHT * (f - sums[x]) / parts[j][CENTER, row : row + ROWS, :]
                    columns[x].append(v)
            fresh.append([jnp.concatenate(c, axis=1) for c in columns])
        for j in range(groups):
            for x in range(planes):
                place(padded, owner_of(j) * planes + x + 1, BASE, jnp.where(inside, fresh[j][x], 0.0))

    for x in range(planes):
        iterate[x] = padded[1, group * planes + x + 1, BASE + 2 : BASE + 2 + own, :]

    stacked = []
    for j in range(groups):
        o = owner_of(j)
        columns = [[] for _ in range(planes // 2)]
        for lanes in lane_tiles(extent):
            sums = sums_of(j, lanes)
            r = [packed[o, x * ROWS : (x + 1) * ROWS, lanes] - sums[x] for x in range(planes)]
            for x in range(planes // 2):
                columns[x].append(r[2 * x] + r[2 * x + 1])
        stacked += [jnp.concatenate(c, axis=1) for c in columns]
    result = 0.5 * paired_rows(paired_lanes(jnp.concatenate(stacked, axis=0)))
    place_of = lax.broadcasted_iota(jnp.int32, (ROWS, result.shape[1]), 0)
    for j in range(groups):
        for x in range(planes // 2):
            at = owner_of(j) * (planes // 2) + x
            tile = result[(j * (planes // 2) + x) * ROWS :][:ROWS]
            value = pltpu.roll(tile, ROWS - 2, 0)
            for i in range(1, own // 2):
                value = jnp.where(place_of == i, pltpu.roll(tile, ROWS - 2 - i, 0), value)
            for s in range(subs):
                coarse[s, at] = value[: own // 2]


def coarse_kernel(groups, subs, planes, start, *refs):
    gathered, parts = refs[0], refs[1 : 1 + groups]
    out, padded, right = refs[1 + groups :]
    _, rows, extent = right.shape
    each = rows // subs
    group = lax.axis_index("grp")

    def owner_of(j):
        return jnp.bitwise_xor(group, j)

    for plane in range(groups * planes + 2):
        for z in range(3):
            padded[z, plane, :, :] = jnp.zeros(padded.shape[2:], jnp.float32)
    for s in range(subs):
        for x in range(groups * planes):
            right[x, s * each : (s + 1) * each, :] = gathered[s, x]

    def row_of(x, t):
        return start + x * rows + t * ROWS

    tiles = rows // ROWS
    for j in range(groups):
        for x in range(planes):
            at = owner_of(j) * planes + x
            for t in range(tiles):
                row = row_of(x, t)
                v = WEIGHT * right[at, t * ROWS : (t + 1) * ROWS, :] / parts[j][CENTER, row : row + ROWS, :]
                place(padded, at + 1, BASE + t * ROWS, v)

    def sweep(_, carry):
        fresh = []
        for j in range(groups):
            for t in range(tiles):
                sums = stencil(
                    padded,
                    lambda k, x, l: parts[j][k, row_of(x, t) : row_of(x, t) + ROWS, :],
                    owner_of(j) * planes,
                    planes,
                    BASE + t * ROWS,
                    slice(0, extent),
                )
                for x in range(planes):
                    at = owner_of(j) * planes + x
                    row = row_of(x, t)
                    v = padded[1, at + 1, BASE + t * ROWS : BASE + (t + 1) * ROWS, :]
                    f = right[at, t * ROWS : (t + 1) * ROWS, :]
                    v = v + WEIGHT * (f - sums[x]) / parts[j][CENTER, row : row + ROWS, :]
                    fresh.append((at + 1, BASE + t * ROWS, v))
        for plane, row, v in fresh:
            place(padded, plane, row, v)
        return carry

    lax.fori_loop(0, NB - 1, sweep, 0)
    for x in range(planes):
        out[x] = padded[1, group * planes + x + 1, BASE : BASE + rows, :]


def swaps(pairs):
    return [p for a, b in pairs for p in ((a, b), (b, a))]


def body(source, fine, middle, coarse):
    groups, subs = lax.axis_size("grp"), lax.axis_size("sub")
    _, planes, rows, extent = fine.shape
    _, middle_planes, middle_rows, middle_extent = middle.shape
    _, coarse_planes, coarse_rows, coarse_extent = coarse.shape

    x_pairs = swaps([(i, i + 1) for i in range(0, subs, 2)])
    zx_pairs = swaps([(i, i + 1) for i in range(1, subs - 1, 2)])
    core_pairs = swaps([(i, i + 1) for i in range(0, groups, 2)])
    y_pairs = swaps([(i, (i + 1) % groups) for i in range(1, groups, 2)])

    def along_sub(pair):
        to_x, to_zx = pair
        from_zx = lax.ppermute(to_zx, "sub", zx_pairs)
        return lax.ppermute(to_x, "sub", x_pairs), from_zx

    def exchange(v, edges):
        halo = along_sub(edges)
        to_core, to_y = call(
            faces_kernel, [shape(rows + 8, extent)] * 2, [v, *halo]
        )
        from_core = lax.ppermute(to_core, "grp", core_pairs)
        from_y = lax.ppermute(to_y, "grp", y_pairs)
        return (*halo, from_core, from_y)

    vmem = pl.BlockSpec(memory_space=pltpu.VMEM)
    v, *edges = call(
        start_kernel,
        [shape(planes, rows, extent), shape(planes, extent), shape(planes, extent)],
        [source, fine[CENTER : CENTER + 1]],
    )
    padded_fine = pltpu.VMEM((3, planes + 2, rows + 16, extent), jnp.float32)

    sent = call(
        coefficient_edges_kernel,
        [shape(27, middle_planes, 2, middle_extent)] * 2,
        [middle],
    )
    middle_center = middle[CENTER : CENTER + 1]
    halo_c = along_sub(sent)
    start = middle_planes * (middle_extent // LANES) * ROWS
    mine = call(
        coefficient_pack_kernel,
        shape(27, start + coarse_planes * coarse_rows, LANES),
        [middle, *halo_c, coarse],
    )
    parts = {0: mine}
    bit = groups // 2
    while bit:
        pairs = [(i, i ^ bit) for i in range(groups)]
        for known in sorted(parts):
            parts[known ^ bit] = lax.ppermute(parts[known], "grp", pairs)
        bit //= 2
    parts = [parts[j] for j in range(groups)]

    for _ in range(NU0 - 1):
        v, *edges = call(
            functools.partial(sweep_kernel, groups),
            [shape(planes, rows, extent), shape(planes, extent), shape(planes, extent)],
            [v, source, fine, *exchange(v, edges)],
            [padded_fine],
        )
    fine_iterate = v
    middle_source, *edges = call(
        functools.partial(residual_kernel, groups),
        [shape(middle_planes, middle_rows, middle_extent)]
        + [shape(4 * middle_planes, middle_extent)] * 2,
        [v, source, fine, *exchange(v, edges), middle_center],
        [padded_fine, pltpu.VMEM((planes // 2 * rows, extent), jnp.float32)],
    )
    packed = call(
        middle_faces_kernel,
        shape(middle_planes * ROWS + 8, middle_extent),
        [middle_source, *along_sub(edges)],
    )
    packed = lax.all_gather(packed, "grp", axis=0, tiled=False)
    middle_iterate, coarse_source = call(
        functools.partial(middle_kernel, groups, subs, middle_planes),
        [
            shape(middle_planes, middle_rows, middle_extent),
            shape(subs, groups * coarse_planes, coarse_rows // subs, coarse_extent),
        ],
        [packed, *parts],
        [
            pltpu.VMEM((3, groups * middle_planes + 2, ROWS + 16, middle_extent), jnp.float32),
            pltpu.VMEM((middle_extent // LANES, ROWS, LANES), jnp.float32),
        ],
    )
    gathered = lax.all_to_all(coarse_source, "sub", 0, 0, tiled=True)
    coarse_iterate = call(
        functools.partial(coarse_kernel, groups, subs, coarse_planes, start),
        shape(coarse_planes, coarse_rows, coarse_extent),
        [gathered, *parts],
        [
            pltpu.VMEM((3, groups * coarse_planes + 2, coarse_rows + 16, coarse_extent), jnp.float32),
            pltpu.VMEM((groups * coarse_planes, coarse_rows, coarse_extent), jnp.float32),
        ],
    )
    return fine_iterate, middle_iterate, coarse_iterate


def solution(mesh):
    placed = (
        P("grp", "sub", None),
        P(None, "grp", "sub", None),
        P(None, "grp", "sub", None),
        P(None, "grp", None, None),
    )
    return jax.shard_map(
        body,
        mesh=mesh,
        in_specs=placed,
        out_specs=(P("grp", "sub", None), P("grp", "sub", None), P("grp", None, None)),
        check_vma=False,
    )
```

```python
import functools

import jax
import jax.numpy as jnp
from jax import lax
from jax.experimental import pallas as pl
from jax.experimental.pallas import tpu as pltpu
from jax.sharding import PartitionSpec as P

NU0 = 3
NB = 16
WEIGHT = 0.8
CENTER = 13
LANES = 128
ROWS = 8
BASE = 8


def shape(*dims):
    return jax.ShapeDtypeStruct(dims, jnp.float32)


def call(kernel, outs, args, scratch=(), in_specs=None, limit=12, cost=20_000_000):
    vmem = pl.BlockSpec(memory_space=pltpu.VMEM)
    return pl.pallas_call(
        kernel,
        out_shape=outs,
        in_specs=in_specs or [vmem] * len(args),
        out_specs=jax.tree.map(lambda _: vmem, outs),
        scratch_shapes=list(scratch),
        compiler_params=pltpu.CompilerParams(vmem_limit_bytes=limit << 20),
        cost_estimate=pl.CostEstimate(flops=0, bytes_accessed=cost, transcendentals=0),
    )(*args)


def even(axis):
    return lax.rem(lax.axis_index(axis), 2) == 0


def pick(condition, a, b):
    return jnp.where(jnp.broadcast_to(condition, a.shape), a, b)


def shifted(values):
    extent = values.shape[-1]
    lane = lax.broadcasted_iota(jnp.int32, values.shape, values.ndim - 1)
    before = pltpu.roll(values, 1, values.ndim - 1)
    after = pltpu.roll(values, extent - 1, values.ndim - 1)
    return (
        jnp.where(lane == 0, 0.0, before),
        values,
        jnp.where(lane == extent - 1, 0.0, after),
    )


def place(padded, plane, row, values):
    for z, part in enumerate(shifted(values)):
        padded[z, plane, row : row + values.shape[0], :] = part


def stencil(padded, coefficient, first, planes, row, lanes, center=True):
    sums = [None] * planes
    for p in range(planes + 2):
        near = [
            [padded[z, first + p, row - 1 + y : row - 1 + y + ROWS, lanes] for z in range(3)]
            for y in range(3)
        ]
        for x in range(3):
            if not 0 <= p - x < planes:
                continue
            for y in range(3):
                for z in range(3):
                    if not center and 9 * x + 3 * y + z == CENTER:
                        continue
                    term = coefficient(9 * x + 3 * y + z, p - x, lanes) * near[y][z]
                    sums[p - x] = term if sums[p - x] is None else sums[p - x] + term
    return sums


def lane_tiles(extent):
    return [slice(l, l + LANES) for l in range(0, extent, LANES)]


def paired_lanes(values):
    extent = values.shape[-1]
    row = lax.broadcasted_iota(jnp.int32, (extent, extent // 2), 0)
    column = lax.broadcasted_iota(jnp.int32, (extent, extent // 2), 1)
    pairs = jnp.where(lax.shift_right_logical(row, 1) == column, 1.0, 0.0)
    return lax.dot_general(
        values,
        pairs,
        (((1,), (0,)), ((), ())),
        precision=lax.Precision.HIGHEST,
        preferred_element_type=jnp.float32,
    )


def paired_rows(values):
    return values + pltpu.roll(values, values.shape[0] - 1, 0)


def put_edges(v, to_x, to_zx):
    last = v.shape[1] - 1
    for x in range(v.shape[0]):
        first_row, last_row = v[x, 0:1, :], v[x, last : last + 1, :]
        to_x[x : x + 1, :] = pick(even("sub"), last_row, first_row)
        to_zx[x : x + 1, :] = pick(even("sub"), first_row, last_row)


def edges_kernel(v, to_x, to_zx):
    put_edges(v, to_x, to_zx)


def keep_kernel(v, out):
    out[...] = v[...]


def faces_kernel(v, from_x, from_zx, to_core, to_y):
    planes, rows, _ = v.shape
    before = pick(even("sub"), from_zx[0:planes, :], from_x[...])
    after = pick(even("sub"), from_x[...], from_zx[0:planes, :])
    for ref, swap in ((to_core, False), (to_y, True)):
        def choose(a, b):
            return pick(even("grp"), b, a) if swap else pick(even("grp"), a, b)

        ref[0:rows, :] = choose(v[planes - 1], v[0])
        ref[rows : rows + 1, :] = choose(before[planes - 1 :], before[0:1])
        ref[rows + 1 : rows + 2, :] = choose(after[planes - 1 :], after[0:1])


def fill_fine(groups, padded, v, from_x, from_zx, from_core, from_y):
    planes, rows, _ = v.shape
    group = lax.axis_index("grp")
    for x in range(planes):
        place(padded, x + 1, BASE, v[x])
    befores = shifted(pick(even("sub"), from_zx[0:planes, :], from_x[...]))
    afters = shifted(pick(even("sub"), from_x[...], from_zx[0:planes, :]))
    for z in range(3):
        for x in range(planes):
            padded[z, x + 1, BASE - 1 : BASE, :] = befores[z][x : x + 1]
            padded[z, x + 1, BASE + rows : BASE + rows + 1, :] = afters[z][x : x + 1]
    low = pick(even("grp"), from_y[...], from_core[...])
    high = pick(even("grp"), from_core[...], from_y[...])
    low = pick(group == 0, jnp.zeros_like(low), low)
    high = pick(group == groups - 1, jnp.zeros_like(high), high)
    for plane, face in ((0, low), (planes + 1, high)):
        for z, part in enumerate(shifted(face)):
            padded[z, plane, BASE : BASE + rows, :] = part[0:rows]
            padded[z, plane, BASE - 1 : BASE, :] = part[rows : rows + 1]
            padded[z, plane, BASE + rows : BASE + rows + 1, :] = part[rows + 1 : rows + 2]


def sweep_kernel(groups, v, first, c, from_x, from_zx, from_core, from_y, out, to_x, to_zx, padded):
    planes, rows, extent = v.shape
    fill_fine(groups, padded, v, from_x, from_zx, from_core, from_y)
    for lanes in lane_tiles(extent):
        sums = stencil(padded, lambda k, x, l: c[k, x, :, l], 0, planes, BASE, lanes, center=False)
        for x in range(planes):
            out[x, :, lanes] = first[x, :, lanes] + (1.0 - WEIGHT) * v[x, :, lanes] - sums[x]
    put_edges(out, to_x, to_zx)


def residual_kernel(groups, v, first, c, from_x, from_zx, from_core, from_y, center, iterate, to_x, to_zx, padded, held):
    planes, rows, extent = v.shape
    fill_fine(groups, padded, v, from_x, from_zx, from_core, from_y)
    for lanes in lane_tiles(extent):
        sums = stencil(padded, lambda k, x, l: c[k, x, :, l], 0, planes, BASE, lanes, center=False)
        r = []
        for x in range(planes):
            part = first[x, :, lanes] - WEIGHT * v[x, :, lanes] - sums[x]
            r.append((1.0 / WEIGHT) * c[CENTER, x, :, lanes] * part)
        for x in range(planes // 2):
            held[x * rows : (x + 1) * rows, lanes] = r[2 * x] + r[2 * x + 1]
    total = (0.5 * WEIGHT) * paired_rows(paired_lanes(held[...]))
    half = rows // 2
    for x in range(planes // 2):
        for y in range(half):
            row = x * rows + 2 * y
            iterate[x, y : y + 1, :] = total[row : row + 1]
    iterate[...] = iterate[...] / center[...]
    for x in range(planes // 2):
        first, last = iterate[x, 0:3, :], iterate[x, half - 3 : half, :]
        to_x[4 * x : 4 * x + 3, :] = pick(even("sub"), last, first)
        to_zx[4 * x : 4 * x + 3, :] = pick(even("sub"), first, last)


def middle_faces_kernel(mine, from_x, from_zx, out):
    planes, half, _ = mine.shape
    before = pick(even("sub"), from_zx[0 : 4 * planes, :], from_x[...])
    after = pick(even("sub"), from_x[...], from_zx[0 : 4 * planes, :])
    for x in range(planes):
        row = x * ROWS
        out[row : row + 2, :] = before[4 * x + 1 : 4 * x + 3]
        out[row + 2 : row + 2 + half, :] = mine[x]
        out[row + 2 + half : row + ROWS, :] = after[4 * x : 4 * x + 2]
        extra = planes * ROWS + 2 * x
        out[extra : extra + 1, :] = before[4 * x : 4 * x + 1]
        out[extra + 1 : extra + 2, :] = after[4 * x + 2 : 4 * x + 3]


def coefficient_edges_kernel(c, to_x, to_zx):
    rows = c.shape[2]
    first, last = c[:, :, 0:2, :], c[:, :, rows - 2 : rows, :]
    to_x[...] = pick(even("sub"), last, first)
    to_zx[...] = pick(even("sub"), first, last)


def coefficient_scale_kernel(c, out):
    for x in range(c.shape[1]):
        out[:, x] = scaled(c[:, x])


def scaled(c):
    center = c[CENTER : CENTER + 1]
    ratio = WEIGHT * c / jnp.where(center > 0.0, center, 1.0)
    index = lax.broadcasted_iota(jnp.int32, c.shape, 0)
    return jnp.where(index == CENTER, c, ratio)


def coefficient_pack_kernel(known, *refs):
    coarse, (c, from_x, from_zx, _, __, middle_part, whole) = refs[:known], refs[known:]
    _, planes, rows, extent = c.shape
    tiles = extent // LANES
    before = pick(even("sub"), from_zx[...], from_x[...])
    after = pick(even("sub"), from_x[...], from_zx[...])
    for x in range(planes):
        for l, lanes in enumerate(lane_tiles(extent)):
            row = (x * tiles + l) * ROWS
            whole[:, row : row + 2, :] = before[:, x, :, lanes]
            whole[:, row + 2 : row + 2 + rows, :] = c[:, x, :, lanes]
            whole[:, row + 2 + rows : row + ROWS, :] = after[:, x, :, lanes]
    row = planes * tiles * ROWS
    for t in range(0, row, ROWS):
        part = scaled(whole[:, t : t + ROWS, :])
        whole[:, t : t + ROWS, :] = part
        middle_part[:, t : t + ROWS, :] = part
    for ref in coarse:
        for x in range(ref.shape[1]):
            for t in range(0, ref.shape[2], ROWS):
                whole[:, row : row + ROWS, :] = scaled(ref[:, x, t : t + ROWS, :])
                row += ROWS


def middle_kernel(groups, planes, packed, near_core, near_y, far_below, far_above, own, core, other, iterate, coarse, padded, first, fresh):
    extent = packed.shape[-1]
    tiles = extent // LANES
    half = ROWS - 4
    group = lax.axis_index("grp")
    window = 3 * planes

    below = pick(even("grp"), near_y[...], near_core[...])
    above = pick(even("grp"), near_core[...], near_y[...])
    blocks = {-2: far_below[...], -1: below, 0: packed[...], 1: above, 2: far_above[...]}
    for p in range(window + 2):
        away, x = (p - 1) // planes - 1, (p - 1) % planes
        inside = (group + away >= 0) & (group + away < groups)
        block = pick(inside, blocks[away], jnp.zeros_like(blocks[away]))
        extra = planes * ROWS + 2 * x
        for row, count, at in ((x * ROWS, ROWS, BASE), (extra, 1, BASE - 1), (extra + 1, 1, BASE + ROWS)):
            v = block[row : row + count]
            place(padded, p, at, v)
            if count == ROWS and 0 < p <= window:
                first[p - 1] = v

    def work(parts):
        def coefficient(low):
            def get(k, x, lanes):
                w = low + x
                row = (w % planes * tiles + lanes.start // LANES) * ROWS
                return parts[w // planes][k, row : row + ROWS, :]

            return get

        for margin in range(2):
            low, high = planes - 2 + margin, 2 * planes + 2 - margin
            for lanes in lane_tiles(extent):
                sums = stencil(padded, coefficient(low), low, high - low, BASE, lanes, center=False)
                for w in range(low, high):
                    v = padded[1, w + 1, BASE : BASE + ROWS, lanes]
                    fresh[w, :, lanes] = first[w, :, lanes] + (1.0 - WEIGHT) * v - sums[w - low]
            for w in range(low, high):
                place(padded, w + 1, BASE, fresh[w])
        low = planes
        for lanes in lane_tiles(extent):
            sums = stencil(padded, coefficient(low), low, planes, BASE, lanes, center=False)
            for x in range(planes):
                v = fresh[low + x, :, lanes]
                rest = first[low + x, :, lanes] - WEIGHT * v - sums[x]
                fresh[x, :, lanes] = (1.0 / WEIGHT) * coefficient(low)(CENTER, x, lanes) * rest

    @pl.when(even("grp"))
    def _():
        work((other, own, core))

    @pl.when(jnp.logical_not(even("grp")))
    def _():
        work((core, own, other))

    for x in range(planes):
        iterate[x] = padded[1, planes + x + 1, BASE + 2 : BASE + 2 + half, :]
    place_of = lax.broadcasted_iota(jnp.int32, (ROWS, extent // 2), 0)
    for x in range(planes // 2):
        total = 0.5 * paired_rows(paired_lanes(fresh[2 * x] + fresh[2 * x + 1]))
        value = pltpu.roll(total, ROWS - 2, 0)
        for i in range(1, half // 2):
            value = jnp.where(place_of == i, pltpu.roll(total, ROWS - 2 - i, 0), value)
        for device in range(coarse.shape[0]):
            coarse[device, x] = value[: half // 2]


def coarse_order_kernel(planes, rows, start, offsets, own, core, out):
    group = lax.axis_index("grp")
    for ref, flip in ((own, 0), (core, 1)):
        for i, offset in enumerate(offsets):
            owner = jnp.bitwise_xor(group, offset ^ flip)
            for x in range(planes):
                row = start + (i * planes + x) * rows
                out[owner * planes + x] = ref[:, row : row + rows, :]


def coarse_kernel(groups, planes, gathered, c, out, padded, first):
    total, rows, extent = first.shape
    subs = gathered.shape[0] // groups
    each = rows // subs
    for plane in range(total + 2):
        for z in range(3):
            padded[z, plane, :, :] = jnp.zeros(padded.shape[2:], jnp.float32)
    for g in range(groups):
        for s in range(subs):
            for x in range(planes):
                first[g * planes + x, s * each : (s + 1) * each, :] = gathered[g * subs + s, x]
    for p in range(total):
        first[p] = WEIGHT * first[p] / c[p, CENTER]
        place(padded, p + 1, BASE, first[p])

    def sweep(_, carry):
        fresh = []
        for t in range(0, rows, ROWS):
            sums = stencil(
                padded,
                lambda k, x, l: c[x, k, t : t + ROWS, l],
                0,
                total,
                BASE + t,
                slice(0, extent),
                center=False,
            )
            for p in range(total):
                v = padded[1, p + 1, BASE + t : BASE + t + ROWS, :]
                fresh.append((p + 1, BASE + t, first[p, t : t + ROWS, :] + (1.0 - WEIGHT) * v - sums[p]))
        for plane, row, v in fresh:
            place(padded, plane, row, v)
        return carry

    lax.fori_loop(0, NB - 1, sweep, 0)
    for x in range(planes):
        out[x] = padded[1, lax.axis_index("grp") * planes + x + 1, BASE : BASE + rows, :]


def after(value, *others):
    return lax.optimization_barrier((value, *others))[0]


def after_all(values, *others):
    return lax.optimization_barrier((*values, *others))[: len(values)]


def swaps(pairs):
    return [p for a, b in pairs for p in ((a, b), (b, a))]


def body(source, fine, middle, coarse):
    groups, subs = lax.axis_size("grp"), lax.axis_size("sub")
    _, planes, rows, extent = fine.shape
    _, middle_planes, middle_rows, middle_extent = middle.shape
    _, coarse_planes, coarse_rows, coarse_extent = coarse.shape

    x_pairs = swaps([(i, i + 1) for i in range(0, subs, 2)])
    zx_pairs = swaps([(i, i + 1) for i in range(1, subs - 1, 2)])
    core_pairs = swaps([(i, i + 1) for i in range(0, groups, 2)])
    y_pairs = swaps([(i, i + 1) for i in range(1, groups - 1, 2)])
    y_ring = y_pairs + [(groups - 1, 0), (0, groups - 1)]

    def along_sub(pair):
        to_x, to_zx = pair
        from_x = lax.ppermute(to_x, "sub", x_pairs)
        return from_x, lax.ppermute(to_zx, "sub", zx_pairs)

    def along_grp(v, halo):
        to_core, to_y = call(faces_kernel, [shape(rows + 8, extent)] * 2, [v, *halo])
        from_core = lax.ppermute(to_core, "grp", core_pairs)
        from_y = lax.ppermute(to_y, "grp", y_ring)
        return (*halo, from_core, from_y)

    weights = call(coefficient_scale_kernel, shape(*fine.shape), [fine])
    v = WEIGHT * source / fine[CENTER]
    first = v
    to_x, to_zx = call(edges_kernel, [shape(planes, extent), shape(4 * planes, extent)], [v])
    padded_fine = pltpu.VMEM((3, planes + 2, rows + 16, extent), jnp.float32)

    def sweep(v, halo):
        v, *edges = call(
            functools.partial(sweep_kernel, groups),
            [shape(planes, rows, extent), shape(planes, extent), shape(4 * planes, extent)],
            [v, first, weights, *halo],
            [padded_fine],
        )
        return v, along_sub(edges)

    edges_c = call(
        coefficient_edges_kernel,
        [shape(27, middle_planes, 2, middle_extent)] * 2,
        [middle],
    )
    halo = along_sub((to_x, to_zx))
    halo = along_grp(after(v, weights), halo)
    halo_c = along_sub(after_all(edges_c, *halo[2:]))
    v = after(v, *edges_c)
    known = {0: after(coarse, *halo[2:])}
    bit = groups // 2
    while bit > 1:
        for offset in sorted(known):
            known[offset ^ bit] = lax.ppermute(known[offset], "grp", [(i, i ^ bit) for i in range(groups)])
        bit //= 2
    offsets = sorted(known)
    v, halo = sweep(v, halo)
    halo = along_grp(v, halo)
    start = middle_planes * (middle_extent // LANES) * ROWS
    middle_part, own = call(
        functools.partial(coefficient_pack_kernel, len(known)),
        [shape(27, start, LANES), shape(27, start + len(known) * coarse_planes * coarse_rows, LANES)],
        [*(known[o] for o in offsets), middle, *halo_c, *halo[2:]],
    )
    core = lax.ppermute(own, "grp", core_pairs)
    other = lax.ppermute(middle_part, "grp", y_pairs)
    v, halo = sweep(v, halo)
    fine_iterate = call(keep_kernel, shape(planes, rows, extent), [v])
    halo = along_grp(v, halo)
    iterate, *edges = call(
        functools.partial(residual_kernel, groups),
        [shape(middle_planes, middle_rows, middle_extent)]
        + [shape(4 * middle_planes, middle_extent), shape(8 * middle_planes, middle_extent)],
        [v, first, weights, *halo, middle[CENTER]],
        [padded_fine, pltpu.VMEM((planes // 2 * rows, extent), jnp.float32)],
    )
    packed = call(
        middle_faces_kernel,
        shape(middle_planes * ROWS + 8, middle_extent),
        [iterate, *along_sub(edges)],
    )
    near_core = lax.ppermute(packed, "grp", core_pairs)
    if groups == 4:
        far_below = far_above = lax.ppermute(packed, "grp", swaps([(0, 2), (1, 3)]))
        near_y = lax.ppermute(far_below, "grp", core_pairs)
    else:
        near_y = lax.ppermute(packed, "grp", y_pairs)
        up = [(i, i + 2) for i in range(groups - 2)]
        far_below = lax.ppermute(packed, "grp", up)
        far_above = lax.ppermute(packed, "grp", [(j, i) for i, j in up])
    window = pltpu.VMEM((3 * middle_planes, ROWS, middle_extent), jnp.float32)
    middle_iterate, coarse_source = call(
        functools.partial(middle_kernel, groups, middle_planes),
        [
            shape(middle_planes, middle_rows, middle_extent),
            shape(groups * subs, coarse_planes, coarse_rows // subs, coarse_extent),
        ],
        [packed, near_core, near_y, far_below, far_above, own, core, other],
        [
            pltpu.VMEM((3, 3 * middle_planes + 2, ROWS + 16, middle_extent), jnp.float32),
            window,
            window,
        ],
    )
    gathered = lax.all_to_all(coarse_source, ("grp", "sub"), 0, 0, tiled=True)
    total = groups * coarse_planes
    ordered = call(
        functools.partial(coarse_order_kernel, coarse_planes, coarse_rows, start, offsets),
        shape(total, 27, coarse_rows, coarse_extent),
        [own, core],
    )
    coarse_iterate = call(
        functools.partial(coarse_kernel, groups, coarse_planes),
        shape(coarse_planes, coarse_rows, coarse_extent),
        [gathered, ordered],
        [
            pltpu.VMEM((3, total + 2, coarse_rows + 16, coarse_extent), jnp.float32),
            pltpu.VMEM((total, coarse_rows, coarse_extent), jnp.float32),
        ],
    )
    return fine_iterate, middle_iterate, coarse_iterate


def solution(mesh):
    placed = (
        P("grp", "sub", None),
        P(None, "grp", "sub", None),
        P(None, "grp", "sub", None),
        P(None, "grp", None, None),
    )
    return jax.shard_map(
        body,
        mesh=mesh,
        in_specs=placed,
        out_specs=(P("grp", "sub", None), P("grp", "sub", None), P("grp", None, None)),
        check_vma=False,
    )
```

```python
import functools

import jax
import jax.numpy as jnp
from jax import lax
from jax.experimental import pallas as pl
from jax.experimental.pallas import tpu as pltpu
from jax.sharding import PartitionSpec as P

NU0 = 3
NB = 16
WEIGHT = 0.8
CENTER = 13
LANES = 128
ROWS = 8
BASE = 8


def shape(*dims):
    return jax.ShapeDtypeStruct(dims, jnp.float32)


def call(kernel, outs, args, scratch=(), in_specs=None, limit=12, cost=20_000_000):
    vmem = pl.BlockSpec(memory_space=pltpu.VMEM)
    return pl.pallas_call(
        kernel,
        out_shape=outs,
        in_specs=in_specs or [vmem] * len(args),
        out_specs=jax.tree.map(lambda _: vmem, outs),
        scratch_shapes=list(scratch),
        compiler_params=pltpu.CompilerParams(vmem_limit_bytes=limit << 20),
        cost_estimate=pl.CostEstimate(flops=0, bytes_accessed=cost, transcendentals=0),
    )(*args)


def even(axis):
    return lax.rem(lax.axis_index(axis), 2) == 0


def pick(condition, a, b):
    return jnp.where(jnp.broadcast_to(condition, a.shape), a, b)


def sides(from_x, from_zx):
    sub, subs = lax.axis_index("sub"), lax.axis_size("sub")
    from_zx = pick((sub == 0) | (sub == subs - 1), jnp.zeros_like(from_zx), from_zx)
    return pick(even("sub"), from_zx, from_x), pick(even("sub"), from_x, from_zx)


def shifted(values):
    extent = values.shape[-1]
    lane = lax.broadcasted_iota(jnp.int32, values.shape, values.ndim - 1)
    before = pltpu.roll(values, 1, values.ndim - 1)
    after = pltpu.roll(values, extent - 1, values.ndim - 1)
    return (
        jnp.where(lane == 0, 0.0, before),
        values,
        jnp.where(lane == extent - 1, 0.0, after),
    )


def place(padded, plane, row, values):
    for z, part in enumerate(shifted(values)):
        padded[z, plane, row : row + values.shape[0], :] = part


def stencil(padded, coefficient, first, planes, row, lanes, center=True):
    sums = [None] * planes
    for p in range(planes + 2):
        near = [
            [padded[z, first + p, row - 1 + y : row - 1 + y + ROWS, lanes] for z in range(3)]
            for y in range(3)
        ]
        for x in range(3):
            if not 0 <= p - x < planes:
                continue
            for y in range(3):
                for z in range(3):
                    if not center and 9 * x + 3 * y + z == CENTER:
                        continue
                    term = coefficient(9 * x + 3 * y + z, p - x, lanes) * near[y][z]
                    sums[p - x] = term if sums[p - x] is None else sums[p - x] + term
    return sums


def lane_tiles(extent):
    return [slice(l, l + LANES) for l in range(0, extent, LANES)]


def paired_lanes(values):
    extent = values.shape[-1]
    row = lax.broadcasted_iota(jnp.int32, (extent, extent // 2), 0)
    column = lax.broadcasted_iota(jnp.int32, (extent, extent // 2), 1)
    pairs = jnp.where(lax.shift_right_logical(row, 1) == column, 1.0, 0.0)
    return lax.dot_general(
        values,
        pairs,
        (((1,), (0,)), ((), ())),
        precision=lax.Precision.HIGHEST,
        preferred_element_type=jnp.float32,
    )


def paired_rows(values):
    return values + pltpu.roll(values, values.shape[0] - 1, 0)


def put_edges(v, to_x, to_zx):
    last = v.shape[1] - 1
    for x in range(v.shape[0]):
        first_row, last_row = v[x, 0:1, :], v[x, last : last + 1, :]
        to_x[x : x + 1, :] = pick(even("sub"), last_row, first_row)
        to_zx[x : x + 1, :] = pick(even("sub"), first_row, last_row)


def edges_kernel(v, to_x, to_zx):
    put_edges(v, to_x, to_zx)


def keep_kernel(v, out):
    out[...] = v[...]


def faces_kernel(v, from_x, from_zx, to_core, to_y):
    planes, rows, _ = v.shape
    before, after = sides(from_x[...], from_zx[0:planes, :])
    for ref, swap in ((to_core, False), (to_y, True)):
        def choose(a, b):
            return pick(even("grp"), b, a) if swap else pick(even("grp"), a, b)

        ref[0:rows, :] = choose(v[planes - 1], v[0])
        ref[rows : rows + 1, :] = choose(before[planes - 1 :], before[0:1])
        ref[rows + 1 : rows + 2, :] = choose(after[planes - 1 :], after[0:1])


def fill_fine(groups, padded, v, from_x, from_zx, from_core, from_y):
    planes, rows, _ = v.shape
    group = lax.axis_index("grp")
    for x in range(planes):
        place(padded, x + 1, BASE, v[x])
    befores, afters = map(shifted, sides(from_x[...], from_zx[0:planes, :]))
    for z in range(3):
        for x in range(planes):
            padded[z, x + 1, BASE - 1 : BASE, :] = befores[z][x : x + 1]
            padded[z, x + 1, BASE + rows : BASE + rows + 1, :] = afters[z][x : x + 1]
    low = pick(even("grp"), from_y[...], from_core[...])
    high = pick(even("grp"), from_core[...], from_y[...])
    low = pick(group == 0, jnp.zeros_like(low), low)
    high = pick(group == groups - 1, jnp.zeros_like(high), high)
    for plane, face in ((0, low), (planes + 1, high)):
        for z, part in enumerate(shifted(face)):
            padded[z, plane, BASE : BASE + rows, :] = part[0:rows]
            padded[z, plane, BASE - 1 : BASE, :] = part[rows : rows + 1]
            padded[z, plane, BASE + rows : BASE + rows + 1, :] = part[rows + 1 : rows + 2]


def sweep_kernel(groups, v, first, c, from_x, from_zx, from_core, from_y, out, to_x, to_zx, padded):
    planes, rows, extent = v.shape
    fill_fine(groups, padded, v, from_x, from_zx, from_core, from_y)
    for lanes in lane_tiles(extent):
        sums = stencil(padded, lambda k, x, l: c[k, x, :, l], 0, planes, BASE, lanes, center=False)
        for x in range(planes):
            out[x, :, lanes] = first[x, :, lanes] + (1.0 - WEIGHT) * v[x, :, lanes] - sums[x]
    put_edges(out, to_x, to_zx)


def residual_kernel(groups, v, first, c, from_x, from_zx, from_core, from_y, center, iterate, to_x, to_zx, padded, held):
    planes, rows, extent = v.shape
    fill_fine(groups, padded, v, from_x, from_zx, from_core, from_y)
    for lanes in lane_tiles(extent):
        sums = stencil(padded, lambda k, x, l: c[k, x, :, l], 0, planes, BASE, lanes, center=False)
        r = []
        for x in range(planes):
            part = first[x, :, lanes] - WEIGHT * v[x, :, lanes] - sums[x]
            r.append((1.0 / WEIGHT) * c[CENTER, x, :, lanes] * part)
        for x in range(planes // 2):
            held[x * rows : (x + 1) * rows, lanes] = r[2 * x] + r[2 * x + 1]
    total = (0.5 * WEIGHT) * paired_rows(paired_lanes(held[...]))
    half = rows // 2
    for x in range(planes // 2):
        for y in range(half):
            row = x * rows + 2 * y
            iterate[x, y : y + 1, :] = total[row : row + 1]
    iterate[...] = iterate[...] / center[...]
    for x in range(planes // 2):
        first, last = iterate[x, 0:3, :], iterate[x, half - 3 : half, :]
        to_x[4 * x : 4 * x + 3, :] = pick(even("sub"), last, first)
        to_zx[4 * x : 4 * x + 3, :] = pick(even("sub"), first, last)


def middle_faces_kernel(mine, from_x, from_zx, out):
    planes, half, _ = mine.shape
    before, after = sides(from_x[...], from_zx[0 : 4 * planes, :])
    for x in range(planes):
        row = x * ROWS
        out[row : row + 2, :] = before[4 * x + 1 : 4 * x + 3]
        out[row + 2 : row + 2 + half, :] = mine[x]
        out[row + 2 + half : row + ROWS, :] = after[4 * x : 4 * x + 2]
        extra = planes * ROWS + 2 * x
        out[extra : extra + 1, :] = before[4 * x : 4 * x + 1]
        out[extra + 1 : extra + 2, :] = after[4 * x + 2 : 4 * x + 3]


def coefficient_edges_kernel(c, to_x, to_zx):
    rows = c.shape[2]
    first, last = c[:, :, 0:2, :], c[:, :, rows - 2 : rows, :]
    to_x[...] = pick(even("sub"), last, first)
    to_zx[...] = pick(even("sub"), first, last)


def coefficient_scale_kernel(c, out):
    for x in range(c.shape[1]):
        out[:, x] = scaled(c[:, x])


def scaled(c):
    center = c[CENTER : CENTER + 1]
    ratio = WEIGHT * c / jnp.where(center > 0.0, center, 1.0)
    index = lax.broadcasted_iota(jnp.int32, c.shape, 0)
    return jnp.where(index == CENTER, c, ratio)


def coefficient_pack_kernel(known, *refs):
    coarse, (c, from_x, from_zx, _, __, middle_part, whole) = refs[:known], refs[known:]
    _, planes, rows, extent = c.shape
    tiles = extent // LANES
    before, after = sides(from_x[...], from_zx[...])
    for x in range(planes):
        for l, lanes in enumerate(lane_tiles(extent)):
            row = (x * tiles + l) * ROWS
            whole[:, row : row + 2, :] = before[:, x, :, lanes]
            whole[:, row + 2 : row + 2 + rows, :] = c[:, x, :, lanes]
            whole[:, row + 2 + rows : row + ROWS, :] = after[:, x, :, lanes]
    row = planes * tiles * ROWS
    for t in range(0, row, ROWS):
        part = scaled(whole[:, t : t + ROWS, :])
        whole[:, t : t + ROWS, :] = part
        middle_part[:, t : t + ROWS, :] = part
    for ref in coarse:
        for x in range(ref.shape[1]):
            for t in range(0, ref.shape[2], ROWS):
                whole[:, row : row + ROWS, :] = scaled(ref[:, x, t : t + ROWS, :])
                row += ROWS


def middle_kernel(groups, planes, packed, near_core, near_y, far_below, far_above, own, core, other, iterate, coarse, padded, first, fresh):
    extent = packed.shape[-1]
    tiles = extent // LANES
    half = ROWS - 4
    group = lax.axis_index("grp")
    window = 3 * planes

    below = pick(even("grp"), near_y[...], near_core[...])
    above = pick(even("grp"), near_core[...], near_y[...])
    blocks = {-2: far_below[...], -1: below, 0: packed[...], 1: above, 2: far_above[...]}
    for p in range(window + 2):
        away, x = (p - 1) // planes - 1, (p - 1) % planes
        inside = (group + away >= 0) & (group + away < groups)
        block = pick(inside, blocks[away], jnp.zeros_like(blocks[away]))
        extra = planes * ROWS + 2 * x
        for row, count, at in ((x * ROWS, ROWS, BASE), (extra, 1, BASE - 1), (extra + 1, 1, BASE + ROWS)):
            v = block[row : row + count]
            place(padded, p, at, v)
            if count == ROWS and 0 < p <= window:
                first[p - 1] = v

    def work(parts):
        def coefficient(low):
            def get(k, x, lanes):
                w = low + x
                row = (w % planes * tiles + lanes.start // LANES) * ROWS
                return parts[w // planes][k, row : row + ROWS, :]

            return get

        for margin in range(2):
            low, high = planes - 2 + margin, 2 * planes + 2 - margin
            for lanes in lane_tiles(extent):
                sums = stencil(padded, coefficient(low), low, high - low, BASE, lanes, center=False)
                for w in range(low, high):
                    v = padded[1, w + 1, BASE : BASE + ROWS, lanes]
                    fresh[w, :, lanes] = first[w, :, lanes] + (1.0 - WEIGHT) * v - sums[w - low]
            for w in range(low, high):
                place(padded, w + 1, BASE, fresh[w])
        low = planes
        for lanes in lane_tiles(extent):
            sums = stencil(padded, coefficient(low), low, planes, BASE, lanes, center=False)
            for x in range(planes):
                v = fresh[low + x, :, lanes]
                rest = first[low + x, :, lanes] - WEIGHT * v - sums[x]
                fresh[x, :, lanes] = (1.0 / WEIGHT) * coefficient(low)(CENTER, x, lanes) * rest

    @pl.when(even("grp"))
    def _():
        work((other, own, core))

    @pl.when(jnp.logical_not(even("grp")))
    def _():
        work((core, own, other))

    for x in range(planes):
        iterate[x] = padded[1, planes + x + 1, BASE + 2 : BASE + 2 + half, :]
    place_of = lax.broadcasted_iota(jnp.int32, (ROWS, extent // 2), 0)
    for x in range(planes // 2):
        total = 0.5 * paired_rows(paired_lanes(fresh[2 * x] + fresh[2 * x + 1]))
        value = pltpu.roll(total, ROWS - 2, 0)
        for i in range(1, half // 2):
            value = jnp.where(place_of == i, pltpu.roll(total, ROWS - 2 - i, 0), value)
        for device in range(coarse.shape[0]):
            coarse[device, x] = value[: half // 2]


def coarse_order_kernel(planes, rows, start, offsets, own, core, out):
    group = lax.axis_index("grp")
    for ref, flip in ((own, 0), (core, 1)):
        for i, offset in enumerate(offsets):
            owner = jnp.bitwise_xor(group, offset ^ flip)
            for x in range(planes):
                row = start + (i * planes + x) * rows
                out[owner * planes + x] = ref[:, row : row + rows, :]


def coarse_kernel(groups, planes, gathered, c, out, padded, first):
    total, rows, extent = first.shape
    subs = gathered.shape[0] // groups
    each = rows // subs
    for plane in range(total + 2):
        for z in range(3):
            padded[z, plane, :, :] = jnp.zeros(padded.shape[2:], jnp.float32)
    for g in range(groups):
        for s in range(subs):
            for x in range(planes):
                first[g * planes + x, s * each : (s + 1) * each, :] = gathered[g * subs + s, x]
    for p in range(total):
        first[p] = WEIGHT * first[p] / c[p, CENTER]
        place(padded, p + 1, BASE, first[p])

    def sweep(_, carry):
        fresh = []
        for t in range(0, rows, ROWS):
            sums = stencil(
                padded,
                lambda k, x, l: c[x, k, t : t + ROWS, l],
                0,
                total,
                BASE + t,
                slice(0, extent),
                center=False,
            )
            for p in range(total):
                v = padded[1, p + 1, BASE + t : BASE + t + ROWS, :]
                fresh.append((p + 1, BASE + t, first[p, t : t + ROWS, :] + (1.0 - WEIGHT) * v - sums[p]))
        for plane, row, v in fresh:
            place(padded, plane, row, v)
        return carry

    lax.fori_loop(0, NB - 1, sweep, 0)
    for x in range(planes):
        out[x] = padded[1, lax.axis_index("grp") * planes + x + 1, BASE : BASE + rows, :]


def after(value, *others):
    return lax.optimization_barrier((value, *others))[0]


def after_all(values, *others):
    return lax.optimization_barrier((*values, *others))[: len(values)]


def swaps(pairs):
    return [p for a, b in pairs for p in ((a, b), (b, a))]


def body(source, fine, middle, coarse):
    groups, subs = lax.axis_size("grp"), lax.axis_size("sub")
    _, planes, rows, extent = fine.shape
    _, middle_planes, middle_rows, middle_extent = middle.shape
    _, coarse_planes, coarse_rows, coarse_extent = coarse.shape

    x_pairs = swaps([(i, i + 1) for i in range(0, subs, 2)])
    zx_pairs = swaps(
        [(g * subs + i, g * subs + i + 1) for g in range(groups) for i in range(1, subs - 1, 2)]
        + [(g * subs + i, (g + 1) * subs + i) for g in range(0, groups, 2) for i in (0, subs - 1)]
    )
    core_pairs = swaps([(i, i + 1) for i in range(0, groups, 2)])
    y_pairs = swaps([(i, i + 1) for i in range(1, groups - 1, 2)])
    y_ring = y_pairs + [(groups - 1, 0), (0, groups - 1)]

    def along_sub(pair):
        to_x, to_zx = pair
        from_x = lax.ppermute(to_x, "sub", x_pairs)
        return from_x, lax.ppermute(to_zx, ("grp", "sub"), zx_pairs)

    def along_grp(v, halo):
        to_core, to_y = call(faces_kernel, [shape(rows + 8, extent)] * 2, [v, *halo])
        from_core = lax.ppermute(to_core, "grp", core_pairs)
        from_y = lax.ppermute(to_y, "grp", y_ring)
        return (*halo, from_core, from_y)

    weights = call(coefficient_scale_kernel, shape(*fine.shape), [fine])
    v = WEIGHT * source / fine[CENTER]
    first = v
    to_x, to_zx = call(edges_kernel, [shape(planes, extent), shape(4 * planes, extent)], [v])
    padded_fine = pltpu.VMEM((3, planes + 2, rows + 16, extent), jnp.float32)

    def sweep(v, halo):
        v, *edges = call(
            functools.partial(sweep_kernel, groups),
            [shape(planes, rows, extent), shape(planes, extent), shape(4 * planes, extent)],
            [v, first, weights, *halo],
            [padded_fine],
        )
        return v, along_sub(edges)

    edges_c = call(
        coefficient_edges_kernel,
        [shape(27, middle_planes, 2, middle_extent)] * 2,
        [middle],
    )
    halo = along_sub((to_x, to_zx))
    halo_c = along_sub(after_all(edges_c, *halo))
    halo = along_grp(after(v, weights, *edges_c), halo)
    known = {0: after(coarse, *halo[2:])}
    bit = groups // 2
    while bit > 1:
        for offset in sorted(known):
            known[offset ^ bit] = lax.ppermute(known[offset], "grp", [(i, i ^ bit) for i in range(groups)])
        bit //= 2
    offsets = sorted(known)
    v, halo = sweep(v, halo)
    halo = along_grp(v, halo)
    start = middle_planes * (middle_extent // LANES) * ROWS
    middle_part, own = call(
        functools.partial(coefficient_pack_kernel, len(known)),
        [shape(27, start, LANES), shape(27, start + len(known) * coarse_planes * coarse_rows, LANES)],
        [*(known[o] for o in offsets), middle, *halo_c, *halo[2:]],
    )
    core = lax.ppermute(own, "grp", core_pairs)
    other = lax.ppermute(middle_part, "grp", y_pairs)
    v, halo = sweep(v, halo)
    fine_iterate = call(keep_kernel, shape(planes, rows, extent), [v])
    halo = along_grp(v, halo)
    iterate, *edges = call(
        functools.partial(residual_kernel, groups),
        [shape(middle_planes, middle_rows, middle_extent)]
        + [shape(4 * middle_planes, middle_extent), shape(8 * middle_planes, middle_extent)],
        [v, first, weights, *halo, middle[CENTER]],
        [padded_fine, pltpu.VMEM((planes // 2 * rows, extent), jnp.float32)],
    )
    packed = call(
        middle_faces_kernel,
        shape(middle_planes * ROWS + 8, middle_extent),
        [iterate, *along_sub(edges)],
    )
    near_core = lax.ppermute(packed, "grp", core_pairs)
    if groups == 4:
        far_below = far_above = lax.ppermute(packed, "grp", swaps([(0, 2), (1, 3)]))
        near_y = lax.ppermute(far_below, "grp", core_pairs)
    else:
        near_y = lax.ppermute(packed, "grp", y_pairs)
        up = [(i, i + 2) for i in range(groups - 2)]
        far_below = lax.ppermute(packed, "grp", up)
        far_above = lax.ppermute(packed, "grp", [(j, i) for i, j in up])
    window = pltpu.VMEM((3 * middle_planes, ROWS, middle_extent), jnp.float32)
    middle_iterate, coarse_source = call(
        functools.partial(middle_kernel, groups, middle_planes),
        [
            shape(middle_planes, middle_rows, middle_extent),
            shape(groups * subs, coarse_planes, coarse_rows // subs, coarse_extent),
        ],
        [packed, near_core, near_y, far_below, far_above, own, core, other],
        [
            pltpu.VMEM((3, 3 * middle_planes + 2, ROWS + 16, middle_extent), jnp.float32),
            window,
            window,
        ],
    )
    gathered = lax.all_to_all(coarse_source, ("grp", "sub"), 0, 0, tiled=True)
    total = groups * coarse_planes
    ordered = call(
        functools.partial(coarse_order_kernel, coarse_planes, coarse_rows, start, offsets),
        shape(total, 27, coarse_rows, coarse_extent),
        [own, core],
    )
    coarse_iterate = call(
        functools.partial(coarse_kernel, groups, coarse_planes),
        shape(coarse_planes, coarse_rows, coarse_extent),
        [gathered, ordered],
        [
            pltpu.VMEM((3, total + 2, coarse_rows + 16, coarse_extent), jnp.float32),
            pltpu.VMEM((total, coarse_rows, coarse_extent), jnp.float32),
        ],
    )
    return fine_iterate, middle_iterate, coarse_iterate


def solution(mesh):
    placed = (
        P("grp", "sub", None),
        P(None, "grp", "sub", None),
        P(None, "grp", "sub", None),
        P(None, "grp", None, None),
    )
    return jax.shard_map(
        body,
        mesh=mesh,
        in_specs=placed,
        out_specs=(P("grp", "sub", None), P("grp", "sub", None), P("grp", None, None)),
        check_vma=False,
    )
```

```python
import functools

import jax
import jax.numpy as jnp
from jax import lax
from jax.experimental import pallas as pl
from jax.experimental.pallas import tpu as pltpu
from jax.sharding import PartitionSpec as P

NU0 = 3
NB = 16
WEIGHT = 0.8
CENTER = 13
LANES = 128
ROWS = 8


def shape(*dims):
    return jax.ShapeDtypeStruct(dims, jnp.float32)


def call(kernel, outs, args, scratch=(), out_specs=None):
    vmem = pl.BlockSpec(memory_space=pltpu.VMEM)
    return pl.pallas_call(
        kernel,
        out_shape=outs,
        in_specs=[vmem] * len(args),
        out_specs=out_specs or jax.tree.map(lambda _: vmem, outs),
        scratch_shapes=list(scratch),
        compiler_params=pltpu.CompilerParams(vmem_limit_bytes=12 << 20),
    )(*args)


def even(axis):
    return lax.rem(lax.axis_index(axis), 2) == 0


def pick(condition, a, b):
    return jnp.where(jnp.broadcast_to(condition, a.shape), a, b)


def sides(from_x, from_zx):
    sub, subs = lax.axis_index("sub"), lax.axis_size("sub")
    from_zx = pick((sub == 0) | (sub == subs - 1), jnp.zeros_like(from_zx), from_zx)
    return pick(even("sub"), from_zx, from_x), pick(even("sub"), from_x, from_zx)


def rolled(values):
    extent = values.shape[-1]
    return pltpu.roll(values, 1, 1), values, pltpu.roll(values, extent - 1, 1)


def homed(k, part, first=True, last=True):
    rows, extent = part.shape
    y, z = k // 3 % 3, k % 3
    lane = lax.broadcasted_iota(jnp.int32, part.shape, 1)
    if z == 0 and first:
        part = jnp.where(lane == 0, 0.0, part)
    if z == 2 and last:
        part = jnp.where(lane == extent - 1, 0.0, part)
    if y != 1:
        part = pltpu.roll(part, rows - 1 if y == 0 else 1, 0)
    return part


def neighbours(values, before=None, after=None):
    here = rolled(values)
    if before is None:
        return here, here, here
    row = lax.broadcasted_iota(jnp.int32, values.shape, 0)
    lower = [jnp.where(row == values.shape[0] - 1, b, h) for b, h in zip(rolled(before), here)]
    upper = [jnp.where(row == 0, a, h) for a, h in zip(rolled(after), here)]
    return lower, here, upper


def outer_terms(near, coefficient, lanes):
    sums = [None] * 3
    for x in range(3):
        for y in range(3):
            for z in range(3):
                k = 9 * x + 3 * y + z
                if k == CENTER or near[x] is None:
                    continue
                term = coefficient(k) * near[x][y][z][:, lanes]
                sums[y] = term if sums[y] is None else sums[y] + term
    rows = sums[1].shape[0]
    return sums[1] + (pltpu.roll(sums[0], 1, 0) + pltpu.roll(sums[2], rows - 1, 0))


def lane_tiles(extent):
    return [slice(l, l + LANES) for l in range(0, extent, LANES)]


def paired_lanes(values):
    rows, extent = values.shape
    row = lax.broadcasted_iota(jnp.int32, (extent, extent // 2), 0)
    column = lax.broadcasted_iota(jnp.int32, (extent, extent // 2), 1)
    pairs = jnp.where(lax.shift_right_logical(row, 1) == column, 1.0, 0.0).astype(jnp.bfloat16)
    parts = []
    for _ in range(3):
        part = values.astype(jnp.bfloat16).astype(jnp.float32)
        parts.append(part)
        values = values - part
    if 3 * rows % 16:
        parts.append(jnp.zeros_like(values))
    stacked = jnp.concatenate(parts, axis=0).astype(jnp.bfloat16)
    sums = lax.dot_general(stacked, pairs, (((1,), (0,)), ((), ())), preferred_element_type=jnp.float32)
    return sums[:rows] + (sums[rows : 2 * rows] + sums[2 * rows : 3 * rows])


def paired_rows(values):
    return values + pltpu.roll(values, values.shape[0] - 1, 0)


def put_edges(v, to_x, to_zx):
    last = v.shape[1] - 1
    for x in range(v.shape[0]):
        first_row, last_row = v[x, 0:1, :], v[x, last : last + 1, :]
        to_x[x : x + 1, :] = pick(even("sub"), last_row, first_row)
        to_zx[x : x + 1, :] = pick(even("sub"), first_row, last_row)


def edges_kernel(v, to_x, to_zx):
    put_edges(v, to_x, to_zx)


def faces_kernel(v, from_x, from_zx, to_core, to_y):
    planes, rows, _ = v.shape
    before, after = sides(from_x[...], from_zx[0:planes, :])
    for ref, swap in ((to_core, False), (to_y, True)):
        def choose(a, b):
            return pick(even("grp"), b, a) if swap else pick(even("grp"), a, b)

        ref[0:rows, :] = choose(v[planes - 1], v[0])
        ref[rows : rows + 1, :] = choose(before[planes - 1 :], before[0:1])
        ref[rows + 1 : rows + 2, :] = choose(after[planes - 1 :], after[0:1])


def fine_neighbours(groups, v, from_x, from_zx, from_core, from_y):
    planes, rows, _ = v.shape
    group = lax.axis_index("grp")
    before, after = sides(from_x[...], from_zx[0:planes, :])
    low = pick(even("grp"), from_y[...], from_core[...])
    high = pick(even("grp"), from_core[...], from_y[...])
    low = pick(group == 0, jnp.zeros_like(low), low)
    high = pick(group == groups - 1, jnp.zeros_like(high), high)
    faces = [neighbours(f[0:rows], f[rows : rows + 1], f[rows + 1 : rows + 2]) for f in (low, high)]
    inner = [neighbours(v[x], before[x : x + 1], after[x : x + 1]) for x in range(planes)]
    return [faces[0], *inner, faces[1]]


def sweep_kernel(groups, v, first, c, from_x, from_zx, from_core, from_y, out, to_x, to_zx):
    planes, rows, extent = v.shape
    near = fine_neighbours(groups, v, from_x, from_zx, from_core, from_y)
    for x in range(planes):
        for lanes in lane_tiles(extent):
            sums = outer_terms(near[x : x + 3], lambda k: c[k, x, :, lanes], lanes)
            out[x, :, lanes] = first[x, :, lanes] + (1.0 - WEIGHT) * v[x, :, lanes] - sums
    put_edges(out, to_x, to_zx)


def residual_kernel(
    groups, v, first, c, from_x, from_zx, from_core, from_y, center, iterate, to_x, to_zx, held
):
    planes, rows, extent = v.shape
    near = fine_neighbours(groups, v, from_x, from_zx, from_core, from_y)
    for x in range(0, planes, 2):
        for lanes in lane_tiles(extent):
            total = None
            for p in (x, x + 1):
                sums = outer_terms(near[p : p + 3], lambda k: c[k, p, :, lanes], lanes)
                part = first[p, :, lanes] - WEIGHT * v[p, :, lanes] - sums
                part = (1.0 / WEIGHT) * c[CENTER, p, :, lanes] * part
                total = part if total is None else total + part
            held[x // 2 * rows : (x // 2 + 1) * rows, lanes] = total
    total = (0.5 * WEIGHT) * paired_rows(paired_lanes(held[...]))
    half = rows // 2
    for x in range(planes // 2):
        for y in range(half):
            row = x * rows + 2 * y
            iterate[x, y : y + 1, :] = total[row : row + 1]
    iterate[...] = iterate[...] / center[...]
    for x in range(planes // 2):
        first_rows, last_rows = iterate[x, 0:3, :], iterate[x, half - 3 : half, :]
        to_x[4 * x : 4 * x + 3, :] = pick(even("sub"), last_rows, first_rows)
        to_zx[4 * x : 4 * x + 3, :] = pick(even("sub"), first_rows, last_rows)


def middle_faces_kernel(mine, from_x, from_zx, out):
    planes, half, _ = mine.shape
    before, after = sides(from_x[...], from_zx[0 : 4 * planes, :])
    for x in range(planes):
        row = x * ROWS
        out[row : row + 2, :] = before[4 * x + 1 : 4 * x + 3]
        out[row + 2 : row + 2 + half, :] = mine[x]
        out[row + 2 + half : row + ROWS, :] = after[4 * x : 4 * x + 2]
        extra = planes * ROWS + 2 * x
        out[extra : extra + 1, :] = before[4 * x : 4 * x + 1]
        out[extra + 1 : extra + 2, :] = after[4 * x + 2 : 4 * x + 3]


def coefficient_edges_kernel(c, to_x, to_zx):
    rows = c.shape[2]
    first, last = c[:, :, 0:2, :], c[:, :, rows - 2 : rows, :]
    to_x[...] = pick(even("sub"), last, first)
    to_zx[0:27] = pick(even("sub"), first, last)


def coefficient_scale_kernel(c, out):
    for x in range(c.shape[1]):
        out[:, x] = scaled(c[:, x])
        for k in range(27):
            out[k, x] = homed(k, out[k, x])


def scaled(c):
    center = c[CENTER : CENTER + 1]
    ratio = WEIGHT / jnp.where(center > 0.0, center, 1.0)
    index = lax.broadcasted_iota(jnp.int32, c.shape, 0)
    return c * jnp.where(index == CENTER, 1.0, ratio)


def coefficient_pack_kernel(known, *refs):
    coarse, (c, from_x, from_zx, _, __, middle_part, whole) = refs[:known], refs[known:]
    _, planes, rows, extent = c.shape
    tiles = extent // LANES
    before, after = sides(from_x[...], from_zx[0:27])
    for x in range(planes):
        for l, lanes in enumerate(lane_tiles(extent)):
            row = (x * tiles + l) * ROWS
            whole[:, row : row + 2, :] = before[:, x, :, lanes]
            whole[:, row + 2 : row + 2 + rows, :] = c[:, x, :, lanes]
            whole[:, row + 2 + rows : row + ROWS, :] = after[:, x, :, lanes]
    row = planes * tiles * ROWS
    for t in range(0, row, ROWS):
        part = scaled(whole[:, t : t + ROWS, :])
        l = t // ROWS % tiles
        for k in range(27):
            ready = homed(k, part[k], l == 0, l == tiles - 1)
            whole[k, t : t + ROWS, :] = ready
            middle_part[k, t : t + ROWS, :] = ready
    for ref in coarse:
        for x in range(ref.shape[1]):
            for t in range(0, ref.shape[2], ROWS):
                whole[:, row : row + ROWS, :] = scaled(ref[:, x, t : t + ROWS, :])
                row += ROWS


def middle_kernel(
    groups, planes, packed, near_core, near_y, far_below, far_above, own, core, other, iterate, coarse, held
):
    extent = packed.shape[-1]
    tiles = extent // LANES
    half = ROWS - 4
    group = lax.axis_index("grp")
    window = 3 * planes

    below = pick(even("grp"), near_y[...], near_core[...])
    above = pick(even("grp"), near_core[...], near_y[...])
    blocks = {-2: far_below[...], -1: below, 0: packed[...], 1: above, 2: far_above[...]}
    for away in (-2, -1, 1, 2):
        inside = (group + away >= 0) & (group + away < groups)
        blocks[away] = pick(inside, blocks[away], jnp.zeros_like(blocks[away]))
    first, near = [], []
    for p in range(-1, window + 1):
        block, x = blocks[p // planes - 1], p % planes
        v, extra = block[x * ROWS : (x + 1) * ROWS], planes * ROWS + 2 * x
        first.append(v)
        near.append(neighbours(v, block[extra : extra + 1], block[extra + 1 : extra + 2]))

    def work(parts):
        def terms(forms, w, lanes):
            row = (w % planes * tiles + lanes.start // LANES) * ROWS
            return outer_terms(forms, lambda k: parts[w // planes][k, row : row + ROWS, :], lanes)

        def swept(forms, field, w):
            sums = jnp.concatenate([terms(forms, w, lanes) for lanes in lane_tiles(extent)], axis=1)
            return first[w + 1] + (1.0 - WEIGHT) * field - sums

        low, high = planes - 2, 2 * planes + 2
        once = {w: swept(near[w : w + 3], first[w + 1], w) for w in range(low, high)}
        forms = {w: neighbours(v) for w, v in once.items()}
        low, high = low + 1, high - 1
        twice = {w: swept([forms[w + x] for x in (-1, 0, 1)], once[w], w) for w in range(low, high)}
        forms = {w: neighbours(v) for w, v in twice.items()}
        for x in range(planes):
            w = planes + x
            iterate[x] = twice[w][2 : 2 + half]
            for lanes in lane_tiles(extent):
                row = (x * tiles + lanes.start // LANES) * ROWS
                sums = terms([forms[w + i] for i in (-1, 0, 1)], w, lanes)
                rest = first[w + 1][:, lanes] - WEIGHT * twice[w][:, lanes] - sums
                held[x, :, lanes] = (1.0 / WEIGHT) * own[CENTER, row : row + ROWS, :] * rest

    @pl.when(even("grp"))
    def _():
        work((other, own, core))

    @pl.when(jnp.logical_not(even("grp")))
    def _():
        work((core, own, other))

    place_of = lax.broadcasted_iota(jnp.int32, (ROWS, extent // 2), 0)
    for x in range(planes // 2):
        total = 0.5 * paired_rows(paired_lanes(held[2 * x] + held[2 * x + 1]))
        value = pltpu.roll(total, ROWS - 2, 0)
        for i in range(1, half // 2):
            value = jnp.where(place_of == i, pltpu.roll(total, ROWS - 2 - i, 0), value)
        for device in range(coarse.shape[0]):
            coarse[device, x] = value[: half // 2]


def coarse_order_kernel(planes, rows, start, offsets, own, core, out):
    group = lax.axis_index("grp")
    row_of = lax.broadcasted_iota(jnp.int32, (rows, out.shape[-1]), 0)
    for ref, flip in ((own, 0), (core, 1)):
        for i, offset in enumerate(offsets):
            owner = jnp.bitwise_xor(group, offset ^ flip)
            for x in range(planes):
                row = start + (i * planes + x) * rows
                for k in range(27):
                    part = ref[k, row : row + rows, :]
                    if k // 3 % 3 != 1:
                        outside = 0 if k // 3 % 3 == 0 else rows - 1
                        part = jnp.where(row_of == outside, 0.0, part)
                    out[owner * planes + x, k] = homed(k, part)


def coarse_kernel(groups, planes, gathered, c, fine, middle, out, fine_out, middle_out, first, sems):
    kept = [
        pltpu.make_async_copy(fine, fine_out, sems.at[0]),
        pltpu.make_async_copy(middle, middle_out, sems.at[1]),
    ]
    for copy in kept:
        copy.start()
    total, rows, extent = first.shape
    subs = gathered.shape[0] // groups
    each = rows // subs
    for g in range(groups):
        for s in range(subs):
            for x in range(planes):
                first[g * planes + x, s * each : (s + 1) * each, :] = gathered[g * subs + s, x]
    for p in range(total):
        first[p] = WEIGHT * first[p] / c[p, CENTER]

    def sweep(_, field):
        near = [None, *map(neighbours, field), None]
        every = slice(0, extent)
        fresh = []
        for p in range(total):
            sums = outer_terms(near[p : p + 3], lambda k: c[p, k], every)
            fresh.append(first[p] + (1.0 - WEIGHT) * field[p] - sums)
        return tuple(fresh)

    field = lax.fori_loop(0, NB - 1, sweep, tuple(first[p] for p in range(total)))
    for p in range(total):
        first[p] = field[p]
    for x in range(planes):
        out[x] = first[lax.axis_index("grp") * planes + x]
    for copy in kept:
        copy.wait()


def after(value, *others):
    return lax.optimization_barrier((value, *others))[0]


def after_all(values, *others):
    return lax.optimization_barrier((*values, *others))[: len(values)]


def swaps(pairs):
    return [p for a, b in pairs for p in ((a, b), (b, a))]


def body(source, fine, middle, coarse):
    groups, subs = lax.axis_size("grp"), lax.axis_size("sub")
    _, planes, rows, extent = fine.shape
    _, middle_planes, middle_rows, middle_extent = middle.shape
    _, coarse_planes, coarse_rows, coarse_extent = coarse.shape

    x_pairs = swaps([(i, i + 1) for i in range(0, subs, 2)])
    zx_pairs = swaps(
        [(g * subs + i, g * subs + i + 1) for g in range(groups) for i in range(1, subs - 1, 2)]
        + [(g * subs + i, (g + 1) * subs + i) for g in range(0, groups, 2) for i in (0, subs - 1)]
    )
    core_pairs = swaps([(i, i + 1) for i in range(0, groups, 2)])
    y_pairs = swaps([(i, i + 1) for i in range(1, groups - 1, 2)])
    y_ring = y_pairs + [(groups - 1, 0), (0, groups - 1)]

    def along_sub(pair):
        to_x, to_zx = pair
        from_x = lax.ppermute(to_x, "sub", x_pairs)
        return from_x, lax.ppermute(to_zx, ("grp", "sub"), zx_pairs)

    def along_grp(v, halo):
        to_core, to_y = call(faces_kernel, [shape(rows + 8, extent)] * 2, [v, *halo])
        from_core = lax.ppermute(to_core, "grp", core_pairs)
        from_y = lax.ppermute(to_y, "grp", y_ring)
        return (*halo, from_core, from_y)

    weights = call(coefficient_scale_kernel, shape(*fine.shape), [fine])
    v = WEIGHT * source / fine[CENTER]
    first = v
    to_x, to_zx = call(edges_kernel, [shape(planes, extent), shape(4 * planes, extent)], [v])

    def sweep(v, halo):
        v, *edges = call(
            functools.partial(sweep_kernel, groups),
            [shape(planes, rows, extent), shape(planes, extent), shape(4 * planes, extent)],
            [v, first, weights, *halo],
        )
        return v, along_sub(edges)

    edges_c = call(
        coefficient_edges_kernel,
        [shape(27, middle_planes, 2, middle_extent), shape(28, middle_planes, 2, middle_extent)],
        [middle],
    )
    halo = along_sub((to_x, to_zx))
    halo_c = along_sub(after_all(edges_c, *halo))
    halo = along_grp(after(v, weights, *edges_c), halo)
    known = {0: after(coarse, *halo[2:])}
    bit = groups // 2
    while bit > 1:
        for offset in sorted(known):
            known[offset ^ bit] = lax.ppermute(known[offset], "grp", [(i, i ^ bit) for i in range(groups)])
        bit //= 2
    offsets = sorted(known)
    v, halo = sweep(v, halo)
    halo = along_grp(v, halo)
    start = middle_planes * (middle_extent // LANES) * ROWS
    middle_part, own = call(
        functools.partial(coefficient_pack_kernel, len(known)),
        [shape(27, start, LANES), shape(27, start + len(known) * coarse_planes * coarse_rows, LANES)],
        [*(known[o] for o in offsets), middle, *halo_c, *halo[2:]],
    )
    core = lax.ppermute(own, "grp", core_pairs)
    other = lax.ppermute(middle_part, "grp", y_pairs)
    v, halo = sweep(v, halo)
    fine_iterate = v
    halo = along_grp(v, halo)
    iterate, *edges = call(
        functools.partial(residual_kernel, groups),
        [shape(middle_planes, middle_rows, middle_extent)]
        + [shape(4 * middle_planes, middle_extent), shape(8 * middle_planes, middle_extent)],
        [v, first, weights, *halo, middle[CENTER]],
        [pltpu.VMEM((planes // 2 * rows, extent), jnp.float32)],
    )
    total = groups * coarse_planes
    ordered = call(
        functools.partial(coarse_order_kernel, coarse_planes, coarse_rows, start, offsets),
        shape(total, 27, coarse_rows, coarse_extent),
        [own, core],
    )
    packed = call(
        middle_faces_kernel,
        shape(middle_planes * ROWS + 8, middle_extent),
        [after(iterate, ordered), *along_sub(edges)],
    )
    near_core = lax.ppermute(packed, "grp", core_pairs)
    if groups == 4:
        far_below = far_above = lax.ppermute(packed, "grp", swaps([(0, 2), (1, 3)]))
        near_y = lax.ppermute(packed, "grp", y_ring)
    else:
        near_y = lax.ppermute(packed, "grp", y_pairs)
        up = [(i, i + 2) for i in range(groups - 2)]
        far_below = lax.ppermute(packed, "grp", up)
        far_above = lax.ppermute(packed, "grp", [(j, i) for i, j in up])
    middle_iterate, coarse_source = call(
        functools.partial(middle_kernel, groups, middle_planes),
        [
            shape(middle_planes, middle_rows, middle_extent),
            shape(groups * subs, coarse_planes, coarse_rows // subs, coarse_extent),
        ],
        [packed, near_core, near_y, far_below, far_above, own, core, other],
        [pltpu.VMEM((middle_planes, ROWS, middle_extent), jnp.float32)],
    )
    gathered = lax.all_to_all(coarse_source, ("grp", "sub"), 0, 0, tiled=True)
    vmem, hbm = pl.BlockSpec(memory_space=pltpu.VMEM), pl.BlockSpec(memory_space=pl.ANY)
    coarse_iterate, fine_iterate, middle_iterate = call(
        functools.partial(coarse_kernel, groups, coarse_planes),
        [
            shape(coarse_planes, coarse_rows, coarse_extent),
            shape(*fine_iterate.shape),
            shape(*middle_iterate.shape),
        ],
        [gathered, ordered, fine_iterate, middle_iterate],
        [
            pltpu.VMEM((total, coarse_rows, coarse_extent), jnp.float32),
            pltpu.SemaphoreType.DMA((2,)),
        ],
        out_specs=[vmem, hbm, hbm],
    )
    return fine_iterate, middle_iterate, coarse_iterate


def solution(mesh):
    placed = (
        P("grp", "sub", None),
        P(None, "grp", "sub", None),
        P(None, "grp", "sub", None),
        P(None, "grp", None, None),
    )
    return jax.shard_map(
        body,
        mesh=mesh,
        in_specs=placed,
        out_specs=(P("grp", "sub", None), P("grp", "sub", None), P("grp", None, None)),
        check_vma=False,
    )
```

```python
import functools

import jax
import jax.numpy as jnp
from jax import lax
from jax.experimental import pallas as pl
from jax.experimental.pallas import tpu as pltpu
from jax.sharding import PartitionSpec as P

NU0 = 3
NB = 16
WEIGHT = 0.8
CENTER = 13
LANES = 128
ROWS = 8


def shape(*dims):
    return jax.ShapeDtypeStruct(dims, jnp.float32)


def call(kernel, outs, args, scratch=(), out_specs=None):
    vmem = pl.BlockSpec(memory_space=pltpu.VMEM)
    return pl.pallas_call(
        kernel,
        out_shape=outs,
        in_specs=[vmem] * len(args),
        out_specs=out_specs or jax.tree.map(lambda _: vmem, outs),
        scratch_shapes=list(scratch),
        compiler_params=pltpu.CompilerParams(vmem_limit_bytes=12 << 20),
    )(*args)


def even(axis):
    return lax.rem(lax.axis_index(axis), 2) == 0


def pick(condition, a, b):
    return jnp.where(jnp.broadcast_to(condition, a.shape), a, b)


def sides(from_x, from_zx):
    sub, subs = lax.axis_index("sub"), lax.axis_size("sub")
    from_zx = pick((sub == 0) | (sub == subs - 1), jnp.zeros_like(from_zx), from_zx)
    return pick(even("sub"), from_zx, from_x), pick(even("sub"), from_x, from_zx)


def rolled(values):
    extent = values.shape[-1]
    return pltpu.roll(values, 1, 1), values, pltpu.roll(values, extent - 1, 1)


def homed(k, part, first=True, last=True):
    rows, extent = part.shape
    y, z = k // 3 % 3, k % 3
    lane = lax.broadcasted_iota(jnp.int32, part.shape, 1)
    if z == 0 and first:
        part = jnp.where(lane == 0, 0.0, part)
    if z == 2 and last:
        part = jnp.where(lane == extent - 1, 0.0, part)
    if y != 1:
        part = pltpu.roll(part, rows - 1 if y == 0 else 1, 0)
    return part


def neighbours(values, before=None, after=None):
    here = rolled(values)
    if before is None:
        return here, here, here
    row = lax.broadcasted_iota(jnp.int32, values.shape, 0)
    lower = [jnp.where(row == values.shape[0] - 1, b, h) for b, h in zip(rolled(before), here)]
    upper = [jnp.where(row == 0, a, h) for a, h in zip(rolled(after), here)]
    return lower, here, upper


def outer_terms(near, coefficient, lanes):
    sums = [None] * 3
    for x in range(3):
        for y in range(3):
            for z in range(3):
                k = 9 * x + 3 * y + z
                if k == CENTER or near[x] is None:
                    continue
                term = coefficient(k) * near[x][y][z][:, lanes]
                sums[y] = term if sums[y] is None else sums[y] + term
    rows = sums[1].shape[0]
    return sums[1] + (pltpu.roll(sums[0], 1, 0) + pltpu.roll(sums[2], rows - 1, 0))


def lane_tiles(extent):
    return [slice(l, l + LANES) for l in range(0, extent, LANES)]


def paired_lanes(values):
    rows, extent = values.shape
    row = lax.broadcasted_iota(jnp.int32, (extent, extent // 2), 0)
    column = lax.broadcasted_iota(jnp.int32, (extent, extent // 2), 1)
    pairs = jnp.where(lax.shift_right_logical(row, 1) == column, 1.0, 0.0).astype(jnp.bfloat16)
    parts = []
    for _ in range(3):
        part = values.astype(jnp.bfloat16).astype(jnp.float32)
        parts.append(part)
        values = values - part
    if 3 * rows % 16:
        parts.append(jnp.zeros_like(values))
    stacked = jnp.concatenate(parts, axis=0).astype(jnp.bfloat16)
    sums = lax.dot_general(stacked, pairs, (((1,), (0,)), ((), ())), preferred_element_type=jnp.float32)
    return sums[:rows] + (sums[rows : 2 * rows] + sums[2 * rows : 3 * rows])


def paired_rows(values):
    return values + pltpu.roll(values, values.shape[0] - 1, 0)


def put_edges(v, to_x, to_zx):
    last = v.shape[1] - 1
    for x in range(v.shape[0]):
        first_row, last_row = v[x, 0:1, :], v[x, last : last + 1, :]
        to_x[x : x + 1, :] = pick(even("sub"), last_row, first_row)
        to_zx[x : x + 1, :] = pick(even("sub"), first_row, last_row)


def edges_kernel(v, to_x, to_zx):
    put_edges(v, to_x, to_zx)


def faces_kernel(v, from_x, from_zx, to_core, to_y):
    planes, rows, _ = v.shape
    before, after = sides(from_x[...], from_zx[0:planes, :])
    for ref, swap in ((to_core, False), (to_y, True)):
        def choose(a, b):
            return pick(even("grp"), b, a) if swap else pick(even("grp"), a, b)

        ref[0:rows, :] = choose(v[planes - 1], v[0])
        ref[rows : rows + 1, :] = choose(before[planes - 1 :], before[0:1])
        ref[rows + 1 : rows + 2, :] = choose(after[planes - 1 :], after[0:1])


def fine_neighbours(groups, v, from_x, from_zx, from_core, from_y):
    planes, rows, _ = v.shape
    group = lax.axis_index("grp")
    before, after = sides(from_x[...], from_zx[0:planes, :])
    low = pick(even("grp"), from_y[...], from_core[...])
    high = pick(even("grp"), from_core[...], from_y[...])
    low = pick(group == 0, jnp.zeros_like(low), low)
    high = pick(group == groups - 1, jnp.zeros_like(high), high)
    faces = [neighbours(f[0:rows], f[rows : rows + 1], f[rows + 1 : rows + 2]) for f in (low, high)]
    inner = [neighbours(v[x], before[x : x + 1], after[x : x + 1]) for x in range(planes)]
    return [faces[0], *inner, faces[1]]


def sweep_kernel(groups, v, first, c, from_x, from_zx, from_core, from_y, out, to_x, to_zx):
    planes, rows, extent = v.shape
    near = fine_neighbours(groups, v, from_x, from_zx, from_core, from_y)
    for x in range(planes):
        for lanes in lane_tiles(extent):
            sums = outer_terms(near[x : x + 3], lambda k: c[k, x, :, lanes], lanes)
            out[x, :, lanes] = first[x, :, lanes] + (1.0 - WEIGHT) * v[x, :, lanes] - sums
    put_edges(out, to_x, to_zx)


def residual_kernel(
    groups, v, first, c, from_x, from_zx, from_core, from_y, center, iterate, to_x, to_zx, held
):
    planes, rows, extent = v.shape
    near = fine_neighbours(groups, v, from_x, from_zx, from_core, from_y)
    for x in range(0, planes, 2):
        for lanes in lane_tiles(extent):
            total = None
            for p in (x, x + 1):
                sums = outer_terms(near[p : p + 3], lambda k: c[k, p, :, lanes], lanes)
                part = first[p, :, lanes] - WEIGHT * v[p, :, lanes] - sums
                part = (1.0 / WEIGHT) * c[CENTER, p, :, lanes] * part
                total = part if total is None else total + part
            held[x // 2 * rows : (x // 2 + 1) * rows, lanes] = total
    total = (0.5 * WEIGHT) * paired_rows(paired_lanes(held[...]))
    half = rows // 2
    for x in range(planes // 2):
        for y in range(half):
            row = x * rows + 2 * y
            iterate[x, y : y + 1, :] = total[row : row + 1]
    iterate[...] = iterate[...] / center[...]
    for x in range(planes // 2):
        first_rows, last_rows = iterate[x, 0:3, :], iterate[x, half - 3 : half, :]
        to_x[4 * x : 4 * x + 3, :] = pick(even("sub"), last_rows, first_rows)
        to_zx[4 * x : 4 * x + 3, :] = pick(even("sub"), first_rows, last_rows)


def middle_faces_kernel(mine, from_x, from_zx, out):
    planes, half, _ = mine.shape
    before, after = sides(from_x[...], from_zx[0 : 4 * planes, :])
    for x in range(planes):
        row = x * ROWS
        out[row : row + 2, :] = before[4 * x + 1 : 4 * x + 3]
        out[row + 2 : row + 2 + half, :] = mine[x]
        out[row + 2 + half : row + ROWS, :] = after[4 * x : 4 * x + 2]
        extra = planes * ROWS + 2 * x
        out[extra : extra + 1, :] = before[4 * x : 4 * x + 1]
        out[extra + 1 : extra + 2, :] = after[4 * x + 2 : 4 * x + 3]


def coefficient_edges_kernel(c, to_x, to_zx):
    rows = c.shape[2]
    first, last = c[:, :, 0:2, :], c[:, :, rows - 2 : rows, :]
    to_x[...] = pick(even("sub"), last, first)
    to_zx[...] = pick(even("sub"), first, last)


def coefficient_scale_kernel(c, out):
    for x in range(c.shape[1]):
        out[:, x] = scaled(c[:, x])
        for k in range(27):
            out[k, x] = homed(k, out[k, x])


def scaled(c):
    center = c[CENTER : CENTER + 1]
    ratio = WEIGHT / jnp.where(center > 0.0, center, 1.0)
    index = lax.broadcasted_iota(jnp.int32, c.shape, 0)
    return c * jnp.where(index == CENTER, 1.0, ratio)


def coefficient_pack_kernel(known, *refs):
    coarse, (c, from_x, from_zx, _, __, middle_part, whole) = refs[:known], refs[known:]
    _, planes, rows, extent = c.shape
    tiles = extent // LANES
    before, after = sides(from_x[...], from_zx[...])
    for x in range(planes):
        for l, lanes in enumerate(lane_tiles(extent)):
            row = (x * tiles + l) * ROWS
            whole[:, row : row + 2, :] = before[:, x, :, lanes]
            whole[:, row + 2 : row + 2 + rows, :] = c[:, x, :, lanes]
            whole[:, row + 2 + rows : row + ROWS, :] = after[:, x, :, lanes]
    row = planes * tiles * ROWS
    for t in range(0, row, ROWS):
        part = scaled(whole[:, t : t + ROWS, :])
        l = t // ROWS % tiles
        for k in range(27):
            ready = homed(k, part[k], l == 0, l == tiles - 1)
            whole[k, t : t + ROWS, :] = ready
            middle_part[k, t : t + ROWS, :] = ready
    for ref in coarse:
        for x in range(ref.shape[1]):
            for t in range(0, ref.shape[2], ROWS):
                whole[:, row : row + ROWS, :] = scaled(ref[:, x, t : t + ROWS, :])
                row += ROWS


def middle_kernel(
    groups, planes, packed, near_core, near_y, far_below, far_above, own, core, other, iterate, coarse, held
):
    extent = packed.shape[-1]
    tiles = extent // LANES
    half = ROWS - 4
    group = lax.axis_index("grp")
    window = 3 * planes

    below = pick(even("grp"), near_y[...], near_core[...])
    above = pick(even("grp"), near_core[...], near_y[...])
    blocks = {-2: far_below[...], -1: below, 0: packed[...], 1: above, 2: far_above[...]}
    for away in (-2, -1, 1, 2):
        inside = (group + away >= 0) & (group + away < groups)
        blocks[away] = pick(inside, blocks[away], jnp.zeros_like(blocks[away]))
    first, near = [], []
    for p in range(-1, window + 1):
        block, x = blocks[p // planes - 1], p % planes
        v, extra = block[x * ROWS : (x + 1) * ROWS], planes * ROWS + 2 * x
        first.append(v)
        near.append(neighbours(v, block[extra : extra + 1], block[extra + 1 : extra + 2]))

    def work(parts):
        def terms(forms, w, lanes):
            row = (w % planes * tiles + lanes.start // LANES) * ROWS
            return outer_terms(forms, lambda k: parts[w // planes][k, row : row + ROWS, :], lanes)

        def swept(forms, field, w):
            sums = jnp.concatenate([terms(forms, w, lanes) for lanes in lane_tiles(extent)], axis=1)
            return first[w + 1] + (1.0 - WEIGHT) * field - sums

        low, high = planes - 2, 2 * planes + 2
        once = {w: swept(near[w : w + 3], first[w + 1], w) for w in range(low, high)}
        forms = {w: neighbours(v) for w, v in once.items()}
        low, high = low + 1, high - 1
        twice = {w: swept([forms[w + x] for x in (-1, 0, 1)], once[w], w) for w in range(low, high)}
        forms = {w: neighbours(v) for w, v in twice.items()}
        for x in range(planes):
            w = planes + x
            iterate[x] = twice[w][2 : 2 + half]
            for lanes in lane_tiles(extent):
                row = (x * tiles + lanes.start // LANES) * ROWS
                sums = terms([forms[w + i] for i in (-1, 0, 1)], w, lanes)
                rest = first[w + 1][:, lanes] - WEIGHT * twice[w][:, lanes] - sums
                held[x, :, lanes] = (1.0 / WEIGHT) * own[CENTER, row : row + ROWS, :] * rest

    @pl.when(even("grp"))
    def _():
        work((other, own, core))

    @pl.when(jnp.logical_not(even("grp")))
    def _():
        work((core, own, other))

    place_of = lax.broadcasted_iota(jnp.int32, (ROWS, extent // 2), 0)
    for x in range(planes // 2):
        total = 0.5 * paired_rows(paired_lanes(held[2 * x] + held[2 * x + 1]))
        value = pltpu.roll(total, ROWS - 2, 0)
        for i in range(1, half // 2):
            value = jnp.where(place_of == i, pltpu.roll(total, ROWS - 2 - i, 0), value)
        for device in range(coarse.shape[0]):
            coarse[device, x] = value[: half // 2]


def coarse_order_kernel(planes, rows, start, offsets, own, core, out):
    group = lax.axis_index("grp")
    row_of = lax.broadcasted_iota(jnp.int32, (rows, out.shape[-1]), 0)
    for ref, flip in ((own, 0), (core, 1)):
        for i, offset in enumerate(offsets):
            owner = jnp.bitwise_xor(group, offset ^ flip)
            for x in range(planes):
                row = start + (i * planes + x) * rows
                for k in range(27):
                    part = ref[k, row : row + rows, :]
                    if k // 3 % 3 != 1:
                        outside = 0 if k // 3 % 3 == 0 else rows - 1
                        part = jnp.where(row_of == outside, 0.0, part)
                    out[owner * planes + x, k] = homed(k, part)


def coarse_kernel(groups, planes, gathered, c, fine, middle, out, fine_out, middle_out, first, sems):
    kept = [
        pltpu.make_async_copy(fine, fine_out, sems.at[0]),
        pltpu.make_async_copy(middle, middle_out, sems.at[1]),
    ]
    for copy in kept:
        copy.start()
    total, rows, extent = first.shape
    subs = gathered.shape[0] // groups
    each = rows // subs
    for g in range(groups):
        for s in range(subs):
            for x in range(planes):
                first[g * planes + x, s * each : (s + 1) * each, :] = gathered[g * subs + s, x]
    for p in range(total):
        first[p] = WEIGHT * first[p] / c[p, CENTER]

    def sweep(_, field):
        near = [None, *map(neighbours, field), None]
        every = slice(0, extent)
        fresh = []
        for p in range(total):
            sums = outer_terms(near[p : p + 3], lambda k: c[p, k], every)
            fresh.append(first[p] + (1.0 - WEIGHT) * field[p] - sums)
        return tuple(fresh)

    field = lax.fori_loop(0, NB - 1, sweep, tuple(first[p] for p in range(total)))
    for p in range(total):
        first[p] = field[p]
    for x in range(planes):
        out[x] = first[lax.axis_index("grp") * planes + x]
    for copy in kept:
        copy.wait()


def after(value, *others):
    return lax.optimization_barrier((value, *others))[0]


def after_all(values, *others):
    return lax.optimization_barrier((*values, *others))[: len(values)]


def swaps(pairs):
    return [p for a, b in pairs for p in ((a, b), (b, a))]


def body(source, fine, middle, coarse):
    groups, subs = lax.axis_size("grp"), lax.axis_size("sub")
    _, planes, rows, extent = fine.shape
    _, middle_planes, middle_rows, middle_extent = middle.shape
    _, coarse_planes, coarse_rows, coarse_extent = coarse.shape

    x_pairs = swaps([(i, i + 1) for i in range(0, subs, 2)])
    zx_pairs = swaps(
        [(g * subs + i, g * subs + i + 1) for g in range(groups) for i in range(1, subs - 1, 2)]
        + [(g * subs + i, (g + 1) * subs + i) for g in range(0, groups, 2) for i in (0, subs - 1)]
    )
    core_pairs = swaps([(i, i + 1) for i in range(0, groups, 2)])
    y_pairs = swaps([(i, i + 1) for i in range(1, groups - 1, 2)])
    y_ring = y_pairs + [(groups - 1, 0), (0, groups - 1)]

    def along_sub(pair):
        to_x, to_zx = pair
        from_x = lax.ppermute(to_x, "sub", x_pairs)
        return from_x, lax.ppermute(to_zx, ("grp", "sub"), zx_pairs)

    def along_grp(v, halo):
        to_core, to_y = call(faces_kernel, [shape(rows + 8, extent)] * 2, [v, *halo])
        from_core = lax.ppermute(to_core, "grp", core_pairs)
        from_y = lax.ppermute(to_y, "grp", y_ring)
        return (*halo, from_core, from_y)

    weights = call(coefficient_scale_kernel, shape(*fine.shape), [fine])
    v = WEIGHT * source / fine[CENTER]
    first = v
    to_x, to_zx = call(edges_kernel, [shape(planes, extent), shape(4 * planes, extent)], [v])

    def sweep(v, halo):
        v, *edges = call(
            functools.partial(sweep_kernel, groups),
            [shape(planes, rows, extent), shape(planes, extent), shape(4 * planes, extent)],
            [v, first, weights, *halo],
        )
        return v, along_sub(edges)

    edges_c = call(
        coefficient_edges_kernel,
        [shape(27, middle_planes, 2, middle_extent)] * 2,
        [middle],
    )
    halo = along_sub((to_x, to_zx))
    halo_c = along_sub(after_all(edges_c, *halo))
    halo = along_grp(after(v, weights, *edges_c), halo)
    known = {0: after(coarse, *halo[2:])}
    bit = groups // 2
    while bit > 1:
        for offset in sorted(known):
            known[offset ^ bit] = lax.ppermute(known[offset], "grp", [(i, i ^ bit) for i in range(groups)])
        bit //= 2
    offsets = sorted(known)
    v, halo = sweep(v, halo)
    halo = along_grp(v, halo)
    start = middle_planes * (middle_extent // LANES) * ROWS
    middle_part, own = call(
        functools.partial(coefficient_pack_kernel, len(known)),
        [shape(27, start, LANES), shape(27, start + len(known) * coarse_planes * coarse_rows, LANES)],
        [*(known[o] for o in offsets), middle, *halo_c, *halo[2:]],
    )
    core = lax.ppermute(own, "grp", core_pairs)
    other = lax.ppermute(middle_part, "grp", y_pairs)
    v, halo = sweep(v, halo)
    fine_iterate = v
    halo = along_grp(v, halo)
    iterate, *edges = call(
        functools.partial(residual_kernel, groups),
        [shape(middle_planes, middle_rows, middle_extent)]
        + [shape(4 * middle_planes, middle_extent), shape(8 * middle_planes, middle_extent)],
        [v, first, weights, *halo, middle[CENTER]],
        [pltpu.VMEM((planes // 2 * rows, extent), jnp.float32)],
    )
    total = groups * coarse_planes
    ordered = call(
        functools.partial(coarse_order_kernel, coarse_planes, coarse_rows, start, offsets),
        shape(total, 27, coarse_rows, coarse_extent),
        [own, core],
    )
    packed = call(
        middle_faces_kernel,
        shape(middle_planes * ROWS + 8, middle_extent),
        [after(iterate, ordered), *along_sub(edges)],
    )
    near_core = lax.ppermute(packed, "grp", core_pairs)
    if groups == 4:
        far_below = far_above = lax.ppermute(packed, "grp", swaps([(0, 2), (1, 3)]))
        near_y = lax.ppermute(packed, "grp", y_ring)
    else:
        near_y = lax.ppermute(packed, "grp", y_pairs)
        up = [(i, i + 2) for i in range(groups - 2)]
        far_below = lax.ppermute(packed, "grp", up)
        far_above = lax.ppermute(packed, "grp", [(j, i) for i, j in up])
    middle_iterate, coarse_source = call(
        functools.partial(middle_kernel, groups, middle_planes),
        [
            shape(middle_planes, middle_rows, middle_extent),
            shape(groups * subs, coarse_planes, coarse_rows // subs, coarse_extent),
        ],
        [packed, near_core, near_y, far_below, far_above, own, core, other],
        [pltpu.VMEM((middle_planes, ROWS, middle_extent), jnp.float32)],
    )
    gathered = lax.all_to_all(coarse_source, ("grp", "sub"), 0, 0, tiled=True)
    vmem, hbm = pl.BlockSpec(memory_space=pltpu.VMEM), pl.BlockSpec(memory_space=pl.ANY)
    coarse_iterate, fine_iterate, middle_iterate = call(
        functools.partial(coarse_kernel, groups, coarse_planes),
        [
            shape(coarse_planes, coarse_rows, coarse_extent),
            shape(*fine_iterate.shape),
            shape(*middle_iterate.shape),
        ],
        [gathered, ordered, fine_iterate, middle_iterate],
        [
            pltpu.VMEM((total, coarse_rows, coarse_extent), jnp.float32),
            pltpu.SemaphoreType.DMA((2,)),
        ],
        out_specs=[vmem, hbm, hbm],
    )
    return fine_iterate, middle_iterate, coarse_iterate


def solution(mesh):
    placed = (
        P("grp", "sub", None),
        P(None, "grp", "sub", None),
        P(None, "grp", "sub", None),
        P(None, "grp", None, None),
    )
    return jax.shard_map(
        body,
        mesh=mesh,
        in_specs=placed,
        out_specs=(P("grp", "sub", None), P("grp", "sub", None), P("grp", None, None)),
        check_vma=False,
    )
```

```python
import functools

import jax
import jax.numpy as jnp
from jax import lax
from jax.experimental import pallas as pl
from jax.experimental.pallas import tpu as pltpu
from jax.sharding import PartitionSpec as P

NU0 = 3
NB = 16
WEIGHT = 0.8
CENTER = 13
LANES = 128
ROWS = 8


def shape(*dims):
    return jax.ShapeDtypeStruct(dims, jnp.float32)


def call(kernel, outs, args, scratch=(), out_specs=None):
    vmem = pl.BlockSpec(memory_space=pltpu.VMEM)
    return pl.pallas_call(
        kernel,
        out_shape=outs,
        in_specs=[vmem] * len(args),
        out_specs=out_specs or jax.tree.map(lambda _: vmem, outs),
        scratch_shapes=list(scratch),
        compiler_params=pltpu.CompilerParams(vmem_limit_bytes=12 << 20),
    )(*args)


def even(axis):
    return lax.rem(lax.axis_index(axis), 2) == 0


def pick(condition, a, b):
    return jnp.where(jnp.broadcast_to(condition, a.shape), a, b)


def sides(from_x, from_zx):
    sub, subs = lax.axis_index("sub"), lax.axis_size("sub")
    from_zx = pick((sub == 0) | (sub == subs - 1), jnp.zeros_like(from_zx), from_zx)
    return pick(even("sub"), from_zx, from_x), pick(even("sub"), from_x, from_zx)


def rolled(values):
    extent = values.shape[-1]
    return pltpu.roll(values, 1, 1), values, pltpu.roll(values, extent - 1, 1)


def homed(k, part, first=True, last=True):
    rows, extent = part.shape
    y, z = k // 3 % 3, k % 3
    lane = lax.broadcasted_iota(jnp.int32, part.shape, 1)
    if z == 0 and first:
        part = jnp.where(lane == 0, 0.0, part)
    if z == 2 and last:
        part = jnp.where(lane == extent - 1, 0.0, part)
    if y != 1:
        part = pltpu.roll(part, rows - 1 if y == 0 else 1, 0)
    return part


def neighbours(values, before=None, after=None):
    here = rolled(values)
    if before is None:
        return here, here, here
    row = lax.broadcasted_iota(jnp.int32, values.shape, 0)
    lower = [jnp.where(row == values.shape[0] - 1, b, h) for b, h in zip(rolled(before), here)]
    upper = [jnp.where(row == 0, a, h) for a, h in zip(rolled(after), here)]
    return lower, here, upper


def outer_terms(near, coefficient, lanes):
    sums = [None] * 3
    for x in range(3):
        for y in range(3):
            for z in range(3):
                k = 9 * x + 3 * y + z
                if k == CENTER or near[x] is None:
                    continue
                term = coefficient(k) * near[x][y][z][:, lanes]
                sums[y] = term if sums[y] is None else sums[y] + term
    rows = sums[1].shape[0]
    return sums[1] + (pltpu.roll(sums[0], 1, 0) + pltpu.roll(sums[2], rows - 1, 0))


def lane_tiles(extent):
    return [slice(l, l + LANES) for l in range(0, extent, LANES)]


def paired_lanes(values):
    rows, extent = values.shape
    row = lax.broadcasted_iota(jnp.int32, (extent, extent // 2), 0)
    column = lax.broadcasted_iota(jnp.int32, (extent, extent // 2), 1)
    pairs = jnp.where(lax.shift_right_logical(row, 1) == column, 1.0, 0.0).astype(jnp.bfloat16)
    parts = []
    for _ in range(3):
        part = values.astype(jnp.bfloat16).astype(jnp.float32)
        parts.append(part)
        values = values - part
    if 3 * rows % 16:
        parts.append(jnp.zeros_like(values))
    stacked = jnp.concatenate(parts, axis=0).astype(jnp.bfloat16)
    sums = lax.dot_general(stacked, pairs, (((1,), (0,)), ((), ())), preferred_element_type=jnp.float32)
    return sums[:rows] + (sums[rows : 2 * rows] + sums[2 * rows : 3 * rows])


def paired_rows(values):
    return values + pltpu.roll(values, values.shape[0] - 1, 0)


def put_edges(v, to_x, to_zx):
    last = v.shape[1] - 1
    for x in range(v.shape[0]):
        first_row, last_row = v[x, 0:1, :], v[x, last : last + 1, :]
        to_x[x : x + 1, :] = pick(even("sub"), last_row, first_row)
        to_zx[x : x + 1, :] = pick(even("sub"), first_row, last_row)


def edges_kernel(v, to_x, to_zx):
    put_edges(v, to_x, to_zx)


def faces_kernel(v, from_x, from_zx, to_core, to_y):
    planes, rows, _ = v.shape
    before, after = sides(from_x[...], from_zx[0:planes, :])
    for ref, swap in ((to_core, False), (to_y, True)):
        def choose(a, b):
            return pick(even("grp"), b, a) if swap else pick(even("grp"), a, b)

        ref[0:rows, :] = choose(v[planes - 1], v[0])
        ref[rows : rows + 1, :] = choose(before[planes - 1 :], before[0:1])
        ref[rows + 1 : rows + 2, :] = choose(after[planes - 1 :], after[0:1])


def fine_neighbours(groups, v, from_x, from_zx, from_core, from_y):
    planes, rows, _ = v.shape
    group = lax.axis_index("grp")
    before, after = sides(from_x[...], from_zx[0:planes, :])
    low = pick(even("grp"), from_y[...], from_core[...])
    high = pick(even("grp"), from_core[...], from_y[...])
    low = pick(group == 0, jnp.zeros_like(low), low)
    high = pick(group == groups - 1, jnp.zeros_like(high), high)
    faces = [neighbours(f[0:rows], f[rows : rows + 1], f[rows + 1 : rows + 2]) for f in (low, high)]
    inner = [neighbours(v[x], before[x : x + 1], after[x : x + 1]) for x in range(planes)]
    return [faces[0], *inner, faces[1]]


def sweep_kernel(groups, v, first, c, from_x, from_zx, from_core, from_y, out, to_x, to_zx):
    planes, rows, extent = v.shape
    near = fine_neighbours(groups, v, from_x, from_zx, from_core, from_y)
    for x in range(planes):
        for lanes in lane_tiles(extent):
            sums = outer_terms(near[x : x + 3], lambda k: c[k, x, :, lanes], lanes)
            out[x, :, lanes] = first[x, :, lanes] + (1.0 - WEIGHT) * v[x, :, lanes] - sums
    put_edges(out, to_x, to_zx)


def residual_kernel(
    groups, v, first, c, from_x, from_zx, from_core, from_y, center, iterate, to_x, to_zx, held
):
    planes, rows, extent = v.shape
    near = fine_neighbours(groups, v, from_x, from_zx, from_core, from_y)
    for x in range(0, planes, 2):
        for lanes in lane_tiles(extent):
            total = None
            for p in (x, x + 1):
                sums = outer_terms(near[p : p + 3], lambda k: c[k, p, :, lanes], lanes)
                part = first[p, :, lanes] - WEIGHT * v[p, :, lanes] - sums
                part = (1.0 / WEIGHT) * c[CENTER, p, :, lanes] * part
                total = part if total is None else total + part
            held[x // 2 * rows : (x // 2 + 1) * rows, lanes] = total
    total = (0.5 * WEIGHT) * paired_rows(paired_lanes(held[...]))
    half = rows // 2
    for x in range(planes // 2):
        for y in range(half):
            row = x * rows + 2 * y
            iterate[x, y : y + 1, :] = total[row : row + 1]
    iterate[...] = iterate[...] / center[...]
    for x in range(planes // 2):
        first_rows, last_rows = iterate[x, 0:3, :], iterate[x, half - 3 : half, :]
        to_x[4 * x : 4 * x + 3, :] = pick(even("sub"), last_rows, first_rows)
        to_zx[4 * x : 4 * x + 3, :] = pick(even("sub"), first_rows, last_rows)


def middle_faces_kernel(mine, from_x, from_zx, out):
    planes, half, _ = mine.shape
    before, after = sides(from_x[...], from_zx[0 : 4 * planes, :])
    for x in range(planes):
        row = x * ROWS
        out[row : row + 2, :] = before[4 * x + 1 : 4 * x + 3]
        out[row + 2 : row + 2 + half, :] = mine[x]
        out[row + 2 + half : row + ROWS, :] = after[4 * x : 4 * x + 2]
        extra = planes * ROWS + 2 * x
        out[extra : extra + 1, :] = before[4 * x : 4 * x + 1]
        out[extra + 1 : extra + 2, :] = after[4 * x + 2 : 4 * x + 3]


def coefficient_edges_kernel(c, to_x, to_zx):
    rows = c.shape[2]
    first, last = c[:, :, 0:2, :], c[:, :, rows - 2 : rows, :]
    to_x[...] = pick(even("sub"), last, first)
    to_zx[...] = pick(even("sub"), first, last)


def coefficient_scale_kernel(c, out):
    for x in range(c.shape[1]):
        out[:, x] = scaled(c[:, x])
        for k in range(27):
            out[k, x] = homed(k, out[k, x])


def scaled(c):
    center = c[CENTER : CENTER + 1]
    ratio = WEIGHT / jnp.where(center > 0.0, center, 1.0)
    index = lax.broadcasted_iota(jnp.int32, c.shape, 0)
    return c * jnp.where(index == CENTER, 1.0, ratio)


def coefficient_pack_kernel(known, *refs):
    coarse, (c, from_x, from_zx, _, __, middle_part, whole) = refs[:known], refs[known:]
    _, planes, rows, extent = c.shape
    tiles = extent // LANES
    before, after = sides(from_x[...], from_zx[...])
    for x in range(planes):
        for l, lanes in enumerate(lane_tiles(extent)):
            row = (x * tiles + l) * ROWS
            whole[:, row : row + 2, :] = before[:, x, :, lanes]
            whole[:, row + 2 : row + 2 + rows, :] = c[:, x, :, lanes]
            whole[:, row + 2 + rows : row + ROWS, :] = after[:, x, :, lanes]
    row = planes * tiles * ROWS
    for t in range(0, row, ROWS):
        part = scaled(whole[:, t : t + ROWS, :])
        l = t // ROWS % tiles
        for k in range(27):
            ready = homed(k, part[k], l == 0, l == tiles - 1)
            whole[k, t : t + ROWS, :] = ready
            middle_part[k, t : t + ROWS, :] = ready
    for ref in coarse:
        for x in range(ref.shape[1]):
            for t in range(0, ref.shape[2], ROWS):
                whole[:, row : row + ROWS, :] = scaled(ref[:, x, t : t + ROWS, :])
                row += ROWS


def middle_kernel(
    groups, planes, packed, near_core, near_y, far_below, far_above, own, core, other, iterate, coarse, held
):
    extent = packed.shape[-1]
    tiles = extent // LANES
    half = ROWS - 4
    group = lax.axis_index("grp")
    window = 3 * planes

    below = pick(even("grp"), near_y[...], near_core[...])
    above = pick(even("grp"), near_core[...], near_y[...])
    blocks = {-2: far_below[...], -1: below, 0: packed[...], 1: above, 2: far_above[...]}
    for away in (-2, -1, 1, 2):
        inside = (group + away >= 0) & (group + away < groups)
        blocks[away] = pick(inside, blocks[away], jnp.zeros_like(blocks[away]))
    first, near = [], []
    for p in range(-1, window + 1):
        block, x = blocks[p // planes - 1], p % planes
        v, extra = block[x * ROWS : (x + 1) * ROWS], planes * ROWS + 2 * x
        first.append(v)
        near.append(neighbours(v, block[extra : extra + 1], block[extra + 1 : extra + 2]))

    def work(parts):
        def terms(forms, w, lanes):
            row = (w % planes * tiles + lanes.start // LANES) * ROWS
            return outer_terms(forms, lambda k: parts[w // planes][k, row : row + ROWS, :], lanes)

        def swept(forms, field, w):
            sums = jnp.concatenate([terms(forms, w, lanes) for lanes in lane_tiles(extent)], axis=1)
            return first[w + 1] + (1.0 - WEIGHT) * field - sums

        low, high = planes - 2, 2 * planes + 2
        once = {w: swept(near[w : w + 3], first[w + 1], w) for w in range(low, high)}
        forms = {w: neighbours(v) for w, v in once.items()}
        low, high = low + 1, high - 1
        twice = {w: swept([forms[w + x] for x in (-1, 0, 1)], once[w], w) for w in range(low, high)}
        forms = {w: neighbours(v) for w, v in twice.items()}
        for x in range(planes):
            w = planes + x
            iterate[x] = twice[w][2 : 2 + half]
            for lanes in lane_tiles(extent):
                row = (x * tiles + lanes.start // LANES) * ROWS
                sums = terms([forms[w + i] for i in (-1, 0, 1)], w, lanes)
                rest = first[w + 1][:, lanes] - WEIGHT * twice[w][:, lanes] - sums
                held[x, :, lanes] = (1.0 / WEIGHT) * own[CENTER, row : row + ROWS, :] * rest

    @pl.when(even("grp"))
    def _():
        work((other, own, core))

    @pl.when(jnp.logical_not(even("grp")))
    def _():
        work((core, own, other))

    place_of = lax.broadcasted_iota(jnp.int32, (ROWS, extent // 2), 0)
    for x in range(planes // 2):
        total = 0.5 * paired_rows(paired_lanes(held[2 * x] + held[2 * x + 1]))
        value = pltpu.roll(total, ROWS - 2, 0)
        for i in range(1, half // 2):
            value = jnp.where(place_of == i, pltpu.roll(total, ROWS - 2 - i, 0), value)
        for device in range(coarse.shape[0]):
            coarse[device, x] = value[: half // 2]


def coarse_order_kernel(planes, rows, start, offsets, own, core, out):
    group = lax.axis_index("grp")
    row_of = lax.broadcasted_iota(jnp.int32, (rows, out.shape[-1]), 0)
    for ref, flip in ((own, 0), (core, 1)):
        for i, offset in enumerate(offsets):
            owner = jnp.bitwise_xor(group, offset ^ flip)
            for x in range(planes):
                row = start + (i * planes + x) * rows
                for k in range(27):
                    part = ref[k, row : row + rows, :]
                    if k // 3 % 3 != 1:
                        outside = 0 if k // 3 % 3 == 0 else rows - 1
                        part = jnp.where(row_of == outside, 0.0, part)
                    out[owner * planes + x, k] = homed(k, part)


def coarse_kernel(groups, planes, gathered, c, fine, middle, out, fine_out, middle_out, first, sems):
    kept = [
        pltpu.make_async_copy(fine, fine_out, sems.at[0]),
        pltpu.make_async_copy(middle, middle_out, sems.at[1]),
    ]
    for copy in kept:
        copy.start()
    total, rows, extent = first.shape
    subs = gathered.shape[0] // groups
    each = rows // subs
    for g in range(groups):
        for s in range(subs):
            for x in range(planes):
                first[g * planes + x, s * each : (s + 1) * each, :] = gathered[g * subs + s, x]
    for p in range(total):
        first[p] = WEIGHT * first[p] / c[p, CENTER]

    def sweep(_, field):
        near = [None, *map(neighbours, field), None]
        every = slice(0, extent)
        fresh = []
        for p in range(total):
            sums = outer_terms(near[p : p + 3], lambda k: c[p, k], every)
            fresh.append(first[p] + (1.0 - WEIGHT) * field[p] - sums)
        return tuple(fresh)

    field = lax.fori_loop(0, NB - 1, sweep, tuple(first[p] for p in range(total)))
    for p in range(total):
        first[p] = field[p]
    for x in range(planes):
        out[x] = first[lax.axis_index("grp") * planes + x]
    for copy in kept:
        copy.wait()


def after(value, *others):
    return lax.optimization_barrier((value, *others))[0]


def after_all(values, *others):
    return lax.optimization_barrier((*values, *others))[: len(values)]


def swaps(pairs):
    return [p for a, b in pairs for p in ((a, b), (b, a))]


def body(source, fine, middle, coarse):
    groups, subs = lax.axis_size("grp"), lax.axis_size("sub")
    _, planes, rows, extent = fine.shape
    _, middle_planes, middle_rows, middle_extent = middle.shape
    _, coarse_planes, coarse_rows, coarse_extent = coarse.shape

    x_pairs = swaps([(i, i + 1) for i in range(0, subs, 2)])
    zx_pairs = swaps(
        [(g * subs + i, g * subs + i + 1) for g in range(groups) for i in range(1, subs - 1, 2)]
        + [(g * subs + i, (g + 1) * subs + i) for g in range(0, groups, 2) for i in (0, subs - 1)]
    )
    core_pairs = swaps([(i, i + 1) for i in range(0, groups, 2)])
    y_pairs = swaps([(i, i + 1) for i in range(1, groups - 1, 2)])
    y_ring = y_pairs + [(groups - 1, 0), (0, groups - 1)]

    def along_sub(pair):
        to_x, to_zx = pair
        from_x = lax.ppermute(to_x, "sub", x_pairs)
        return from_x, lax.ppermute(to_zx, ("grp", "sub"), zx_pairs)

    def along_grp(v, halo):
        to_core, to_y = call(faces_kernel, [shape(rows + 8, extent)] * 2, [v, *halo])
        from_core = lax.ppermute(to_core, "grp", core_pairs)
        from_y = lax.ppermute(to_y, "grp", y_ring)
        return (*halo, from_core, from_y)

    weights = call(coefficient_scale_kernel, shape(*fine.shape), [fine])
    v = WEIGHT * source / fine[CENTER]
    first = v
    to_x, to_zx = call(edges_kernel, [shape(planes, extent), shape(4 * planes, extent)], [v])

    def sweep(v, halo):
        v, *edges = call(
            functools.partial(sweep_kernel, groups),
            [shape(planes, rows, extent), shape(planes, extent), shape(4 * planes, extent)],
            [v, first, weights, *halo],
        )
        return v, along_sub(edges)

    edges_c = call(
        coefficient_edges_kernel,
        [shape(27, middle_planes, 2, middle_extent)] * 2,
        [middle],
    )
    halo = along_sub((to_x, to_zx))
    halo_c = along_sub(after_all(edges_c, *halo))
    halo = along_grp(after(v, *edges_c), halo)
    known = {0: coarse}
    bit = groups // 2
    while bit > 1:
        for offset in sorted(known):
            known[offset ^ bit] = lax.ppermute(known[offset], "grp", [(i, i ^ bit) for i in range(groups)])
        bit //= 2
    offsets = sorted(known)
    v, halo = sweep(v, halo)
    halo = along_grp(v, halo)
    start = middle_planes * (middle_extent // LANES) * ROWS
    middle_part, own = call(
        functools.partial(coefficient_pack_kernel, len(known)),
        [shape(27, start, LANES), shape(27, start + len(known) * coarse_planes * coarse_rows, LANES)],
        [*(known[o] for o in offsets), middle, *halo_c, *halo[2:]],
    )
    core = lax.ppermute(own, "grp", core_pairs)
    other = lax.ppermute(middle_part, "grp", y_pairs)
    v, halo = sweep(v, halo)
    fine_iterate = v
    halo = along_grp(v, halo)
    iterate, *edges = call(
        functools.partial(residual_kernel, groups),
        [shape(middle_planes, middle_rows, middle_extent)]
        + [shape(4 * middle_planes, middle_extent), shape(8 * middle_planes, middle_extent)],
        [v, first, weights, *halo, middle[CENTER]],
        [pltpu.VMEM((planes // 2 * rows, extent), jnp.float32)],
    )
    total = groups * coarse_planes
    ordered = call(
        functools.partial(coarse_order_kernel, coarse_planes, coarse_rows, start, offsets),
        shape(total, 27, coarse_rows, coarse_extent),
        [own, core],
    )
    packed = call(
        middle_faces_kernel,
        shape(middle_planes * ROWS + 8, middle_extent),
        [after(iterate, ordered), *along_sub(edges)],
    )
    near_core = lax.ppermute(packed, "grp", core_pairs)
    if groups == 4:
        far_below = far_above = lax.ppermute(packed, "grp", swaps([(0, 2), (1, 3)]))
        near_y = lax.ppermute(packed, "grp", y_ring)
    else:
        near_y = lax.ppermute(packed, "grp", y_pairs)
        up = [(i, i + 2) for i in range(groups - 2)]
        far_below = lax.ppermute(packed, "grp", up)
        far_above = lax.ppermute(packed, "grp", [(j, i) for i, j in up])
    middle_iterate, coarse_source = call(
        functools.partial(middle_kernel, groups, middle_planes),
        [
            shape(middle_planes, middle_rows, middle_extent),
            shape(groups * subs, coarse_planes, coarse_rows // subs, coarse_extent),
        ],
        [packed, near_core, near_y, far_below, far_above, own, core, other],
        [pltpu.VMEM((middle_planes, ROWS, middle_extent), jnp.float32)],
    )
    gathered = lax.all_to_all(coarse_source, ("grp", "sub"), 0, 0, tiled=True)
    vmem, hbm = pl.BlockSpec(memory_space=pltpu.VMEM), pl.BlockSpec(memory_space=pl.ANY)
    coarse_iterate, fine_iterate, middle_iterate = call(
        functools.partial(coarse_kernel, groups, coarse_planes),
        [
            shape(coarse_planes, coarse_rows, coarse_extent),
            shape(*fine_iterate.shape),
            shape(*middle_iterate.shape),
        ],
        [gathered, ordered, fine_iterate, middle_iterate],
        [
            pltpu.VMEM((total, coarse_rows, coarse_extent), jnp.float32),
            pltpu.SemaphoreType.DMA((2,)),
        ],
        out_specs=[vmem, hbm, hbm],
    )
    return fine_iterate, middle_iterate, coarse_iterate


def solution(mesh):
    placed = (
        P("grp", "sub", None),
        P(None, "grp", "sub", None),
        P(None, "grp", "sub", None),
        P(None, "grp", None, None),
    )
    return jax.shard_map(
        body,
        mesh=mesh,
        in_specs=placed,
        out_specs=(P("grp", "sub", None), P("grp", "sub", None), P("grp", None, None)),
        check_vma=False,
    )
```

```python
import functools

import jax
import jax.numpy as jnp
from jax import lax
from jax.experimental import pallas as pl
from jax.experimental.pallas import tpu as pltpu
from jax.sharding import PartitionSpec as P

NU0 = 3
NB = 16
WEIGHT = 0.8
CENTER = 13
LANES = 128
ROWS = 8


def shape(*dims):
    return jax.ShapeDtypeStruct(dims, jnp.float32)


def call(kernel, outs, args, scratch=(), out_specs=None):
    vmem = pl.BlockSpec(memory_space=pltpu.VMEM)
    return pl.pallas_call(
        kernel,
        out_shape=outs,
        in_specs=[vmem] * len(args),
        out_specs=out_specs or jax.tree.map(lambda _: vmem, outs),
        scratch_shapes=list(scratch),
        compiler_params=pltpu.CompilerParams(vmem_limit_bytes=12 << 20),
    )(*args)


def even(axis):
    return lax.rem(lax.axis_index(axis), 2) == 0


def pick(condition, a, b):
    return jnp.where(jnp.broadcast_to(condition, a.shape), a, b)


def sides(from_x, from_zx):
    sub, subs = lax.axis_index("sub"), lax.axis_size("sub")
    from_zx = pick((sub == 0) | (sub == subs - 1), jnp.zeros_like(from_zx), from_zx)
    return pick(even("sub"), from_zx, from_x), pick(even("sub"), from_x, from_zx)


def rolled(values):
    extent = values.shape[-1]
    return pltpu.roll(values, 1, 1), values, pltpu.roll(values, extent - 1, 1)


def homed(k, part, first=True, last=True):
    rows, extent = part.shape
    y, z = k // 3 % 3, k % 3
    lane = lax.broadcasted_iota(jnp.int32, part.shape, 1)
    if z == 0 and first:
        part = jnp.where(lane == 0, 0.0, part)
    if z == 2 and last:
        part = jnp.where(lane == extent - 1, 0.0, part)
    if y != 1:
        part = pltpu.roll(part, rows - 1 if y == 0 else 1, 0)
    return part


def neighbours(values, before=None, after=None):
    here = rolled(values)
    if before is None:
        return here, here, here
    row = lax.broadcasted_iota(jnp.int32, values.shape, 0)
    lower = [jnp.where(row == values.shape[0] - 1, b, h) for b, h in zip(rolled(before), here)]
    upper = [jnp.where(row == 0, a, h) for a, h in zip(rolled(after), here)]
    return lower, here, upper


def outer_terms(near, coefficient, lanes):
    sums = [None] * 3
    for x in range(3):
        for y in range(3):
            for z in range(3):
                k = 9 * x + 3 * y + z
                if k == CENTER or near[x] is None:
                    continue
                term = coefficient(k) * near[x][y][z][:, lanes]
                sums[y] = term if sums[y] is None else sums[y] + term
    rows = sums[1].shape[0]
    return sums[1] + (pltpu.roll(sums[0], 1, 0) + pltpu.roll(sums[2], rows - 1, 0))


def lane_tiles(extent):
    return [slice(l, l + LANES) for l in range(0, extent, LANES)]


def paired_lanes(values):
    rows, extent = values.shape
    row = lax.broadcasted_iota(jnp.int32, (extent, extent // 2), 0)
    column = lax.broadcasted_iota(jnp.int32, (extent, extent // 2), 1)
    pairs = jnp.where(lax.shift_right_logical(row, 1) == column, 1.0, 0.0).astype(jnp.bfloat16)
    parts = []
    for _ in range(3):
        part = values.astype(jnp.bfloat16).astype(jnp.float32)
        parts.append(part)
        values = values - part
    if 3 * rows % 16:
        parts.append(jnp.zeros_like(values))
    stacked = jnp.concatenate(parts, axis=0).astype(jnp.bfloat16)
    sums = lax.dot_general(stacked, pairs, (((1,), (0,)), ((), ())), preferred_element_type=jnp.float32)
    return sums[:rows] + (sums[rows : 2 * rows] + sums[2 * rows : 3 * rows])


def paired_rows(values):
    return values + pltpu.roll(values, values.shape[0] - 1, 0)


def put_edges(v, to_x, to_zx):
    last = v.shape[1] - 1
    for x in range(v.shape[0]):
        first_row, last_row = v[x, 0:1, :], v[x, last : last + 1, :]
        to_x[x : x + 1, :] = pick(even("sub"), last_row, first_row)
        to_zx[x : x + 1, :] = pick(even("sub"), first_row, last_row)


def edges_kernel(v, to_x, to_zx):
    put_edges(v, to_x, to_zx)


def faces_kernel(v, from_x, from_zx, to_core, to_y):
    planes, rows, _ = v.shape
    before, after = sides(from_x[...], from_zx[0:planes, :])
    for ref, swap in ((to_core, False), (to_y, True)):
        def choose(a, b):
            return pick(even("grp"), b, a) if swap else pick(even("grp"), a, b)

        ref[0:rows, :] = choose(v[planes - 1], v[0])
        ref[rows : rows + 1, :] = choose(before[planes - 1 :], before[0:1])
        ref[rows + 1 : rows + 2, :] = choose(after[planes - 1 :], after[0:1])


def fine_neighbours(groups, v, from_x, from_zx, from_core, from_y):
    planes, rows, _ = v.shape
    group = lax.axis_index("grp")
    before, after = sides(from_x[...], from_zx[0:planes, :])
    low = pick(even("grp"), from_y[0 : rows + 8, :], from_core[...])
    high = pick(even("grp"), from_core[...], from_y[0 : rows + 8, :])
    low = pick(group == 0, jnp.zeros_like(low), low)
    high = pick(group == groups - 1, jnp.zeros_like(high), high)
    faces = [neighbours(f[0:rows], f[rows : rows + 1], f[rows + 1 : rows + 2]) for f in (low, high)]
    inner = [neighbours(v[x], before[x : x + 1], after[x : x + 1]) for x in range(planes)]
    return [faces[0], *inner, faces[1]]


def sweep_kernel(groups, v, first, c, from_x, from_zx, from_core, from_y, out, to_x, to_zx):
    planes, rows, extent = v.shape
    near = fine_neighbours(groups, v, from_x, from_zx, from_core, from_y)
    for x in range(planes):
        for lanes in lane_tiles(extent):
            sums = outer_terms(near[x : x + 3], lambda k: c[k, x, :, lanes], lanes)
            out[x, :, lanes] = first[x, :, lanes] + (1.0 - WEIGHT) * v[x, :, lanes] - sums
    put_edges(out, to_x, to_zx)


def residual_kernel(
    groups, v, first, c, from_x, from_zx, from_core, from_y, center, iterate, to_x, to_zx, held
):
    planes, rows, extent = v.shape
    near = fine_neighbours(groups, v, from_x, from_zx, from_core, from_y)
    for x in range(0, planes, 2):
        for lanes in lane_tiles(extent):
            total = None
            for p in (x, x + 1):
                sums = outer_terms(near[p : p + 3], lambda k: c[k, p, :, lanes], lanes)
                part = first[p, :, lanes] - WEIGHT * v[p, :, lanes] - sums
                part = (1.0 / WEIGHT) * c[CENTER, p, :, lanes] * part
                total = part if total is None else total + part
            held[x // 2 * rows : (x // 2 + 1) * rows, lanes] = total
    total = (0.5 * WEIGHT) * paired_rows(paired_lanes(held[...]))
    half = rows // 2
    for x in range(planes // 2):
        for y in range(half):
            row = x * rows + 2 * y
            iterate[x, y : y + 1, :] = total[row : row + 1]
    iterate[...] = iterate[...] / center[...]
    for x in range(planes // 2):
        first_rows, last_rows = iterate[x, 0:3, :], iterate[x, half - 3 : half, :]
        to_x[4 * x : 4 * x + 3, :] = pick(even("sub"), last_rows, first_rows)
        to_zx[4 * x : 4 * x + 3, :] = pick(even("sub"), first_rows, last_rows)


def middle_faces_kernel(mine, from_x, from_zx, out):
    planes, half, _ = mine.shape
    before, after = sides(from_x[...], from_zx[0 : 4 * planes, :])
    for x in range(planes):
        row = x * ROWS
        out[row : row + 2, :] = before[4 * x + 1 : 4 * x + 3]
        out[row + 2 : row + 2 + half, :] = mine[x]
        out[row + 2 + half : row + ROWS, :] = after[4 * x : 4 * x + 2]
        extra = planes * ROWS + 2 * x
        out[extra : extra + 1, :] = before[4 * x : 4 * x + 1]
        out[extra + 1 : extra + 2, :] = after[4 * x + 2 : 4 * x + 3]


def coefficient_edges_kernel(c, to_x, to_zx):
    rows = c.shape[2]
    first, last = c[:, :, 0:2, :], c[:, :, rows - 2 : rows, :]
    to_x[...] = pick(even("sub"), last, first)
    to_zx[...] = pick(even("sub"), first, last)


def coefficient_scale_kernel(c, out):
    for x in range(c.shape[1]):
        out[:, x] = scaled(c[:, x])
        for k in range(27):
            out[k, x] = homed(k, out[k, x])


def scaled(c):
    center = c[CENTER : CENTER + 1]
    ratio = WEIGHT / jnp.where(center > 0.0, center, 1.0)
    index = lax.broadcasted_iota(jnp.int32, c.shape, 0)
    return c * jnp.where(index == CENTER, 1.0, ratio)


def coefficient_pack_kernel(known, *refs):
    coarse, (c, from_x, from_zx, _, __, middle_part, whole) = refs[:known], refs[known:]
    _, planes, rows, extent = c.shape
    tiles = extent // LANES
    before, after = sides(from_x[...], from_zx[...])
    for x in range(planes):
        for l, lanes in enumerate(lane_tiles(extent)):
            row = (x * tiles + l) * ROWS
            whole[:, row : row + 2, :] = before[:, x, :, lanes]
            whole[:, row + 2 : row + 2 + rows, :] = c[:, x, :, lanes]
            whole[:, row + 2 + rows : row + ROWS, :] = after[:, x, :, lanes]
    row = planes * tiles * ROWS
    for t in range(0, row, ROWS):
        part = scaled(whole[:, t : t + ROWS, :])
        l = t // ROWS % tiles
        for k in range(27):
            ready = homed(k, part[k], l == 0, l == tiles - 1)
            whole[k, t : t + ROWS, :] = ready
            middle_part[k, t : t + ROWS, :] = ready
    for ref in coarse:
        for x in range(ref.shape[1]):
            for t in range(0, ref.shape[2], ROWS):
                whole[:, row : row + ROWS, :] = scaled(ref[:, x, t : t + ROWS, :])
                row += ROWS


def middle_kernel(
    groups, planes, packed, near_core, near_y, far_below, far_above, own, core, other, iterate, coarse, held
):
    extent = packed.shape[-1]
    tiles = extent // LANES
    half = ROWS - 4
    group = lax.axis_index("grp")
    window = 3 * planes

    below = pick(even("grp"), near_y[...], near_core[...])
    above = pick(even("grp"), near_core[...], near_y[...])
    blocks = {-2: far_below[...], -1: below, 0: packed[...], 1: above, 2: far_above[...]}
    for away in (-2, -1, 1, 2):
        inside = (group + away >= 0) & (group + away < groups)
        blocks[away] = pick(inside, blocks[away], jnp.zeros_like(blocks[away]))
    first, near = [], []
    for p in range(-1, window + 1):
        block, x = blocks[p // planes - 1], p % planes
        v, extra = block[x * ROWS : (x + 1) * ROWS], planes * ROWS + 2 * x
        first.append(v)
        near.append(neighbours(v, block[extra : extra + 1], block[extra + 1 : extra + 2]))

    def work(parts):
        def terms(forms, w, lanes):
            row = (w % planes * tiles + lanes.start // LANES) * ROWS
            return outer_terms(forms, lambda k: parts[w // planes][k, row : row + ROWS, :], lanes)

        def swept(forms, field, w):
            sums = jnp.concatenate([terms(forms, w, lanes) for lanes in lane_tiles(extent)], axis=1)
            return first[w + 1] + (1.0 - WEIGHT) * field - sums

        low, high = planes - 2, 2 * planes + 2
        once = {w: swept(near[w : w + 3], first[w + 1], w) for w in range(low, high)}
        forms = {w: neighbours(v) for w, v in once.items()}
        low, high = low + 1, high - 1
        twice = {w: swept([forms[w + x] for x in (-1, 0, 1)], once[w], w) for w in range(low, high)}
        forms = {w: neighbours(v) for w, v in twice.items()}
        for x in range(planes):
            w = planes + x
            iterate[x] = twice[w][2 : 2 + half]
            for lanes in lane_tiles(extent):
                row = (x * tiles + lanes.start // LANES) * ROWS
                sums = terms([forms[w + i] for i in (-1, 0, 1)], w, lanes)
                rest = first[w + 1][:, lanes] - WEIGHT * twice[w][:, lanes] - sums
                held[x, :, lanes] = (1.0 / WEIGHT) * own[CENTER, row : row + ROWS, :] * rest

    @pl.when(even("grp"))
    def _():
        work((other, own, core))

    @pl.when(jnp.logical_not(even("grp")))
    def _():
        work((core, own, other))

    place_of = lax.broadcasted_iota(jnp.int32, (ROWS, extent // 2), 0)
    for x in range(planes // 2):
        total = 0.5 * paired_rows(paired_lanes(held[2 * x] + held[2 * x + 1]))
        value = pltpu.roll(total, ROWS - 2, 0)
        for i in range(1, half // 2):
            value = jnp.where(place_of == i, pltpu.roll(total, ROWS - 2 - i, 0), value)
        for device in range(coarse.shape[0]):
            coarse[device, x] = value[: half // 2]


def coarse_order_kernel(planes, rows, start, offsets, own, core, out):
    group = lax.axis_index("grp")
    row_of = lax.broadcasted_iota(jnp.int32, (rows, out.shape[-1]), 0)
    for ref, flip in ((own, 0), (core, 1)):
        for i, offset in enumerate(offsets):
            owner = jnp.bitwise_xor(group, offset ^ flip)
            for x in range(planes):
                row = start + (i * planes + x) * rows
                for k in range(27):
                    part = ref[k, row : row + rows, :]
                    if k // 3 % 3 != 1:
                        outside = 0 if k // 3 % 3 == 0 else rows - 1
                        part = jnp.where(row_of == outside, 0.0, part)
                    out[owner * planes + x, k] = homed(k, part)


def coarse_kernel(groups, planes, gathered, c, fine, middle, out, fine_out, middle_out, first, sems):
    kept = [
        pltpu.make_async_copy(fine, fine_out, sems.at[0]),
        pltpu.make_async_copy(middle, middle_out, sems.at[1]),
    ]
    for copy in kept:
        copy.start()
    total, rows, extent = first.shape
    subs = gathered.shape[0] // groups
    each = rows // subs
    for g in range(groups):
        for s in range(subs):
            for x in range(planes):
                first[g * planes + x, s * each : (s + 1) * each, :] = gathered[g * subs + s, x]
    for p in range(total):
        first[p] = WEIGHT * first[p] / c[p, CENTER]

    def sweep(_, field):
        near = [None, *map(neighbours, field), None]
        every = slice(0, extent)
        fresh = []
        for p in range(total):
            sums = outer_terms(near[p : p + 3], lambda k: c[p, k], every)
            fresh.append(first[p] + (1.0 - WEIGHT) * field[p] - sums)
        return tuple(fresh)

    field = lax.fori_loop(0, NB - 1, sweep, tuple(first[p] for p in range(total)), unroll=5)
    for p in range(total):
        first[p] = field[p]
    for x in range(planes):
        out[x] = first[lax.axis_index("grp") * planes + x]
    for copy in kept:
        copy.wait()


def after(value, *others):
    return lax.optimization_barrier((value, *others))[0]


def after_all(values, *others):
    return lax.optimization_barrier((*values, *others))[: len(values)]


def swaps(pairs):
    return [p for a, b in pairs for p in ((a, b), (b, a))]


def body(source, fine, middle, coarse):
    groups, subs = lax.axis_size("grp"), lax.axis_size("sub")
    _, planes, rows, extent = fine.shape
    _, middle_planes, middle_rows, middle_extent = middle.shape
    _, coarse_planes, coarse_rows, coarse_extent = coarse.shape

    x_pairs = swaps([(i, i + 1) for i in range(0, subs, 2)])
    zx_pairs = swaps(
        [(g * subs + i, g * subs + i + 1) for g in range(groups) for i in range(1, subs - 1, 2)]
        + [(g * subs + i, (g + 1) * subs + i) for g in range(0, groups, 2) for i in (0, subs - 1)]
    )
    core_pairs = swaps([(i, i + 1) for i in range(0, groups, 2)])
    y_pairs = swaps([(i, i + 1) for i in range(1, groups - 1, 2)])
    y_ring = y_pairs + [(groups - 1, 0), (0, groups - 1)]

    def along_sub(pair):
        to_x, to_zx = pair
        from_x = lax.ppermute(to_x, "sub", x_pairs)
        return from_x, lax.ppermute(to_zx, ("grp", "sub"), zx_pairs)

    def along_grp(v, halo):
        to_core, to_y = call(faces_kernel, [shape(rows + 8, extent), shape(2 * rows + 8, extent)], [v, *halo])
        from_core = lax.ppermute(to_core, "grp", core_pairs)
        from_y = lax.ppermute(to_y, "grp", y_ring)
        return (*halo, from_core, from_y)

    weights = call(coefficient_scale_kernel, shape(*fine.shape), [fine])
    v = WEIGHT * source / fine[CENTER]
    first = v
    to_x, to_zx = call(edges_kernel, [shape(planes, extent), shape(2 * planes, extent)], [v])

    def sweep(v, halo):
        v, *edges = call(
            functools.partial(sweep_kernel, groups),
            [shape(planes, rows, extent), shape(planes, extent), shape(2 * planes, extent)],
            [v, first, weights, *halo],
        )
        return v, along_sub(edges)

    edges_c = call(
        coefficient_edges_kernel,
        [shape(27, middle_planes, 2, middle_extent)] * 2,
        [middle],
    )
    halo = along_sub((to_x, to_zx))
    halo_c = along_sub(after_all(edges_c, *halo))
    halo = along_grp(after(v, weights, *edges_c), halo)
    known = {0: after(coarse, first)}
    bit = groups // 2
    while bit > 1:
        for offset in sorted(known):
            known[offset ^ bit] = lax.ppermute(known[offset], "grp", [(i, i ^ bit) for i in range(groups)])
        bit //= 2
    offsets = sorted(known)
    v, halo = sweep(v, halo)
    halo = along_grp(v, halo)
    start = middle_planes * (middle_extent // LANES) * ROWS
    middle_part, own = call(
        functools.partial(coefficient_pack_kernel, len(known)),
        [shape(27, start, LANES), shape(27, start + len(known) * coarse_planes * coarse_rows, LANES)],
        [*(known[o] for o in offsets), middle, *halo_c, *halo[2:]],
    )
    core = lax.ppermute(own, "grp", core_pairs)
    other = lax.ppermute(middle_part, "grp", y_pairs)
    v, halo = sweep(v, halo)
    fine_iterate = v
    halo = along_grp(v, halo)
    iterate, *edges = call(
        functools.partial(residual_kernel, groups),
        [shape(middle_planes, middle_rows, middle_extent)]
        + [shape(4 * middle_planes, middle_extent), shape(8 * middle_planes, middle_extent)],
        [v, first, weights, *halo, middle[CENTER]],
        [pltpu.VMEM((planes // 2 * rows, extent), jnp.float32)],
    )
    total = groups * coarse_planes
    ordered = call(
        functools.partial(coarse_order_kernel, coarse_planes, coarse_rows, start, offsets),
        shape(total, 27, coarse_rows, coarse_extent),
        [own, core],
    )
    packed = call(
        middle_faces_kernel,
        shape(middle_planes * ROWS + 8, middle_extent),
        [after(iterate, ordered), *along_sub(edges)],
    )
    near_core = lax.ppermute(packed, "grp", core_pairs)
    if groups == 4:
        far_below = far_above = lax.ppermute(packed, "grp", swaps([(0, 2), (1, 3)]))
        near_y = lax.ppermute(packed, "grp", y_ring)
    else:
        near_y = lax.ppermute(packed, "grp", y_pairs)
        up = [(i, i + 2) for i in range(groups - 2)]
        far_below = lax.ppermute(packed, "grp", up)
        far_above = lax.ppermute(packed, "grp", [(j, i) for i, j in up])
    middle_iterate, coarse_source = call(
        functools.partial(middle_kernel, groups, middle_planes),
        [
            shape(middle_planes, middle_rows, middle_extent),
            shape(groups * subs, coarse_planes, coarse_rows // subs, coarse_extent),
        ],
        [packed, near_core, near_y, far_below, far_above, own, core, other],
        [pltpu.VMEM((middle_planes, ROWS, middle_extent), jnp.float32)],
    )
    gathered = lax.all_to_all(coarse_source, ("grp", "sub"), 0, 0, tiled=True)
    vmem, hbm = pl.BlockSpec(memory_space=pltpu.VMEM), pl.BlockSpec(memory_space=pl.ANY)
    coarse_iterate, fine_iterate, middle_iterate = call(
        functools.partial(coarse_kernel, groups, coarse_planes),
        [
            shape(coarse_planes, coarse_rows, coarse_extent),
            shape(*fine_iterate.shape),
            shape(*middle_iterate.shape),
        ],
        [gathered, ordered, fine_iterate, middle_iterate],
        [
            pltpu.VMEM((total, coarse_rows, coarse_extent), jnp.float32),
            pltpu.SemaphoreType.DMA((2,)),
        ],
        out_specs=[vmem, hbm, hbm],
    )
    return fine_iterate, middle_iterate, coarse_iterate


def solution(mesh):
    placed = (
        P("grp", "sub", None),
        P(None, "grp", "sub", None),
        P(None, "grp", "sub", None),
        P(None, "grp", None, None),
    )
    return jax.shard_map(
        body,
        mesh=mesh,
        in_specs=placed,
        out_specs=(P("grp", "sub", None), P("grp", "sub", None), P("grp", None, None)),
        check_vma=False,
    )
```

```python
import functools

import jax
import jax.numpy as jnp
from jax import lax
from jax.experimental import pallas as pl
from jax.experimental.pallas import tpu as pltpu
from jax.sharding import PartitionSpec as P

NU0 = 3
NB = 16
WEIGHT = 0.8
CENTER = 13
EARLY = 18
LANES = 128
ROWS = 8


def shape(*dims):
    return jax.ShapeDtypeStruct(dims, jnp.float32)


def call(kernel, outs, args, scratch=(), out_specs=None):
    vmem = pl.BlockSpec(memory_space=pltpu.VMEM)
    return pl.pallas_call(
        kernel,
        out_shape=outs,
        in_specs=[vmem] * len(args),
        out_specs=out_specs or jax.tree.map(lambda _: vmem, outs),
        scratch_shapes=list(scratch),
        compiler_params=pltpu.CompilerParams(vmem_limit_bytes=12 << 20),
    )(*args)


def even(axis):
    return lax.rem(lax.axis_index(axis), 2) == 0


def pick(condition, a, b):
    return jnp.where(jnp.broadcast_to(condition, a.shape), a, b)


def sides(from_x, from_zx):
    sub, subs = lax.axis_index("sub"), lax.axis_size("sub")
    from_zx = pick((sub == 0) | (sub == subs - 1), jnp.zeros_like(from_zx), from_zx)
    return pick(even("sub"), from_zx, from_x), pick(even("sub"), from_x, from_zx)


def rolled(values):
    extent = values.shape[-1]
    return pltpu.roll(values, 1, 1), values, pltpu.roll(values, extent - 1, 1)


def homed(k, part, first=True, last=True):
    rows, extent = part.shape
    y, z = k // 3 % 3, k % 3
    lane = lax.broadcasted_iota(jnp.int32, part.shape, 1)
    if z == 0 and first:
        part = jnp.where(lane == 0, 0.0, part)
    if z == 2 and last:
        part = jnp.where(lane == extent - 1, 0.0, part)
    if y != 1:
        part = pltpu.roll(part, rows - 1 if y == 0 else 1, 0)
    return part


def neighbours(values, before=None, after=None):
    here = rolled(values)
    if before is None:
        return here, here, here
    row = lax.broadcasted_iota(jnp.int32, values.shape, 0)
    lower = [jnp.where(row == values.shape[0] - 1, b, h) for b, h in zip(rolled(before), here)]
    upper = [jnp.where(row == 0, a, h) for a, h in zip(rolled(after), here)]
    return lower, here, upper


def outer_terms(near, coefficient, lanes):
    sums = [None] * 3
    for x in range(3):
        for y in range(3):
            for z in range(3):
                k = 9 * x + 3 * y + z
                if k == CENTER or near[x] is None:
                    continue
                term = coefficient(k) * near[x][y][z][:, lanes]
                sums[y] = term if sums[y] is None else sums[y] + term
    rows = sums[1].shape[0]
    return sums[1] + (pltpu.roll(sums[0], 1, 0) + pltpu.roll(sums[2], rows - 1, 0))


def lane_tiles(extent):
    return [slice(l, l + LANES) for l in range(0, extent, LANES)]


def paired_lanes(values):
    rows, extent = values.shape
    row = lax.broadcasted_iota(jnp.int32, (extent, extent // 2), 0)
    column = lax.broadcasted_iota(jnp.int32, (extent, extent // 2), 1)
    pairs = jnp.where(lax.shift_right_logical(row, 1) == column, 1.0, 0.0).astype(jnp.bfloat16)
    parts = []
    for _ in range(3):
        part = values.astype(jnp.bfloat16).astype(jnp.float32)
        parts.append(part)
        values = values - part
    if 3 * rows % 16:
        parts.append(jnp.zeros_like(values))
    stacked = jnp.concatenate(parts, axis=0).astype(jnp.bfloat16)
    sums = lax.dot_general(stacked, pairs, (((1,), (0,)), ((), ())), preferred_element_type=jnp.float32)
    return sums[:rows] + (sums[rows : 2 * rows] + sums[2 * rows : 3 * rows])


def paired_rows(values):
    return values + pltpu.roll(values, values.shape[0] - 1, 0)


def put_edges(v, to_x, to_zx):
    last = v.shape[1] - 1
    for x in range(v.shape[0]):
        first_row, last_row = v[x, 0:1, :], v[x, last : last + 1, :]
        to_x[x : x + 1, :] = pick(even("sub"), last_row, first_row)
        to_zx[x : x + 1, :] = pick(even("sub"), first_row, last_row)


def edges_kernel(v, to_x, to_zx):
    put_edges(v, to_x, to_zx)


def faces_kernel(v, from_x, from_zx, to_core, to_y):
    planes, rows, _ = v.shape
    before, after = sides(from_x[...], from_zx[0:planes, :])
    for ref, swap in ((to_core, False), (to_y, True)):
        def choose(a, b):
            return pick(even("grp"), b, a) if swap else pick(even("grp"), a, b)

        ref[0:rows, :] = choose(v[planes - 1], v[0])
        ref[rows : rows + 1, :] = choose(before[planes - 1 :], before[0:1])
        ref[rows + 1 : rows + 2, :] = choose(after[planes - 1 :], after[0:1])


def fine_neighbours(groups, v, from_x, from_zx, from_core, from_y):
    planes, rows, _ = v.shape
    group = lax.axis_index("grp")
    before, after = sides(from_x[...], from_zx[0:planes, :])
    low = pick(even("grp"), from_y[0 : rows + 8, :], from_core[...])
    high = pick(even("grp"), from_core[...], from_y[0 : rows + 8, :])
    low = pick(group == 0, jnp.zeros_like(low), low)
    high = pick(group == groups - 1, jnp.zeros_like(high), high)
    faces = [neighbours(f[0:rows], f[rows : rows + 1], f[rows + 1 : rows + 2]) for f in (low, high)]
    inner = [neighbours(v[x], before[x : x + 1], after[x : x + 1]) for x in range(planes)]
    return [faces[0], *inner, faces[1]]


def sweep_kernel(groups, v, first, c, from_x, from_zx, from_core, from_y, out, to_x, to_zx):
    planes, rows, extent = v.shape
    near = fine_neighbours(groups, v, from_x, from_zx, from_core, from_y)
    for x in range(planes):
        for lanes in lane_tiles(extent):
            sums = outer_terms(near[x : x + 3], lambda k: c[k, x, :, lanes], lanes)
            out[x, :, lanes] = first[x, :, lanes] + (1.0 - WEIGHT) * v[x, :, lanes] - sums
    put_edges(out, to_x, to_zx)


def residual_kernel(
    groups, v, first, c, from_x, from_zx, from_core, from_y, center, iterate, to_x, to_zx, held
):
    planes, rows, extent = v.shape
    near = fine_neighbours(groups, v, from_x, from_zx, from_core, from_y)
    for x in range(0, planes, 2):
        for lanes in lane_tiles(extent):
            total = None
            for p in (x, x + 1):
                sums = outer_terms(near[p : p + 3], lambda k: c[k, p, :, lanes], lanes)
                part = first[p, :, lanes] - WEIGHT * v[p, :, lanes] - sums
                part = (1.0 / WEIGHT) * c[CENTER, p, :, lanes] * part
                total = part if total is None else total + part
            held[x // 2 * rows : (x // 2 + 1) * rows, lanes] = total
    total = (0.5 * WEIGHT) * paired_rows(paired_lanes(held[...]))
    half = rows // 2
    for x in range(planes // 2):
        for y in range(half):
            row = x * rows + 2 * y
            iterate[x, y : y + 1, :] = total[row : row + 1]
    iterate[...] = iterate[...] / center[...]
    for x in range(planes // 2):
        first_rows, last_rows = iterate[x, 0:3, :], iterate[x, half - 3 : half, :]
        to_x[4 * x : 4 * x + 3, :] = pick(even("sub"), last_rows, first_rows)
        to_zx[4 * x : 4 * x + 3, :] = pick(even("sub"), first_rows, last_rows)


def middle_faces_kernel(mine, from_x, from_zx, out):
    planes, half, _ = mine.shape
    before, after = sides(from_x[...], from_zx[0 : 4 * planes, :])
    for x in range(planes):
        row = x * ROWS
        out[row : row + 2, :] = before[4 * x + 1 : 4 * x + 3]
        out[row + 2 : row + 2 + half, :] = mine[x]
        out[row + 2 + half : row + ROWS, :] = after[4 * x : 4 * x + 2]
        extra = planes * ROWS + 2 * x
        out[extra : extra + 1, :] = before[4 * x : 4 * x + 1]
        out[extra + 1 : extra + 2, :] = after[4 * x + 2 : 4 * x + 3]


def coefficient_edges_kernel(c, to_x, to_zx):
    rows = c.shape[2]
    first, last = c[:, :, 0:2, :], c[:, :, rows - 2 : rows, :]
    to_x[...] = pick(even("sub"), last, first)
    to_zx[...] = pick(even("sub"), first, last)


def coefficient_scale_kernel(c, out):
    for x in range(c.shape[1]):
        out[:, x] = scaled(c[:, x])
        for k in range(27):
            out[k, x] = homed(k, out[k, x])


def scaled(c):
    center = c[CENTER : CENTER + 1]
    ratio = WEIGHT / jnp.where(center > 0.0, center, 1.0)
    index = lax.broadcasted_iota(jnp.int32, c.shape, 0)
    return c * jnp.where(index == CENTER, 1.0, ratio)


def coefficient_pack_kernel(known, *refs):
    coarse, (c, from_x, from_zx, _, __, early, late, whole) = refs[:known], refs[known:]
    _, planes, rows, extent = c.shape
    tiles = extent // LANES
    before, after = sides(from_x[...], from_zx[...])
    for x in range(planes):
        for l, lanes in enumerate(lane_tiles(extent)):
            row = (x * tiles + l) * ROWS
            whole[:, row : row + 2, :] = before[:, x, :, lanes]
            whole[:, row + 2 : row + 2 + rows, :] = c[:, x, :, lanes]
            whole[:, row + 2 + rows : row + ROWS, :] = after[:, x, :, lanes]
    row = planes * tiles * ROWS
    for t in range(0, row, ROWS):
        part = scaled(whole[:, t : t + ROWS, :])
        l = t // ROWS % tiles
        for k in range(27):
            ready = homed(k, part[k], l == 0, l == tiles - 1)
            whole[k, t : t + ROWS, :] = ready
            if k < EARLY:
                early[k, t : t + ROWS, :] = ready
            else:
                late[k - EARLY, t : t + ROWS, :] = ready
    for ref in coarse:
        for x in range(ref.shape[1]):
            for t in range(0, ref.shape[2], ROWS):
                whole[:, row : row + ROWS, :] = scaled(ref[:, x, t : t + ROWS, :])
                row += ROWS


def middle_kernel(
    groups, planes, packed, near_core, near_y, far_below, far_above, own, core, early, late, iterate, coarse, held
):
    extent = packed.shape[-1]
    tiles = extent // LANES
    half = ROWS - 4
    group = lax.axis_index("grp")
    window = 3 * planes

    below = pick(even("grp"), near_y[...], near_core[...])
    above = pick(even("grp"), near_core[...], near_y[...])
    blocks = {-2: far_below[...], -1: below, 0: packed[...], 1: above, 2: far_above[...]}
    for away in (-2, -1, 1, 2):
        inside = (group + away >= 0) & (group + away < groups)
        blocks[away] = pick(inside, blocks[away], jnp.zeros_like(blocks[away]))
    first, near = [], []
    for p in range(-1, window + 1):
        block, x = blocks[p // planes - 1], p % planes
        v, extra = block[x * ROWS : (x + 1) * ROWS], planes * ROWS + 2 * x
        first.append(v)
        near.append(neighbours(v, block[extra : extra + 1], block[extra + 1 : extra + 2]))

    def work(parts):
        def terms(forms, w, lanes):
            row = (w % planes * tiles + lanes.start // LANES) * ROWS
            return outer_terms(forms, lambda k: parts[w // planes](k)[row : row + ROWS, :], lanes)

        def swept(forms, field, w):
            sums = jnp.concatenate([terms(forms, w, lanes) for lanes in lane_tiles(extent)], axis=1)
            values = first[w + 1] + (1.0 - WEIGHT) * field - sums
            away = w // planes - 1
            if away:
                inside = (group + away >= 0) & (group + away < groups)
                values = pick(inside, values, jnp.zeros_like(values))
            return values

        low, high = planes - 2, 2 * planes + 2
        once = {w: swept(near[w : w + 3], first[w + 1], w) for w in range(low, high)}
        forms = {w: neighbours(v) for w, v in once.items()}
        low, high = low + 1, high - 1
        twice = {w: swept([forms[w + x] for x in (-1, 0, 1)], once[w], w) for w in range(low, high)}
        forms = {w: neighbours(v) for w, v in twice.items()}
        for x in range(planes):
            w = planes + x
            iterate[x] = twice[w][2 : 2 + half]
            for lanes in lane_tiles(extent):
                row = (x * tiles + lanes.start // LANES) * ROWS
                sums = terms([forms[w + i] for i in (-1, 0, 1)], w, lanes)
                rest = first[w + 1][:, lanes] - WEIGHT * twice[w][:, lanes] - sums
                held[x, :, lanes] = (1.0 / WEIGHT) * own[CENTER, row : row + ROWS, :] * rest

    def here(k):
        return own.at[k]

    def beside(k):
        return core.at[k]

    def across(k):
        return early.at[k] if k < EARLY else late.at[k - EARLY]

    @pl.when(even("grp"))
    def _():
        work((across, here, beside))

    @pl.when(jnp.logical_not(even("grp")))
    def _():
        work((beside, here, across))

    place_of = lax.broadcasted_iota(jnp.int32, (ROWS, extent // 2), 0)
    for x in range(planes // 2):
        total = 0.5 * paired_rows(paired_lanes(held[2 * x] + held[2 * x + 1]))
        value = pltpu.roll(total, ROWS - 2, 0)
        for i in range(1, half // 2):
            value = jnp.where(place_of == i, pltpu.roll(total, ROWS - 2 - i, 0), value)
        for device in range(coarse.shape[0]):
            coarse[device, x] = value[: half // 2]


def coarse_order_kernel(planes, rows, start, offsets, own, core, out):
    group = lax.axis_index("grp")
    row_of = lax.broadcasted_iota(jnp.int32, (rows, out.shape[-1]), 0)
    for ref, flip in ((own, 0), (core, 1)):
        for i, offset in enumerate(offsets):
            owner = jnp.bitwise_xor(group, offset ^ flip)
            for x in range(planes):
                row = start + (i * planes + x) * rows
                for k in range(27):
                    part = ref[k, row : row + rows, :]
                    if k // 3 % 3 != 1:
                        outside = 0 if k // 3 % 3 == 0 else rows - 1
                        part = jnp.where(row_of == outside, 0.0, part)
                    out[owner * planes + x, k] = homed(k, part)


def coarse_kernel(groups, planes, gathered, c, fine, middle, out, fine_out, middle_out, first, sems):
    kept = [
        pltpu.make_async_copy(fine, fine_out, sems.at[0]),
        pltpu.make_async_copy(middle, middle_out, sems.at[1]),
    ]
    for copy in kept:
        copy.start()
    total, rows, extent = first.shape
    subs = gathered.shape[0] // groups
    each = rows // subs
    for g in range(groups):
        for s in range(subs):
            for x in range(planes):
                first[g * planes + x, s * each : (s + 1) * each, :] = gathered[g * subs + s, x]
    for p in range(total):
        first[p] = WEIGHT * first[p] / c[p, CENTER]

    def sweep(_, field):
        near = [None, *map(neighbours, field), None]
        every = slice(0, extent)
        fresh = []
        for p in range(total):
            sums = outer_terms(near[p : p + 3], lambda k: c[p, k], every)
            fresh.append(first[p] + (1.0 - WEIGHT) * field[p] - sums)
        return tuple(fresh)

    field = lax.fori_loop(0, NB - 1, sweep, tuple(first[p] for p in range(total)), unroll=5)
    for p in range(total):
        first[p] = field[p]
    for x in range(planes):
        out[x] = first[lax.axis_index("grp") * planes + x]
    for copy in kept:
        copy.wait()


def after(value, *others):
    return lax.optimization_barrier((value, *others))[0]


def after_all(values, *others):
    return lax.optimization_barrier((*values, *others))[: len(values)]


def swaps(pairs):
    return [p for a, b in pairs for p in ((a, b), (b, a))]


def body(source, fine, middle, coarse):
    groups, subs = lax.axis_size("grp"), lax.axis_size("sub")
    _, planes, rows, extent = fine.shape
    _, middle_planes, middle_rows, middle_extent = middle.shape
    _, coarse_planes, coarse_rows, coarse_extent = coarse.shape

    x_pairs = swaps([(i, i + 1) for i in range(0, subs, 2)])
    zx_pairs = swaps(
        [(g * subs + i, g * subs + i + 1) for g in range(groups) for i in range(1, subs - 1, 2)]
        + [(g * subs + i, (g + 1) * subs + i) for g in range(0, groups, 2) for i in (0, subs - 1)]
    )
    core_pairs = swaps([(i, i + 1) for i in range(0, groups, 2)])
    y_pairs = swaps([(i, i + 1) for i in range(1, groups - 1, 2)])
    y_ring = y_pairs + [(groups - 1, 0), (0, groups - 1)]

    def along_sub(pair):
        to_x, to_zx = pair
        from_x = lax.ppermute(to_x, "sub", x_pairs)
        return from_x, lax.ppermute(to_zx, ("grp", "sub"), zx_pairs)

    def along_grp(v, halo):
        to_core, to_y = call(faces_kernel, [shape(rows + 8, extent), shape(2 * rows + 8, extent)], [v, *halo])
        from_core = lax.ppermute(to_core, "grp", core_pairs)
        from_y = lax.ppermute(to_y, "grp", y_ring)
        return (*halo, from_core, from_y)

    weights = call(coefficient_scale_kernel, shape(*fine.shape), [fine])
    v = WEIGHT * source / fine[CENTER]
    first = v
    to_x, to_zx = call(edges_kernel, [shape(planes, extent), shape(2 * planes, extent)], [v])

    def sweep(v, halo):
        v, *edges = call(
            functools.partial(sweep_kernel, groups),
            [shape(planes, rows, extent), shape(planes, extent), shape(2 * planes, extent)],
            [v, first, weights, *halo],
        )
        return v, along_sub(edges)

    edges_c = call(
        coefficient_edges_kernel,
        [shape(27, middle_planes, 2, middle_extent)] * 2,
        [middle],
    )
    halo = along_sub((to_x, to_zx))
    halo_c = along_sub(after_all(edges_c, *halo))
    halo = along_grp(after(v, weights, *edges_c), halo)
    known = {0: after(coarse, first)}
    bit = groups // 2
    while bit > 1:
        for offset in sorted(known):
            known[offset ^ bit] = lax.ppermute(known[offset], "grp", [(i, i ^ bit) for i in range(groups)])
        bit //= 2
    offsets = sorted(known)
    v, halo = sweep(v, halo)
    halo = along_grp(v, halo)
    start = middle_planes * (middle_extent // LANES) * ROWS
    early, late, own = call(
        functools.partial(coefficient_pack_kernel, len(known)),
        [shape(EARLY, start, LANES), shape(27 - EARLY, start, LANES), shape(27, start + len(known) * coarse_planes * coarse_rows, LANES)],
        [*(known[o] for o in offsets), middle, *halo_c, *halo[2:]],
    )
    core = lax.ppermute(own, "grp", core_pairs)
    early = lax.ppermute(early, "grp", y_ring)
    v, halo = sweep(v, halo)
    fine_iterate = v
    halo = along_grp(v, halo)
    late = lax.ppermute(after(late, *halo[2:]), "grp", y_ring)
    iterate, *edges = call(
        functools.partial(residual_kernel, groups),
        [shape(middle_planes, middle_rows, middle_extent)]
        + [shape(4 * middle_planes, middle_extent), shape(8 * middle_planes, middle_extent)],
        [v, first, weights, *halo, middle[CENTER]],
        [pltpu.VMEM((planes // 2 * rows, extent), jnp.float32)],
    )
    total = groups * coarse_planes
    ordered = call(
        functools.partial(coarse_order_kernel, coarse_planes, coarse_rows, start, offsets),
        shape(total, 27, coarse_rows, coarse_extent),
        [own, core],
    )
    packed = call(
        middle_faces_kernel,
        shape(middle_planes * ROWS + 8, middle_extent),
        [after(iterate, ordered), *along_sub(edges)],
    )
    near_core = lax.ppermute(packed, "grp", core_pairs)
    if groups == 4:
        far_below = far_above = lax.ppermute(packed, "grp", swaps([(0, 2), (1, 3)]))
        near_y = lax.ppermute(packed, "grp", y_ring)
    else:
        near_y = lax.ppermute(packed, "grp", y_pairs)
        up = [(i, i + 2) for i in range(groups - 2)]
        far_below = lax.ppermute(packed, "grp", up)
        far_above = lax.ppermute(packed, "grp", [(j, i) for i, j in up])
    middle_iterate, coarse_source = call(
        functools.partial(middle_kernel, groups, middle_planes),
        [
            shape(middle_planes, middle_rows, middle_extent),
            shape(groups * subs, coarse_planes, coarse_rows // subs, coarse_extent),
        ],
        [packed, near_core, near_y, far_below, far_above, own, core, early, late],
        [pltpu.VMEM((middle_planes, ROWS, middle_extent), jnp.float32)],
    )
    gathered = lax.all_to_all(coarse_source, ("grp", "sub"), 0, 0, tiled=True)
    vmem, hbm = pl.BlockSpec(memory_space=pltpu.VMEM), pl.BlockSpec(memory_space=pl.ANY)
    coarse_iterate, fine_iterate, middle_iterate = call(
        functools.partial(coarse_kernel, groups, coarse_planes),
        [
            shape(coarse_planes, coarse_rows, coarse_extent),
            shape(*fine_iterate.shape),
            shape(*middle_iterate.shape),
        ],
        [gathered, ordered, fine_iterate, middle_iterate],
        [
            pltpu.VMEM((total, coarse_rows, coarse_extent), jnp.float32),
            pltpu.SemaphoreType.DMA((2,)),
        ],
        out_specs=[vmem, hbm, hbm],
    )
    return fine_iterate, middle_iterate, coarse_iterate


def solution(mesh):
    placed = (
        P("grp", "sub", None),
        P(None, "grp", "sub", None),
        P(None, "grp", "sub", None),
        P(None, "grp", None, None),
    )
    return jax.shard_map(
        body,
        mesh=mesh,
        in_specs=placed,
        out_specs=(P("grp", "sub", None), P("grp", "sub", None), P("grp", None, None)),
        check_vma=False,
    )
```

```python
import functools

import jax
import jax.numpy as jnp
from jax import lax
from jax.experimental import pallas as pl
from jax.experimental.pallas import tpu as pltpu
from jax.sharding import PartitionSpec as P

NU0 = 3
NB = 16
WEIGHT = 0.8
CENTER = 13
EARLY = 19
LANES = 128
ROWS = 8


def shape(*dims):
    return jax.ShapeDtypeStruct(dims, jnp.float32)


def call(kernel, outs, args, scratch=(), out_specs=None):
    vmem = pl.BlockSpec(memory_space=pltpu.VMEM)
    return pl.pallas_call(
        kernel,
        out_shape=outs,
        in_specs=[vmem] * len(args),
        out_specs=out_specs or jax.tree.map(lambda _: vmem, outs),
        scratch_shapes=list(scratch),
        compiler_params=pltpu.CompilerParams(vmem_limit_bytes=12 << 20),
    )(*args)


def even(axis):
    return lax.rem(lax.axis_index(axis), 2) == 0


def pick(condition, a, b):
    return jnp.where(jnp.broadcast_to(condition, a.shape), a, b)


def sides(from_x, from_zx):
    sub, subs = lax.axis_index("sub"), lax.axis_size("sub")
    from_zx = pick((sub == 0) | (sub == subs - 1), jnp.zeros_like(from_zx), from_zx)
    return pick(even("sub"), from_zx, from_x), pick(even("sub"), from_x, from_zx)


def rolled(values):
    extent = values.shape[-1]
    return pltpu.roll(values, 1, 1), values, pltpu.roll(values, extent - 1, 1)


def homed(k, part, first=True, last=True):
    rows, extent = part.shape
    y, z = k // 3 % 3, k % 3
    lane = lax.broadcasted_iota(jnp.int32, part.shape, 1)
    if z == 0 and first:
        part = jnp.where(lane == 0, 0.0, part)
    if z == 2 and last:
        part = jnp.where(lane == extent - 1, 0.0, part)
    if y != 1:
        part = pltpu.roll(part, rows - 1 if y == 0 else 1, 0)
    return part


def neighbours(values, before=None, after=None):
    here = rolled(values)
    if before is None:
        return here, here, here
    row = lax.broadcasted_iota(jnp.int32, values.shape, 0)
    lower = [jnp.where(row == values.shape[0] - 1, b, h) for b, h in zip(rolled(before), here)]
    upper = [jnp.where(row == 0, a, h) for a, h in zip(rolled(after), here)]
    return lower, here, upper


def outer_terms(near, coefficient, lanes):
    sums = [None] * 3
    for x in range(3):
        for y in range(3):
            for z in range(3):
                k = 9 * x + 3 * y + z
                if k == CENTER or near[x] is None:
                    continue
                term = coefficient(k) * near[x][y][z][:, lanes]
                sums[y] = term if sums[y] is None else sums[y] + term
    rows = sums[1].shape[0]
    return sums[1] + (pltpu.roll(sums[0], 1, 0) + pltpu.roll(sums[2], rows - 1, 0))


def lane_tiles(extent):
    return [slice(l, l + LANES) for l in range(0, extent, LANES)]


def paired_lanes(values):
    rows, extent = values.shape
    row = lax.broadcasted_iota(jnp.int32, (extent, extent // 2), 0)
    column = lax.broadcasted_iota(jnp.int32, (extent, extent // 2), 1)
    pairs = jnp.where(lax.shift_right_logical(row, 1) == column, 1.0, 0.0).astype(jnp.bfloat16)
    parts = []
    for _ in range(3):
        part = values.astype(jnp.bfloat16).astype(jnp.float32)
        parts.append(part)
        values = values - part
    if 3 * rows % 16:
        parts.append(jnp.zeros_like(values))
    stacked = jnp.concatenate(parts, axis=0).astype(jnp.bfloat16)
    sums = lax.dot_general(stacked, pairs, (((1,), (0,)), ((), ())), preferred_element_type=jnp.float32)
    return sums[:rows] + (sums[rows : 2 * rows] + sums[2 * rows : 3 * rows])


def paired_rows(values):
    return values + pltpu.roll(values, values.shape[0] - 1, 0)


def put_edges(v, to_x, to_zx):
    last = v.shape[1] - 1
    for x in range(v.shape[0]):
        first_row, last_row = v[x, 0:1, :], v[x, last : last + 1, :]
        to_x[x : x + 1, :] = pick(even("sub"), last_row, first_row)
        to_zx[x : x + 1, :] = pick(even("sub"), first_row, last_row)


def edges_kernel(v, to_x, to_zx):
    put_edges(v, to_x, to_zx)


def faces_kernel(v, from_x, from_zx, to_core, to_y):
    planes, rows, _ = v.shape
    before, after = sides(from_x[...], from_zx[0:planes, :])
    for ref, swap in ((to_core, False), (to_y, True)):
        def choose(a, b):
            return pick(even("grp"), b, a) if swap else pick(even("grp"), a, b)

        ref[0:rows, :] = choose(v[planes - 1], v[0])
        ref[rows : rows + 1, :] = choose(before[planes - 1 :], before[0:1])
        ref[rows + 1 : rows + 2, :] = choose(after[planes - 1 :], after[0:1])


def fine_neighbours(groups, v, from_x, from_zx, from_core, from_y):
    planes, rows, _ = v.shape
    group = lax.axis_index("grp")
    before, after = sides(from_x[...], from_zx[0:planes, :])
    low = pick(even("grp"), from_y[0 : rows + 8, :], from_core[...])
    high = pick(even("grp"), from_core[...], from_y[0 : rows + 8, :])
    low = pick(group == 0, jnp.zeros_like(low), low)
    high = pick(group == groups - 1, jnp.zeros_like(high), high)
    faces = [neighbours(f[0:rows], f[rows : rows + 1], f[rows + 1 : rows + 2]) for f in (low, high)]
    inner = [neighbours(v[x], before[x : x + 1], after[x : x + 1]) for x in range(planes)]
    return [faces[0], *inner, faces[1]]


def sweep_kernel(groups, v, first, c, from_x, from_zx, from_core, from_y, out, to_x, to_zx):
    planes, rows, extent = v.shape
    near = fine_neighbours(groups, v, from_x, from_zx, from_core, from_y)
    for x in range(planes):
        for lanes in lane_tiles(extent):
            sums = outer_terms(near[x : x + 3], lambda k: c[k, x, :, lanes], lanes)
            out[x, :, lanes] = first[x, :, lanes] + (1.0 - WEIGHT) * v[x, :, lanes] - sums
    put_edges(out, to_x, to_zx)


def residual_kernel(
    groups, v, first, c, from_x, from_zx, from_core, from_y, center, iterate, to_x, to_zx, held
):
    planes, rows, extent = v.shape
    near = fine_neighbours(groups, v, from_x, from_zx, from_core, from_y)
    for x in range(0, planes, 2):
        for lanes in lane_tiles(extent):
            total = None
            for p in (x, x + 1):
                sums = outer_terms(near[p : p + 3], lambda k: c[k, p, :, lanes], lanes)
                part = first[p, :, lanes] - WEIGHT * v[p, :, lanes] - sums
                part = (1.0 / WEIGHT) * c[CENTER, p, :, lanes] * part
                total = part if total is None else total + part
            held[x // 2 * rows : (x // 2 + 1) * rows, lanes] = total
    total = (0.5 * WEIGHT) * paired_rows(paired_lanes(held[...]))
    half = rows // 2
    for x in range(planes // 2):
        for y in range(half):
            row = x * rows + 2 * y
            iterate[x, y : y + 1, :] = total[row : row + 1]
    iterate[...] = iterate[...] / center[...]
    for x in range(planes // 2):
        first_rows, last_rows = iterate[x, 0:3, :], iterate[x, half - 3 : half, :]
        to_x[4 * x : 4 * x + 3, :] = pick(even("sub"), last_rows, first_rows)
        to_zx[4 * x : 4 * x + 3, :] = pick(even("sub"), first_rows, last_rows)


def middle_faces_kernel(mine, from_x, from_zx, out):
    planes, half, _ = mine.shape
    before, after = sides(from_x[...], from_zx[0 : 4 * planes, :])
    for x in range(planes):
        row = x * ROWS
        out[row : row + 2, :] = before[4 * x + 1 : 4 * x + 3]
        out[row + 2 : row + 2 + half, :] = mine[x]
        out[row + 2 + half : row + ROWS, :] = after[4 * x : 4 * x + 2]
        extra = planes * ROWS + 2 * x
        out[extra : extra + 1, :] = before[4 * x : 4 * x + 1]
        out[extra + 1 : extra + 2, :] = after[4 * x + 2 : 4 * x + 3]


def coefficient_edges_kernel(c, to_x, to_zx):
    rows = c.shape[2]
    first, last = c[:, :, 0:2, :], c[:, :, rows - 2 : rows, :]
    to_x[...] = pick(even("sub"), last, first)
    to_zx[...] = pick(even("sub"), first, last)


def coefficient_scale_kernel(c, out):
    for x in range(c.shape[1]):
        out[:, x] = scaled(c[:, x])
        for k in range(27):
            out[k, x] = homed(k, out[k, x])


def scaled(c):
    center = c[CENTER : CENTER + 1]
    ratio = WEIGHT / jnp.where(center > 0.0, center, 1.0)
    index = lax.broadcasted_iota(jnp.int32, c.shape, 0)
    return c * jnp.where(index == CENTER, 1.0, ratio)


def coefficient_pack_kernel(known, *refs):
    coarse, (c, from_x, from_zx, _, __, early, late, whole) = refs[:known], refs[known:]
    _, planes, rows, extent = c.shape
    tiles = extent // LANES
    before, after = sides(from_x[...], from_zx[...])
    for x in range(planes):
        for l, lanes in enumerate(lane_tiles(extent)):
            row = (x * tiles + l) * ROWS
            whole[:, row : row + 2, :] = before[:, x, :, lanes]
            whole[:, row + 2 : row + 2 + rows, :] = c[:, x, :, lanes]
            whole[:, row + 2 + rows : row + ROWS, :] = after[:, x, :, lanes]
    row = planes * tiles * ROWS
    for t in range(0, row, ROWS):
        part = scaled(whole[:, t : t + ROWS, :])
        l = t // ROWS % tiles
        for k in range(27):
            ready = homed(k, part[k], l == 0, l == tiles - 1)
            whole[k, t : t + ROWS, :] = ready
            if k < EARLY:
                early[k, t : t + ROWS, :] = ready
            else:
                late[k - EARLY, t : t + ROWS, :] = ready
    for ref in coarse:
        for x in range(ref.shape[1]):
            for t in range(0, ref.shape[2], ROWS):
                whole[:, row : row + ROWS, :] = scaled(ref[:, x, t : t + ROWS, :])
                row += ROWS


def middle_kernel(
    groups, planes, packed, near_core, near_y, far_below, far_above, own, core, early, late, iterate, coarse, held
):
    extent = packed.shape[-1]
    tiles = extent // LANES
    half = ROWS - 4
    group = lax.axis_index("grp")
    window = 3 * planes

    below = pick(even("grp"), near_y[...], near_core[...])
    above = pick(even("grp"), near_core[...], near_y[...])
    blocks = {-2: far_below[...], -1: below, 0: packed[...], 1: above, 2: far_above[...]}
    for away in (-2, -1, 1, 2):
        inside = (group + away >= 0) & (group + away < groups)
        blocks[away] = pick(inside, blocks[away], jnp.zeros_like(blocks[away]))
    first, near = [], []
    for p in range(-1, window + 1):
        block, x = blocks[p // planes - 1], p % planes
        v, extra = block[x * ROWS : (x + 1) * ROWS], planes * ROWS + 2 * x
        first.append(v)
        near.append(neighbours(v, block[extra : extra + 1], block[extra + 1 : extra + 2]))

    def work(parts):
        def terms(forms, w, lanes):
            row = (w % planes * tiles + lanes.start // LANES) * ROWS
            return outer_terms(forms, lambda k: parts[w // planes](k)[row : row + ROWS, :], lanes)

        def swept(forms, field, w):
            sums = jnp.concatenate([terms(forms, w, lanes) for lanes in lane_tiles(extent)], axis=1)
            values = first[w + 1] + (1.0 - WEIGHT) * field - sums
            away = w // planes - 1
            if away:
                inside = (group + away >= 0) & (group + away < groups)
                values = pick(inside, values, jnp.zeros_like(values))
            return values

        low, high = planes - 2, 2 * planes + 2
        once = {w: swept(near[w : w + 3], first[w + 1], w) for w in range(low, high)}
        forms = {w: neighbours(v) for w, v in once.items()}
        low, high = low + 1, high - 1
        twice = {w: swept([forms[w + x] for x in (-1, 0, 1)], once[w], w) for w in range(low, high)}
        forms = {w: neighbours(v) for w, v in twice.items()}
        for x in range(planes):
            w = planes + x
            iterate[x] = twice[w][2 : 2 + half]
            for lanes in lane_tiles(extent):
                row = (x * tiles + lanes.start // LANES) * ROWS
                sums = terms([forms[w + i] for i in (-1, 0, 1)], w, lanes)
                rest = first[w + 1][:, lanes] - WEIGHT * twice[w][:, lanes] - sums
                held[x, :, lanes] = (1.0 / WEIGHT) * own[CENTER, row : row + ROWS, :] * rest

    def here(k):
        return own.at[k]

    def beside(k):
        return core.at[k]

    def across(k):
        return early.at[k] if k < EARLY else late.at[k - EARLY]

    @pl.when(even("grp"))
    def _():
        work((across, here, beside))

    @pl.when(jnp.logical_not(even("grp")))
    def _():
        work((beside, here, across))

    place_of = lax.broadcasted_iota(jnp.int32, (ROWS, extent // 2), 0)
    for x in range(planes // 2):
        total = 0.5 * paired_rows(paired_lanes(held[2 * x] + held[2 * x + 1]))
        value = pltpu.roll(total, ROWS - 2, 0)
        for i in range(1, half // 2):
            value = jnp.where(place_of == i, pltpu.roll(total, ROWS - 2 - i, 0), value)
        for device in range(coarse.shape[0]):
            coarse[device, x] = value[: half // 2]


def coarse_order_kernel(planes, rows, start, offsets, own, core, out):
    group = lax.axis_index("grp")
    row_of = lax.broadcasted_iota(jnp.int32, (rows, out.shape[-1]), 0)
    for ref, flip in ((own, 0), (core, 1)):
        for i, offset in enumerate(offsets):
            owner = jnp.bitwise_xor(group, offset ^ flip)
            for x in range(planes):
                row = start + (i * planes + x) * rows
                for k in range(27):
                    part = ref[k, row : row + rows, :]
                    if k // 3 % 3 != 1:
                        outside = 0 if k // 3 % 3 == 0 else rows - 1
                        part = jnp.where(row_of == outside, 0.0, part)
                    out[owner * planes + x, k] = homed(k, part)


def coarse_kernel(groups, planes, gathered, c, fine, middle, out, fine_out, middle_out, first, sems):
    kept = [
        pltpu.make_async_copy(fine, fine_out, sems.at[0]),
        pltpu.make_async_copy(middle, middle_out, sems.at[1]),
    ]
    for copy in kept:
        copy.start()
    total, rows, extent = first.shape
    subs = gathered.shape[0] // groups
    each = rows // subs
    for g in range(groups):
        for s in range(subs):
            for x in range(planes):
                first[g * planes + x, s * each : (s + 1) * each, :] = gathered[g * subs + s, x]
    for p in range(total):
        first[p] = WEIGHT * first[p] / c[p, CENTER]

    def sweep(_, field):
        near = [None, *map(neighbours, field), None]
        every = slice(0, extent)
        fresh = []
        for p in range(total):
            sums = outer_terms(near[p : p + 3], lambda k: c[p, k], every)
            fresh.append(first[p] + (1.0 - WEIGHT) * field[p] - sums)
        return tuple(fresh)

    field = lax.fori_loop(0, NB - 1, sweep, tuple(first[p] for p in range(total)), unroll=5)
    for p in range(total):
        first[p] = field[p]
    for x in range(planes):
        out[x] = first[lax.axis_index("grp") * planes + x]
    for copy in kept:
        copy.wait()


def after(value, *others):
    return lax.optimization_barrier((value, *others))[0]


def after_all(values, *others):
    return lax.optimization_barrier((*values, *others))[: len(values)]


def swaps(pairs):
    return [p for a, b in pairs for p in ((a, b), (b, a))]


def body(source, fine, middle, coarse):
    groups, subs = lax.axis_size("grp"), lax.axis_size("sub")
    _, planes, rows, extent = fine.shape
    _, middle_planes, middle_rows, middle_extent = middle.shape
    _, coarse_planes, coarse_rows, coarse_extent = coarse.shape

    x_pairs = swaps([(i, i + 1) for i in range(0, subs, 2)])
    zx_pairs = swaps(
        [(g * subs + i, g * subs + i + 1) for g in range(groups) for i in range(1, subs - 1, 2)]
        + [(g * subs + i, (g + 1) * subs + i) for g in range(0, groups, 2) for i in (0, subs - 1)]
    )
    core_pairs = swaps([(i, i + 1) for i in range(0, groups, 2)])
    y_pairs = swaps([(i, i + 1) for i in range(1, groups - 1, 2)])
    y_ring = y_pairs + [(groups - 1, 0), (0, groups - 1)]

    def along_sub(pair):
        to_x, to_zx = pair
        from_x = lax.ppermute(to_x, "sub", x_pairs)
        return from_x, lax.ppermute(to_zx, ("grp", "sub"), zx_pairs)

    def along_grp(v, halo):
        to_core, to_y = call(faces_kernel, [shape(rows + 8, extent), shape(2 * rows + 8, extent)], [v, *halo])
        from_core = lax.ppermute(to_core, "grp", core_pairs)
        from_y = lax.ppermute(to_y, "grp", y_ring)
        return (*halo, from_core, from_y)

    weights = call(coefficient_scale_kernel, shape(*fine.shape), [fine])
    v = WEIGHT * source / fine[CENTER]
    first = v
    to_x, to_zx = call(edges_kernel, [shape(planes, extent), shape(2 * planes, extent)], [v])

    def sweep(v, halo):
        v, *edges = call(
            functools.partial(sweep_kernel, groups),
            [shape(planes, rows, extent), shape(planes, extent), shape(2 * planes, extent)],
            [v, first, weights, *halo],
        )
        return v, along_sub(edges)

    edges_c = call(
        coefficient_edges_kernel,
        [shape(27, middle_planes, 2, middle_extent)] * 2,
        [middle],
    )
    halo = along_sub((to_x, to_zx))
    halo_c = along_sub(after_all(edges_c, *halo))
    halo = along_grp(after(v, weights, *edges_c), halo)
    known = {0: after(coarse, first)}
    bit = groups // 2
    while bit > 1:
        for offset in sorted(known):
            known[offset ^ bit] = lax.ppermute(known[offset], "grp", [(i, i ^ bit) for i in range(groups)])
        bit //= 2
    offsets = sorted(known)
    v, halo = sweep(v, halo)
    halo = along_grp(v, halo)
    start = middle_planes * (middle_extent // LANES) * ROWS
    early, late, own = call(
        functools.partial(coefficient_pack_kernel, len(known)),
        [shape(EARLY, start, LANES), shape(27 - EARLY, start, LANES), shape(27, start + len(known) * coarse_planes * coarse_rows, LANES)],
        [*(known[o] for o in offsets), middle, *halo_c, *halo[2:]],
    )
    core = lax.ppermute(own, "grp", core_pairs)
    early = lax.ppermute(early, "grp", y_ring)
    v, halo = sweep(v, halo)
    fine_iterate = v
    halo = along_grp(v, halo)
    late = lax.ppermute(after(late, *halo[2:]), "grp", y_ring)
    iterate, *edges = call(
        functools.partial(residual_kernel, groups),
        [shape(middle_planes, middle_rows, middle_extent)]
        + [shape(4 * middle_planes, middle_extent), shape(8 * middle_planes, middle_extent)],
        [v, first, weights, *halo, middle[CENTER]],
        [pltpu.VMEM((planes // 2 * rows, extent), jnp.float32)],
    )
    total = groups * coarse_planes
    ordered = call(
        functools.partial(coarse_order_kernel, coarse_planes, coarse_rows, start, offsets),
        shape(total, 27, coarse_rows, coarse_extent),
        [own, core],
    )
    packed = call(
        middle_faces_kernel,
        shape(middle_planes * ROWS + 8, middle_extent),
        [after(iterate, ordered), *along_sub(edges)],
    )
    near_core = lax.ppermute(packed, "grp", core_pairs)
    if groups == 4:
        far_below = far_above = lax.ppermute(packed, "grp", swaps([(0, 2), (1, 3)]))
        near_y = lax.ppermute(packed, "grp", y_ring)
    else:
        near_y = lax.ppermute(packed, "grp", y_pairs)
        up = [(i, i + 2) for i in range(groups - 2)]
        far_below = lax.ppermute(packed, "grp", up)
        far_above = lax.ppermute(packed, "grp", [(j, i) for i, j in up])
    middle_iterate, coarse_source = call(
        functools.partial(middle_kernel, groups, middle_planes),
        [
            shape(middle_planes, middle_rows, middle_extent),
            shape(groups * subs, coarse_planes, coarse_rows // subs, coarse_extent),
        ],
        [packed, near_core, near_y, far_below, far_above, own, core, early, late],
        [pltpu.VMEM((middle_planes, ROWS, middle_extent), jnp.float32)],
    )
    gathered = lax.all_to_all(coarse_source, ("grp", "sub"), 0, 0, tiled=True)
    vmem, hbm = pl.BlockSpec(memory_space=pltpu.VMEM), pl.BlockSpec(memory_space=pl.ANY)
    coarse_iterate, fine_iterate, middle_iterate = call(
        functools.partial(coarse_kernel, groups, coarse_planes),
        [
            shape(coarse_planes, coarse_rows, coarse_extent),
            shape(*fine_iterate.shape),
            shape(*middle_iterate.shape),
        ],
        [gathered, ordered, fine_iterate, middle_iterate],
        [
            pltpu.VMEM((total, coarse_rows, coarse_extent), jnp.float32),
            pltpu.SemaphoreType.DMA((2,)),
        ],
        out_specs=[vmem, hbm, hbm],
    )
    return fine_iterate, middle_iterate, coarse_iterate


def solution(mesh):
    placed = (
        P("grp", "sub", None),
        P(None, "grp", "sub", None),
        P(None, "grp", "sub", None),
        P(None, "grp", None, None),
    )
    return jax.shard_map(
        body,
        mesh=mesh,
        in_specs=placed,
        out_specs=(P("grp", "sub", None), P("grp", "sub", None), P("grp", None, None)),
        check_vma=False,
    )
```

```python
import functools

import jax
import jax.numpy as jnp
from jax import lax
from jax.experimental import pallas as pl
from jax.experimental.pallas import tpu as pltpu
from jax.sharding import PartitionSpec as P

NU0 = 3
NB = 16
WEIGHT = 0.8
CENTER = 13
EARLY = 19
LANES = 128
ROWS = 8


def shape(*dims):
    return jax.ShapeDtypeStruct(dims, jnp.float32)


def call(kernel, outs, args, scratch=(), out_specs=None):
    vmem = pl.BlockSpec(memory_space=pltpu.VMEM)
    return pl.pallas_call(
        kernel,
        out_shape=outs,
        in_specs=[vmem] * len(args),
        out_specs=out_specs or jax.tree.map(lambda _: vmem, outs),
        scratch_shapes=list(scratch),
        compiler_params=pltpu.CompilerParams(vmem_limit_bytes=12 << 20),
    )(*args)


def even(axis):
    return lax.rem(lax.axis_index(axis), 2) == 0


def pick(condition, a, b):
    return jnp.where(jnp.broadcast_to(condition, a.shape), a, b)


def sides(from_x, from_zx):
    sub, subs = lax.axis_index("sub"), lax.axis_size("sub")
    from_zx = pick((sub == 0) | (sub == subs - 1), jnp.zeros_like(from_zx), from_zx)
    return pick(even("sub"), from_zx, from_x), pick(even("sub"), from_x, from_zx)


def rolled(values):
    extent = values.shape[-1]
    return pltpu.roll(values, 1, 1), values, pltpu.roll(values, extent - 1, 1)


def homed(k, part, first=True, last=True):
    rows, extent = part.shape
    y, z = k // 3 % 3, k % 3
    lane = lax.broadcasted_iota(jnp.int32, part.shape, 1)
    if z == 0 and first:
        part = jnp.where(lane == 0, 0.0, part)
    if z == 2 and last:
        part = jnp.where(lane == extent - 1, 0.0, part)
    if y != 1:
        part = pltpu.roll(part, rows - 1 if y == 0 else 1, 0)
    return part


def neighbours(values, before=None, after=None):
    here = rolled(values)
    if before is None:
        return here, here, here
    row = lax.broadcasted_iota(jnp.int32, values.shape, 0)
    lower = [jnp.where(row == values.shape[0] - 1, b, h) for b, h in zip(rolled(before), here)]
    upper = [jnp.where(row == 0, a, h) for a, h in zip(rolled(after), here)]
    return lower, here, upper


def outer_terms(near, coefficient, lanes):
    sums = [None] * 3
    for x in range(3):
        for y in range(3):
            for z in range(3):
                k = 9 * x + 3 * y + z
                if k == CENTER or near[x] is None:
                    continue
                term = coefficient(k) * near[x][y][z][:, lanes]
                sums[y] = term if sums[y] is None else sums[y] + term
    rows = sums[1].shape[0]
    return sums[1] + (pltpu.roll(sums[0], 1, 0) + pltpu.roll(sums[2], rows - 1, 0))


def lane_tiles(extent):
    return [slice(l, l + LANES) for l in range(0, extent, LANES)]


def paired_lanes(values):
    rows, extent = values.shape
    row = lax.broadcasted_iota(jnp.int32, (extent, extent // 2), 0)
    column = lax.broadcasted_iota(jnp.int32, (extent, extent // 2), 1)
    pairs = jnp.where(lax.shift_right_logical(row, 1) == column, 1.0, 0.0).astype(jnp.bfloat16)
    parts = []
    for _ in range(3):
        part = values.astype(jnp.bfloat16).astype(jnp.float32)
        parts.append(part)
        values = values - part
    if 3 * rows % 16:
        parts.append(jnp.zeros_like(values))
    stacked = jnp.concatenate(parts, axis=0).astype(jnp.bfloat16)
    sums = lax.dot_general(stacked, pairs, (((1,), (0,)), ((), ())), preferred_element_type=jnp.float32)
    return sums[:rows] + (sums[rows : 2 * rows] + sums[2 * rows : 3 * rows])


def paired_rows(values):
    return values + pltpu.roll(values, values.shape[0] - 1, 0)


def put_edges(v, to_x, to_zx):
    last = v.shape[1] - 1
    for x in range(v.shape[0]):
        first_row, last_row = v[x, 0:1, :], v[x, last : last + 1, :]
        to_x[x : x + 1, :] = pick(even("sub"), last_row, first_row)
        to_zx[x : x + 1, :] = pick(even("sub"), first_row, last_row)


def edges_kernel(v, to_x, to_zx):
    put_edges(v, to_x, to_zx)


def faces_kernel(v, from_x, from_zx, to_core, to_y):
    planes, rows, _ = v.shape
    before, after = sides(from_x[...], from_zx[0:planes, :])
    for ref, swap in ((to_core, False), (to_y, True)):
        def choose(a, b):
            return pick(even("grp"), b, a) if swap else pick(even("grp"), a, b)

        ref[0:rows, :] = choose(v[planes - 1], v[0])
        ref[rows : rows + 1, :] = choose(before[planes - 1 :], before[0:1])
        ref[rows + 1 : rows + 2, :] = choose(after[planes - 1 :], after[0:1])


def fine_neighbours(groups, v, from_x, from_zx, from_core, from_y):
    planes, rows, _ = v.shape
    group = lax.axis_index("grp")
    before, after = sides(from_x[...], from_zx[0:planes, :])
    low = pick(even("grp"), from_y[0 : rows + 8, :], from_core[...])
    high = pick(even("grp"), from_core[...], from_y[0 : rows + 8, :])
    low = pick(group == 0, jnp.zeros_like(low), low)
    high = pick(group == groups - 1, jnp.zeros_like(high), high)
    faces = [neighbours(f[0:rows], f[rows : rows + 1], f[rows + 1 : rows + 2]) for f in (low, high)]
    inner = [neighbours(v[x], before[x : x + 1], after[x : x + 1]) for x in range(planes)]
    return [faces[0], *inner, faces[1]]


def sweep_kernel(groups, v, first, c, from_x, from_zx, from_core, from_y, out, to_x, to_zx):
    planes, rows, extent = v.shape
    near = fine_neighbours(groups, v, from_x, from_zx, from_core, from_y)
    for x in range(planes):
        for lanes in lane_tiles(extent):
            sums = outer_terms(near[x : x + 3], lambda k: c[k, x, :, lanes], lanes)
            out[x, :, lanes] = first[x, :, lanes] + (1.0 - WEIGHT) * v[x, :, lanes] - sums
    put_edges(out, to_x, to_zx)


def residual_kernel(
    groups, v, first, c, from_x, from_zx, from_core, from_y, center, iterate, to_x, to_zx, held
):
    planes, rows, extent = v.shape
    near = fine_neighbours(groups, v, from_x, from_zx, from_core, from_y)
    for x in range(0, planes, 2):
        for lanes in lane_tiles(extent):
            total = None
            for p in (x, x + 1):
                sums = outer_terms(near[p : p + 3], lambda k: c[k, p, :, lanes], lanes)
                part = first[p, :, lanes] - WEIGHT * v[p, :, lanes] - sums
                part = (1.0 / WEIGHT) * c[CENTER, p, :, lanes] * part
                total = part if total is None else total + part
            held[x // 2 * rows : (x // 2 + 1) * rows, lanes] = total
    total = (0.5 * WEIGHT) * paired_rows(paired_lanes(held[...]))
    half = rows // 2
    for x in range(planes // 2):
        for y in range(half):
            row = x * rows + 2 * y
            iterate[x, y : y + 1, :] = total[row : row + 1]
    iterate[...] = iterate[...] / center[...]
    for x in range(planes // 2):
        first_rows, last_rows = iterate[x, 0:3, :], iterate[x, half - 3 : half, :]
        to_x[4 * x : 4 * x + 3, :] = pick(even("sub"), last_rows, first_rows)
        to_zx[4 * x : 4 * x + 3, :] = pick(even("sub"), first_rows, last_rows)


def middle_faces_kernel(mine, from_x, from_zx, out):
    planes, half, _ = mine.shape
    before, after = sides(from_x[...], from_zx[0 : 4 * planes, :])
    for x in range(planes):
        row = x * ROWS
        out[row : row + 2, :] = before[4 * x + 1 : 4 * x + 3]
        out[row + 2 : row + 2 + half, :] = mine[x]
        out[row + 2 + half : row + ROWS, :] = after[4 * x : 4 * x + 2]
        extra = planes * ROWS + 2 * x
        out[extra : extra + 1, :] = before[4 * x : 4 * x + 1]
        out[extra + 1 : extra + 2, :] = after[4 * x + 2 : 4 * x + 3]


def coefficient_edges_kernel(c, to_x, to_zx):
    rows = c.shape[2]
    first, last = c[:, :, 0:2, :], c[:, :, rows - 2 : rows, :]
    to_x[...] = pick(even("sub"), last, first)
    to_zx[...] = pick(even("sub"), first, last)


def coefficient_scale_kernel(c, out):
    for x in range(c.shape[1]):
        out[:, x] = scaled(c[:, x])
        for k in range(27):
            out[k, x] = homed(k, out[k, x])


def scaled(c):
    center = c[CENTER : CENTER + 1]
    ratio = WEIGHT / jnp.where(center > 0.0, center, 1.0)
    index = lax.broadcasted_iota(jnp.int32, c.shape, 0)
    return c * jnp.where(index == CENTER, 1.0, ratio)


def coefficient_pack_kernel(known, *refs):
    coarse, (c, from_x, from_zx, _, __, early, late, whole) = refs[:known], refs[known:]
    _, planes, rows, extent = c.shape
    tiles = extent // LANES
    before, after = sides(from_x[...], from_zx[...])
    for x in range(planes):
        for l, lanes in enumerate(lane_tiles(extent)):
            row = (x * tiles + l) * ROWS
            whole[:, row : row + 2, :] = before[:, x, :, lanes]
            whole[:, row + 2 : row + 2 + rows, :] = c[:, x, :, lanes]
            whole[:, row + 2 + rows : row + ROWS, :] = after[:, x, :, lanes]
    row = planes * tiles * ROWS
    for t in range(0, row, ROWS):
        part = scaled(whole[:, t : t + ROWS, :])
        l = t // ROWS % tiles
        for k in range(27):
            ready = homed(k, part[k], l == 0, l == tiles - 1)
            whole[k, t : t + ROWS, :] = ready
            if k < EARLY:
                early[k, t : t + ROWS, :] = ready
            else:
                late[k - EARLY, t : t + ROWS, :] = ready
    for ref in coarse:
        for x in range(ref.shape[1]):
            for t in range(0, ref.shape[2], ROWS):
                whole[:, row : row + ROWS, :] = scaled(ref[:, x, t : t + ROWS, :])
                row += ROWS


def middle_kernel(
    groups, planes, packed, near_core, near_y, far_below, far_above, own, core, early, late, iterate, coarse, held
):
    extent = packed.shape[-1]
    tiles = extent // LANES
    half = ROWS - 4
    group = lax.axis_index("grp")
    window = 3 * planes

    below = pick(even("grp"), near_y[...], near_core[...])
    above = pick(even("grp"), near_core[...], near_y[...])
    blocks = {-2: far_below[...], -1: below, 0: packed[...], 1: above, 2: far_above[...]}
    for away in (-2, -1, 1, 2):
        inside = (group + away >= 0) & (group + away < groups)
        blocks[away] = pick(inside, blocks[away], jnp.zeros_like(blocks[away]))
    first, near = [], []
    for p in range(-1, window + 1):
        block, x = blocks[p // planes - 1], p % planes
        v, extra = block[x * ROWS : (x + 1) * ROWS], planes * ROWS + 2 * x
        first.append(v)
        near.append(neighbours(v, block[extra : extra + 1], block[extra + 1 : extra + 2]))

    def work(parts):
        def terms(forms, w, lanes):
            row = (w % planes * tiles + lanes.start // LANES) * ROWS
            return outer_terms(forms, lambda k: parts[w // planes](k)[row : row + ROWS, :], lanes)

        def swept(forms, field, w):
            sums = jnp.concatenate([terms(forms, w, lanes) for lanes in lane_tiles(extent)], axis=1)
            values = first[w + 1] + (1.0 - WEIGHT) * field - sums
            away = w // planes - 1
            if away:
                inside = (group + away >= 0) & (group + away < groups)
                values = pick(inside, values, jnp.zeros_like(values))
            return values

        low, high = planes - 2, 2 * planes + 2
        once = {w: swept(near[w : w + 3], first[w + 1], w) for w in range(low, high)}
        forms = {w: neighbours(v) for w, v in once.items()}
        low, high = low + 1, high - 1
        twice = {w: swept([forms[w + x] for x in (-1, 0, 1)], once[w], w) for w in range(low, high)}
        forms = {w: neighbours(v) for w, v in twice.items()}
        for x in range(planes):
            w = planes + x
            iterate[x] = twice[w][2 : 2 + half]
            for lanes in lane_tiles(extent):
                row = (x * tiles + lanes.start // LANES) * ROWS
                sums = terms([forms[w + i] for i in (-1, 0, 1)], w, lanes)
                rest = first[w + 1][:, lanes] - WEIGHT * twice[w][:, lanes] - sums
                held[x, :, lanes] = (1.0 / WEIGHT) * own[CENTER, row : row + ROWS, :] * rest

    def here(k):
        return own.at[k]

    def beside(k):
        return core.at[k]

    def across(k):
        return early.at[k] if k < EARLY else late.at[k - EARLY]

    @pl.when(even("grp"))
    def _():
        work((across, here, beside))

    @pl.when(jnp.logical_not(even("grp")))
    def _():
        work((beside, here, across))

    place_of = lax.broadcasted_iota(jnp.int32, (ROWS, extent // 2), 0)
    for x in range(planes // 2):
        total = 0.5 * paired_rows(paired_lanes(held[2 * x] + held[2 * x + 1]))
        value = pltpu.roll(total, ROWS - 2, 0)
        for i in range(1, half // 2):
            value = jnp.where(place_of == i, pltpu.roll(total, ROWS - 2 - i, 0), value)
        for device in range(coarse.shape[0]):
            coarse[device, x] = value[: half // 2]


def coarse_order_kernel(planes, rows, start, offsets, own, core, out):
    group = lax.axis_index("grp")
    row_of = lax.broadcasted_iota(jnp.int32, (rows, out.shape[-1]), 0)
    for ref, flip in ((own, 0), (core, 1)):
        for i, offset in enumerate(offsets):
            owner = jnp.bitwise_xor(group, offset ^ flip)
            for x in range(planes):
                row = start + (i * planes + x) * rows
                for k in range(27):
                    part = ref[k, row : row + rows, :]
                    if k // 3 % 3 != 1:
                        outside = 0 if k // 3 % 3 == 0 else rows - 1
                        part = jnp.where(row_of == outside, 0.0, part)
                    out[owner * planes + x, k] = homed(k, part)


def coarse_kernel(groups, planes, gathered, c, fine, middle, out, fine_out, middle_out, first, sems):
    kept = [
        pltpu.make_async_copy(fine, fine_out, sems.at[0]),
        pltpu.make_async_copy(middle, middle_out, sems.at[1]),
    ]
    for copy in kept:
        copy.start()
    total, rows, extent = first.shape
    subs = gathered.shape[0] // groups
    each = rows // subs
    for g in range(groups):
        for s in range(subs):
            for x in range(planes):
                first[g * planes + x, s * each : (s + 1) * each, :] = gathered[g * subs + s, x]
    for p in range(total):
        first[p] = WEIGHT * first[p] / c[p, CENTER]

    def sweep(_, field):
        near = [None, *map(neighbours, field), None]
        every = slice(0, extent)
        fresh = []
        for p in range(total):
            sums = outer_terms(near[p : p + 3], lambda k: c[p, k], every)
            fresh.append(first[p] + (1.0 - WEIGHT) * field[p] - sums)
        return tuple(fresh)

    field = lax.fori_loop(0, NB - 1, sweep, tuple(first[p] for p in range(total)), unroll=5)
    for p in range(total):
        first[p] = field[p]
    for x in range(planes):
        out[x] = first[lax.axis_index("grp") * planes + x]
    for copy in kept:
        copy.wait()


def after(value, *others):
    return lax.optimization_barrier((value, *others))[0]


def after_all(values, *others):
    return lax.optimization_barrier((*values, *others))[: len(values)]


def swaps(pairs):
    return [p for a, b in pairs for p in ((a, b), (b, a))]


def body(source, fine, middle, coarse):
    groups, subs = lax.axis_size("grp"), lax.axis_size("sub")
    _, planes, rows, extent = fine.shape
    _, middle_planes, middle_rows, middle_extent = middle.shape
    _, coarse_planes, coarse_rows, coarse_extent = coarse.shape

    x_pairs = swaps([(i, i + 1) for i in range(0, subs, 2)])
    zx_pairs = swaps(
        [(g * subs + i, g * subs + i + 1) for g in range(groups) for i in range(1, subs - 1, 2)]
        + [(g * subs + i, (g + 1) * subs + i) for g in range(0, groups, 2) for i in (0, subs - 1)]
    )
    core_pairs = swaps([(i, i + 1) for i in range(0, groups, 2)])
    y_pairs = swaps([(i, i + 1) for i in range(1, groups - 1, 2)])
    y_ring = y_pairs + [(groups - 1, 0), (0, groups - 1)]

    def along_sub(pair):
        to_x, to_zx = pair
        from_x = lax.ppermute(to_x, "sub", x_pairs)
        return from_x, lax.ppermute(to_zx, ("grp", "sub"), zx_pairs)

    def along_grp(v, halo):
        to_core, to_y = call(faces_kernel, [shape(rows + 8, extent), shape(2 * rows + 8, extent)], [v, *halo])
        from_core = lax.ppermute(to_core, "grp", core_pairs)
        from_y = lax.ppermute(to_y, "grp", y_ring)
        return (*halo, from_core, from_y)

    weights = call(coefficient_scale_kernel, shape(*fine.shape), [fine])
    v = WEIGHT * source / fine[CENTER]
    first = v
    to_x, to_zx = call(edges_kernel, [shape(planes, extent), shape(3 * planes, extent)], [v])

    def sweep(v, halo):
        v, *edges = call(
            functools.partial(sweep_kernel, groups),
            [shape(planes, rows, extent), shape(planes, extent), shape(3 * planes, extent)],
            [v, first, weights, *halo],
        )
        return v, along_sub(edges)

    edges_c = call(
        coefficient_edges_kernel,
        [shape(27, middle_planes, 2, middle_extent)] * 2,
        [middle],
    )
    halo = along_sub((to_x, to_zx))
    halo_c = along_sub(after_all(edges_c, *halo))
    halo = along_grp(after(v, weights, *edges_c), halo)
    known = {0: after(coarse, first)}
    bit = groups // 2
    while bit > 1:
        for offset in sorted(known):
            known[offset ^ bit] = lax.ppermute(known[offset], "grp", [(i, i ^ bit) for i in range(groups)])
        bit //= 2
    offsets = sorted(known)
    v, halo = sweep(v, halo)
    halo = along_grp(v, halo)
    start = middle_planes * (middle_extent // LANES) * ROWS
    early, late, own = call(
        functools.partial(coefficient_pack_kernel, len(known)),
        [shape(EARLY, start, LANES), shape(27 - EARLY, start, LANES), shape(27, start + len(known) * coarse_planes * coarse_rows, LANES)],
        [*(known[o] for o in offsets), middle, *halo_c, *halo[:2]],
    )
    early, own = after_all((early, own), *halo[2:])
    core = lax.ppermute(own, "grp", core_pairs)
    early = lax.ppermute(early, "grp", y_ring)
    v, halo = sweep(v, halo)
    fine_iterate = v
    halo = along_grp(v, halo)
    late = lax.ppermute(after(late, *halo[2:]), "grp", y_ring)
    iterate, *edges = call(
        functools.partial(residual_kernel, groups),
        [shape(middle_planes, middle_rows, middle_extent)]
        + [shape(4 * middle_planes, middle_extent), shape(8 * middle_planes, middle_extent)],
        [v, first, weights, *halo, middle[CENTER]],
        [pltpu.VMEM((planes // 2 * rows, extent), jnp.float32)],
    )
    total = groups * coarse_planes
    ordered = call(
        functools.partial(coarse_order_kernel, coarse_planes, coarse_rows, start, offsets),
        shape(total, 27, coarse_rows, coarse_extent),
        [own, core],
    )
    packed = call(
        middle_faces_kernel,
        shape(middle_planes * ROWS + 8, middle_extent),
        [after(iterate, ordered), *along_sub(edges)],
    )
    near_core = lax.ppermute(packed, "grp", core_pairs)
    if groups == 4:
        far_below = far_above = lax.ppermute(packed, "grp", swaps([(0, 2), (1, 3)]))
        near_y = lax.ppermute(packed, "grp", y_ring)
    else:
        near_y = lax.ppermute(packed, "grp", y_pairs)
        up = [(i, i + 2) for i in range(groups - 2)]
        far_below = lax.ppermute(packed, "grp", up)
        far_above = lax.ppermute(packed, "grp", [(j, i) for i, j in up])
    middle_iterate, coarse_source = call(
        functools.partial(middle_kernel, groups, middle_planes),
        [
            shape(middle_planes, middle_rows, middle_extent),
            shape(groups * subs, coarse_planes, coarse_rows // subs, coarse_extent),
        ],
        [packed, near_core, near_y, far_below, far_above, own, core, early, late],
        [pltpu.VMEM((middle_planes, ROWS, middle_extent), jnp.float32)],
    )
    gathered = lax.all_to_all(coarse_source, ("grp", "sub"), 0, 0, tiled=True)
    vmem, hbm = pl.BlockSpec(memory_space=pltpu.VMEM), pl.BlockSpec(memory_space=pl.ANY)
    coarse_iterate, fine_iterate, middle_iterate = call(
        functools.partial(coarse_kernel, groups, coarse_planes),
        [
            shape(coarse_planes, coarse_rows, coarse_extent),
            shape(*fine_iterate.shape),
            shape(*middle_iterate.shape),
        ],
        [gathered, ordered, fine_iterate, middle_iterate],
        [
            pltpu.VMEM((total, coarse_rows, coarse_extent), jnp.float32),
            pltpu.SemaphoreType.DMA((2,)),
        ],
        out_specs=[vmem, hbm, hbm],
    )
    return fine_iterate, middle_iterate, coarse_iterate


def solution(mesh):
    placed = (
        P("grp", "sub", None),
        P(None, "grp", "sub", None),
        P(None, "grp", "sub", None),
        P(None, "grp", None, None),
    )
    return jax.shard_map(
        body,
        mesh=mesh,
        in_specs=placed,
        out_specs=(P("grp", "sub", None), P("grp", "sub", None), P("grp", None, None)),
        check_vma=False,
    )
```

```python
import functools

import jax
import jax.numpy as jnp
from jax import lax
from jax.experimental import pallas as pl
from jax.experimental.pallas import tpu as pltpu
from jax.sharding import PartitionSpec as P

NU0 = 3
NB = 16
WEIGHT = 0.8
CENTER = 13
EARLY = 19
LANES = 128
ROWS = 8


def shape(*dims):
    return jax.ShapeDtypeStruct(dims, jnp.float32)


def call(kernel, outs, args, scratch=(), out_specs=None):
    vmem = pl.BlockSpec(memory_space=pltpu.VMEM)
    return pl.pallas_call(
        kernel,
        out_shape=outs,
        in_specs=[vmem] * len(args),
        out_specs=out_specs or jax.tree.map(lambda _: vmem, outs),
        scratch_shapes=list(scratch),
        compiler_params=pltpu.CompilerParams(vmem_limit_bytes=12 << 20),
    )(*args)


def even(axis):
    return lax.rem(lax.axis_index(axis), 2) == 0


def pick(condition, a, b):
    return jnp.where(jnp.broadcast_to(condition, a.shape), a, b)


def sides(from_x, from_zx):
    sub, subs = lax.axis_index("sub"), lax.axis_size("sub")
    from_zx = pick((sub == 0) | (sub == subs - 1), jnp.zeros_like(from_zx), from_zx)
    return pick(even("sub"), from_zx, from_x), pick(even("sub"), from_x, from_zx)


def rolled(values):
    extent = values.shape[-1]
    return pltpu.roll(values, 1, 1), values, pltpu.roll(values, extent - 1, 1)


def homed(k, part, first=True, last=True):
    rows, extent = part.shape
    y, z = k // 3 % 3, k % 3
    lane = lax.broadcasted_iota(jnp.int32, part.shape, 1)
    if z == 0 and first:
        part = jnp.where(lane == 0, 0.0, part)
    if z == 2 and last:
        part = jnp.where(lane == extent - 1, 0.0, part)
    if y != 1:
        part = pltpu.roll(part, rows - 1 if y == 0 else 1, 0)
    return part


def neighbours(values, before=None, after=None):
    here = rolled(values)
    if before is None:
        return here, here, here
    row = lax.broadcasted_iota(jnp.int32, values.shape, 0)
    lower = [jnp.where(row == values.shape[0] - 1, b, h) for b, h in zip(rolled(before), here)]
    upper = [jnp.where(row == 0, a, h) for a, h in zip(rolled(after), here)]
    return lower, here, upper


def outer_terms(near, coefficient, lanes):
    sums = [None] * 3
    for x in range(3):
        for y in range(3):
            for z in range(3):
                k = 9 * x + 3 * y + z
                if k == CENTER or near[x] is None:
                    continue
                term = coefficient(k) * near[x][y][z][:, lanes]
                sums[y] = term if sums[y] is None else sums[y] + term
    rows = sums[1].shape[0]
    return sums[1] + (pltpu.roll(sums[0], 1, 0) + pltpu.roll(sums[2], rows - 1, 0))


def lane_tiles(extent):
    return [slice(l, l + LANES) for l in range(0, extent, LANES)]


def paired_lanes(values):
    rows, extent = values.shape
    row = lax.broadcasted_iota(jnp.int32, (extent, extent // 2), 0)
    column = lax.broadcasted_iota(jnp.int32, (extent, extent // 2), 1)
    pairs = jnp.where(lax.shift_right_logical(row, 1) == column, 1.0, 0.0).astype(jnp.bfloat16)
    parts = []
    for _ in range(3):
        part = values.astype(jnp.bfloat16).astype(jnp.float32)
        parts.append(part)
        values = values - part
    if 3 * rows % 16:
        parts.append(jnp.zeros_like(values))
    stacked = jnp.concatenate(parts, axis=0).astype(jnp.bfloat16)
    sums = lax.dot_general(stacked, pairs, (((1,), (0,)), ((), ())), preferred_element_type=jnp.float32)
    return sums[:rows] + (sums[rows : 2 * rows] + sums[2 * rows : 3 * rows])


def paired_rows(values):
    return values + pltpu.roll(values, values.shape[0] - 1, 0)


def put_edges(v, to_x, to_zx):
    last = v.shape[1] - 1
    for x in range(v.shape[0]):
        first_row, last_row = v[x, 0:1, :], v[x, last : last + 1, :]
        to_x[x : x + 1, :] = pick(even("sub"), last_row, first_row)
        to_zx[x : x + 1, :] = pick(even("sub"), first_row, last_row)


def edges_kernel(v, to_x, to_zx):
    put_edges(v, to_x, to_zx)


def faces_kernel(v, from_x, from_zx, to_core, to_y):
    planes, rows, _ = v.shape
    before, after = sides(from_x[...], from_zx[0:planes, :])
    for ref, swap in ((to_core, False), (to_y, True)):
        def choose(a, b):
            return pick(even("grp"), b, a) if swap else pick(even("grp"), a, b)

        ref[0:rows, :] = choose(v[planes - 1], v[0])
        ref[rows : rows + 1, :] = choose(before[planes - 1 :], before[0:1])
        ref[rows + 1 : rows + 2, :] = choose(after[planes - 1 :], after[0:1])


def fine_neighbours(groups, v, from_x, from_zx, from_core, from_y):
    planes, rows, _ = v.shape
    group = lax.axis_index("grp")
    before, after = sides(from_x[...], from_zx[0:planes, :])
    low = pick(even("grp"), from_y[0 : rows + 8, :], from_core[...])
    high = pick(even("grp"), from_core[...], from_y[0 : rows + 8, :])
    low = pick(group == 0, jnp.zeros_like(low), low)
    high = pick(group == groups - 1, jnp.zeros_like(high), high)
    faces = [neighbours(f[0:rows], f[rows : rows + 1], f[rows + 1 : rows + 2]) for f in (low, high)]
    inner = [neighbours(v[x], before[x : x + 1], after[x : x + 1]) for x in range(planes)]
    return [faces[0], *inner, faces[1]]


def sweep_kernel(groups, v, first, c, from_x, from_zx, from_core, from_y, out, to_x, to_zx):
    planes, rows, extent = v.shape
    near = fine_neighbours(groups, v, from_x, from_zx, from_core, from_y)
    for x in range(planes):
        for lanes in lane_tiles(extent):
            sums = outer_terms(near[x : x + 3], lambda k: c[k, x, :, lanes], lanes)
            out[x, :, lanes] = first[x, :, lanes] + (1.0 - WEIGHT) * v[x, :, lanes] - sums
    put_edges(out, to_x, to_zx)


def residual_kernel(
    groups, v, first, c, from_x, from_zx, from_core, from_y, center, iterate, to_x, to_zx, held
):
    planes, rows, extent = v.shape
    near = fine_neighbours(groups, v, from_x, from_zx, from_core, from_y)
    for x in range(0, planes, 2):
        for lanes in lane_tiles(extent):
            total = None
            for p in (x, x + 1):
                sums = outer_terms(near[p : p + 3], lambda k: c[k, p, :, lanes], lanes)
                part = first[p, :, lanes] - WEIGHT * v[p, :, lanes] - sums
                part = (1.0 / WEIGHT) * c[CENTER, p, :, lanes] * part
                total = part if total is None else total + part
            held[x // 2 * rows : (x // 2 + 1) * rows, lanes] = total
    total = (0.5 * WEIGHT) * paired_rows(paired_lanes(held[...]))
    half = rows // 2
    for x in range(planes // 2):
        for y in range(half):
            row = x * rows + 2 * y
            iterate[x, y : y + 1, :] = total[row : row + 1]
    iterate[...] = iterate[...] / center[...]
    for x in range(planes // 2):
        first_rows, last_rows = iterate[x, 0:3, :], iterate[x, half - 3 : half, :]
        to_x[4 * x : 4 * x + 3, :] = pick(even("sub"), last_rows, first_rows)
        to_zx[4 * x : 4 * x + 3, :] = pick(even("sub"), first_rows, last_rows)


def middle_faces_kernel(mine, from_x, from_zx, out, larger):
    planes, half, _ = mine.shape
    before, after = sides(from_x[...], from_zx[0 : 4 * planes, :])
    for x in range(planes):
        row = x * ROWS
        out[row : row + 2, :] = before[4 * x + 1 : 4 * x + 3]
        out[row + 2 : row + 2 + half, :] = mine[x]
        out[row + 2 + half : row + ROWS, :] = after[4 * x : 4 * x + 2]
        extra = planes * ROWS + 2 * x
        out[extra : extra + 1, :] = before[4 * x : 4 * x + 1]
        out[extra + 1 : extra + 2, :] = after[4 * x + 2 : 4 * x + 3]
    larger[0 : out.shape[0], :] = out[...]


def coefficient_edges_kernel(c, to_x, to_zx):
    rows = c.shape[2]
    first, last = c[:, :, 0:2, :], c[:, :, rows - 2 : rows, :]
    to_x[...] = pick(even("sub"), last, first)
    to_zx[...] = pick(even("sub"), first, last)


def coefficient_scale_kernel(c, out):
    for x in range(c.shape[1]):
        out[:, x] = scaled(c[:, x])
        for k in range(27):
            out[k, x] = homed(k, out[k, x])


def scaled(c):
    center = c[CENTER : CENTER + 1]
    ratio = WEIGHT / jnp.where(center > 0.0, center, 1.0)
    index = lax.broadcasted_iota(jnp.int32, c.shape, 0)
    return c * jnp.where(index == CENTER, 1.0, ratio)


def coefficient_pack_kernel(known, *refs):
    coarse, (c, from_x, from_zx, _, __, early, late, whole) = refs[:known], refs[known:]
    _, planes, rows, extent = c.shape
    tiles = extent // LANES
    before, after = sides(from_x[...], from_zx[...])
    for x in range(planes):
        for l, lanes in enumerate(lane_tiles(extent)):
            row = (x * tiles + l) * ROWS
            whole[:, row : row + 2, :] = before[:, x, :, lanes]
            whole[:, row + 2 : row + 2 + rows, :] = c[:, x, :, lanes]
            whole[:, row + 2 + rows : row + ROWS, :] = after[:, x, :, lanes]
    row = planes * tiles * ROWS
    for t in range(0, row, ROWS):
        part = scaled(whole[:, t : t + ROWS, :])
        l = t // ROWS % tiles
        for k in range(27):
            ready = homed(k, part[k], l == 0, l == tiles - 1)
            whole[k, t : t + ROWS, :] = ready
            if k < EARLY:
                early[k, t : t + ROWS, :] = ready
            else:
                late[k - EARLY, t : t + ROWS, :] = ready
    for ref in coarse:
        for x in range(ref.shape[1]):
            for t in range(0, ref.shape[2], ROWS):
                whole[:, row : row + ROWS, :] = scaled(ref[:, x, t : t + ROWS, :])
                row += ROWS


def middle_kernel(
    groups, planes, packed, near_core, near_y, far_below, far_above, own, core, early, late, iterate, coarse, held
):
    extent = packed.shape[-1]
    tiles = extent // LANES
    half = ROWS - 4
    group = lax.axis_index("grp")
    window = 3 * planes

    below = pick(even("grp"), near_y[...], near_core[0 : near_y.shape[0], :])
    above = pick(even("grp"), near_core[0 : near_y.shape[0], :], near_y[...])
    blocks = {-2: far_below[...], -1: below, 0: packed[...], 1: above, 2: far_above[...]}
    for away in (-2, -1, 1, 2):
        inside = (group + away >= 0) & (group + away < groups)
        blocks[away] = pick(inside, blocks[away], jnp.zeros_like(blocks[away]))
    first, near = [], []
    for p in range(-1, window + 1):
        block, x = blocks[p // planes - 1], p % planes
        v, extra = block[x * ROWS : (x + 1) * ROWS], planes * ROWS + 2 * x
        first.append(v)
        near.append(neighbours(v, block[extra : extra + 1], block[extra + 1 : extra + 2]))

    def work(parts):
        def terms(forms, w, lanes):
            row = (w % planes * tiles + lanes.start // LANES) * ROWS
            return outer_terms(forms, lambda k: parts[w // planes](k)[row : row + ROWS, :], lanes)

        def swept(forms, field, w):
            sums = jnp.concatenate([terms(forms, w, lanes) for lanes in lane_tiles(extent)], axis=1)
            values = first[w + 1] + (1.0 - WEIGHT) * field - sums
            away = w // planes - 1
            if away:
                inside = (group + away >= 0) & (group + away < groups)
                values = pick(inside, values, jnp.zeros_like(values))
            return values

        low, high = planes - 2, 2 * planes + 2
        once = {w: swept(near[w : w + 3], first[w + 1], w) for w in range(low, high)}
        forms = {w: neighbours(v) for w, v in once.items()}
        low, high = low + 1, high - 1
        twice = {w: swept([forms[w + x] for x in (-1, 0, 1)], once[w], w) for w in range(low, high)}
        forms = {w: neighbours(v) for w, v in twice.items()}
        for x in range(planes):
            w = planes + x
            iterate[x] = twice[w][2 : 2 + half]
            for lanes in lane_tiles(extent):
                row = (x * tiles + lanes.start // LANES) * ROWS
                sums = terms([forms[w + i] for i in (-1, 0, 1)], w, lanes)
                rest = first[w + 1][:, lanes] - WEIGHT * twice[w][:, lanes] - sums
                held[x, :, lanes] = (1.0 / WEIGHT) * own[CENTER, row : row + ROWS, :] * rest

    def here(k):
        return own.at[k]

    def beside(k):
        return core.at[k]

    def across(k):
        return early.at[k] if k < EARLY else late.at[k - EARLY]

    @pl.when(even("grp"))
    def _():
        work((across, here, beside))

    @pl.when(jnp.logical_not(even("grp")))
    def _():
        work((beside, here, across))

    place_of = lax.broadcasted_iota(jnp.int32, (ROWS, extent // 2), 0)
    for x in range(planes // 2):
        total = 0.5 * paired_rows(paired_lanes(held[2 * x] + held[2 * x + 1]))
        value = pltpu.roll(total, ROWS - 2, 0)
        for i in range(1, half // 2):
            value = jnp.where(place_of == i, pltpu.roll(total, ROWS - 2 - i, 0), value)
        for device in range(coarse.shape[0]):
            coarse[device, x] = value[: half // 2]


def coarse_order_kernel(planes, rows, start, offsets, own, core, out):
    group = lax.axis_index("grp")
    row_of = lax.broadcasted_iota(jnp.int32, (rows, out.shape[-1]), 0)
    for ref, flip in ((own, 0), (core, 1)):
        for i, offset in enumerate(offsets):
            owner = jnp.bitwise_xor(group, offset ^ flip)
            for x in range(planes):
                row = start + (i * planes + x) * rows
                for k in range(27):
                    part = ref[k, row : row + rows, :]
                    if k // 3 % 3 != 1:
                        outside = 0 if k // 3 % 3 == 0 else rows - 1
                        part = jnp.where(row_of == outside, 0.0, part)
                    out[owner * planes + x, k] = homed(k, part)


def coarse_kernel(groups, planes, gathered, c, fine, middle, out, fine_out, middle_out, first, sems):
    kept = [
        pltpu.make_async_copy(fine, fine_out, sems.at[0]),
        pltpu.make_async_copy(middle, middle_out, sems.at[1]),
    ]
    for copy in kept:
        copy.start()
    total, rows, extent = first.shape
    subs = gathered.shape[0] // groups
    each = rows // subs
    for g in range(groups):
        for s in range(subs):
            for x in range(planes):
                first[g * planes + x, s * each : (s + 1) * each, :] = gathered[g * subs + s, x]
    for p in range(total):
        first[p] = WEIGHT * first[p] / c[p, CENTER]

    def sweep(_, field):
        near = [None, *map(neighbours, field), None]
        every = slice(0, extent)
        fresh = []
        for p in range(total):
            sums = outer_terms(near[p : p + 3], lambda k: c[p, k], every)
            fresh.append(first[p] + (1.0 - WEIGHT) * field[p] - sums)
        return tuple(fresh)

    field = lax.fori_loop(0, NB - 1, sweep, tuple(first[p] for p in range(total)), unroll=5)
    for p in range(total):
        first[p] = field[p]
    for x in range(planes):
        out[x] = first[lax.axis_index("grp") * planes + x]
    for copy in kept:
        copy.wait()


def after(value, *others):
    return lax.optimization_barrier((value, *others))[0]


def after_all(values, *others):
    return lax.optimization_barrier((*values, *others))[: len(values)]


def swaps(pairs):
    return [p for a, b in pairs for p in ((a, b), (b, a))]


def body(source, fine, middle, coarse):
    groups, subs = lax.axis_size("grp"), lax.axis_size("sub")
    _, planes, rows, extent = fine.shape
    _, middle_planes, middle_rows, middle_extent = middle.shape
    _, coarse_planes, coarse_rows, coarse_extent = coarse.shape

    x_pairs = swaps([(i, i + 1) for i in range(0, subs, 2)])
    zx_pairs = swaps(
        [(g * subs + i, g * subs + i + 1) for g in range(groups) for i in range(1, subs - 1, 2)]
        + [(g * subs + i, (g + 1) * subs + i) for g in range(0, groups, 2) for i in (0, subs - 1)]
    )
    core_pairs = swaps([(i, i + 1) for i in range(0, groups, 2)])
    y_pairs = swaps([(i, i + 1) for i in range(1, groups - 1, 2)])
    y_ring = y_pairs + [(groups - 1, 0), (0, groups - 1)]

    def along_sub(pair):
        to_x, to_zx = pair
        from_x = lax.ppermute(to_x, "sub", x_pairs)
        return from_x, lax.ppermute(to_zx, ("grp", "sub"), zx_pairs)

    def along_grp(v, halo):
        to_core, to_y = call(faces_kernel, [shape(rows + 8, extent), shape(2 * rows + 8, extent)], [v, *halo])
        from_core = lax.ppermute(to_core, "grp", core_pairs)
        from_y = lax.ppermute(to_y, "grp", y_ring)
        return (*halo, from_core, from_y)

    weights = call(coefficient_scale_kernel, shape(*fine.shape), [fine])
    v = WEIGHT * source / fine[CENTER]
    first = v
    to_x, to_zx = call(edges_kernel, [shape(planes, extent), shape(3 * planes, extent)], [v])

    def sweep(v, halo):
        v, *edges = call(
            functools.partial(sweep_kernel, groups),
            [shape(planes, rows, extent), shape(planes, extent), shape(3 * planes, extent)],
            [v, first, weights, *halo],
        )
        return v, along_sub(edges)

    edges_c = call(
        coefficient_edges_kernel,
        [shape(27, middle_planes, 2, middle_extent)] * 2,
        [middle],
    )
    halo = along_sub((to_x, to_zx))
    halo_c = along_sub(after_all(edges_c, *halo))
    halo = along_grp(after(v, weights, *edges_c), halo)
    known = {0: after(coarse, first)}
    bit = groups // 2
    while bit > 1:
        for offset in sorted(known):
            known[offset ^ bit] = lax.ppermute(known[offset], "grp", [(i, i ^ bit) for i in range(groups)])
        bit //= 2
    offsets = sorted(known)
    v, halo = sweep(v, halo)
    halo = along_grp(v, halo)
    start = middle_planes * (middle_extent // LANES) * ROWS
    early, late, own = call(
        functools.partial(coefficient_pack_kernel, len(known)),
        [shape(EARLY, start, LANES), shape(27 - EARLY, start, LANES), shape(27, start + len(known) * coarse_planes * coarse_rows, LANES)],
        [*(known[o] for o in offsets), middle, *halo_c, *halo[2:]],
    )
    core = lax.ppermute(own, "grp", core_pairs)
    early = lax.ppermute(early, "grp", y_ring)
    v, halo = sweep(v, halo)
    fine_iterate = v
    halo = along_grp(v, halo)
    late = lax.ppermute(after(late, *halo[2:]), "grp", y_ring)
    iterate, *edges = call(
        functools.partial(residual_kernel, groups),
        [shape(middle_planes, middle_rows, middle_extent)]
        + [shape(4 * middle_planes, middle_extent), shape(8 * middle_planes, middle_extent)],
        [v, first, weights, *halo, middle[CENTER]],
        [pltpu.VMEM((planes // 2 * rows, extent), jnp.float32)],
    )
    total = groups * coarse_planes
    ordered = call(
        functools.partial(coarse_order_kernel, coarse_planes, coarse_rows, start, offsets),
        shape(total, 27, coarse_rows, coarse_extent),
        [own, core],
    )
    packed, larger = call(
        middle_faces_kernel,
        [shape(middle_planes * ROWS + 8, middle_extent), shape(middle_planes * ROWS + 16, middle_extent)],
        [after(iterate, ordered), *along_sub(edges)],
    )
    near_core = lax.ppermute(larger, "grp", core_pairs)
    if groups == 4:
        far_below = far_above = lax.ppermute(packed, "grp", swaps([(0, 2), (1, 3)]))
        near_y = lax.ppermute(packed, "grp", y_ring)
    else:
        near_y = lax.ppermute(packed, "grp", y_pairs)
        up = [(i, i + 2) for i in range(groups - 2)]
        far_below = lax.ppermute(packed, "grp", up)
        far_above = lax.ppermute(packed, "grp", [(j, i) for i, j in up])
    middle_iterate, coarse_source = call(
        functools.partial(middle_kernel, groups, middle_planes),
        [
            shape(middle_planes, middle_rows, middle_extent),
            shape(groups * subs, coarse_planes, coarse_rows // subs, coarse_extent),
        ],
        [packed, near_core, near_y, far_below, far_above, own, core, early, late],
        [pltpu.VMEM((middle_planes, ROWS, middle_extent), jnp.float32)],
    )
    gathered = lax.all_to_all(coarse_source, ("grp", "sub"), 0, 0, tiled=True)
    vmem, hbm = pl.BlockSpec(memory_space=pltpu.VMEM), pl.BlockSpec(memory_space=pl.ANY)
    coarse_iterate, fine_iterate, middle_iterate = call(
        functools.partial(coarse_kernel, groups, coarse_planes),
        [
            shape(coarse_planes, coarse_rows, coarse_extent),
            shape(*fine_iterate.shape),
            shape(*middle_iterate.shape),
        ],
        [gathered, ordered, fine_iterate, middle_iterate],
        [
            pltpu.VMEM((total, coarse_rows, coarse_extent), jnp.float32),
            pltpu.SemaphoreType.DMA((2,)),
        ],
        out_specs=[vmem, hbm, hbm],
    )
    return fine_iterate, middle_iterate, coarse_iterate


def solution(mesh):
    placed = (
        P("grp", "sub", None),
        P(None, "grp", "sub", None),
        P(None, "grp", "sub", None),
        P(None, "grp", None, None),
    )
    return jax.shard_map(
        body,
        mesh=mesh,
        in_specs=placed,
        out_specs=(P("grp", "sub", None), P("grp", "sub", None), P("grp", None, None)),
        check_vma=False,
    )
```
